32 devices in a mesh: dp: 8 (over y, x, core), tensor: 4 (over z).
Axes of the slice: x: 2, y: 2, z: 4, core: 2. Of those that a mesh axis runs over, the one named last changes fastest.
Arguments:
- x_post: bfloat16 [1024, 32, 512], P('tensor', 'dp'), may hold values from -6 to 6
- x_dual: bfloat16 [1024, 32, 512], P('tensor', 'dp'), may hold values from -6 to 6
- cot_post: bfloat16 [1024, 32, 512], P('tensor', 'dp'), may hold values from -6 to 6
- cot_dual: bfloat16 [1024, 32, 512], P('tensor', 'dp'), may hold values from -6 to 6
- segment_ids: int32 [1024, 32], P(None, 'dp'), may hold values from 0 to 3, as said below
- w_qkv: bfloat16 [3, 512, 512], P(None, None, 'tensor'), may hold values from -0.375 to 0.375
- w_out: bfloat16 [512, 512], P('tensor'), may hold values from -0.5 to 0.5
- w_up: bfloat16 [512, 2048], P(None, 'tensor'), may hold values from -0.25 to 0.25
- w_down: bfloat16 [2048, 512], P('tensor'), may hold values from -0.125 to 0.125
- gain_one: float32 [512], replicated, may hold values from 0.1 to 1.9
- bias_one: float32 [512], replicated, may hold values from -4 to 4
- gain_two: float32 [512], replicated, may hold values from 0.1 to 1.9
- bias_two: float32 [512], replicated, may hold values from -4 to 4
Outputs:
- post_out: float32 [1024, 32, 512], P('tensor', 'dp')
- dual_out: float32 [1024, 32, 512], P('tensor', 'dp')
- grad_post: float32 [1024, 32, 512], P('tensor', 'dp')
- grad_qkv: float32 [3, 512, 512], P(None, 'dp', 'tensor')
- grad_out: float32 [512, 512], P('tensor', 'dp')
- grad_up: float32 [512, 2048], P('dp', 'tensor')
- grad_down: float32 [2048, 512], P('tensor', 'dp')
- grad_gain_one: float32 [512], P(('dp', 'tensor'))
- grad_bias_one: float32 [512], P(('dp', 'tensor'))
- grad_gain_two: float32 [512], P(('dp', 'tensor'))
- grad_bias_two: float32 [512], P(('dp', 'tensor'))
The draws below stay inside these ranges and needn't reach their ends.
Inputs may be any that keep to these rules, and one draw needn't show every extreme that they name: `segment_ids`: down each column (one packed row of 1024 tokens) the ids start at 0 and never fall; equal ids mark one document. In each aligned block of 4 columns one column holds a single document; every other column holds exactly four documents.
All inputs are finite; a program needn't handle non-finite values.
Results may differ from the reference program's by a relative error of at most 0.017.
The reference program's roundings to bfloat16 on the way count: a program that leaves them out, or rounds other values in their place, can miss the bound.
Values may be sent and summed in bfloat16 or wider, within the bound.
A program may use at most 192 MiB of HBM per device.

```python
import jax
import jax.numpy as jnp
from jax import lax

D = 512
HEADS = 8
FF = 2048
L = 1024
SEQ_DEV = 4
COLS = 32


def draw_segment_ids(key, part):
    key = jax.random.fold_in(key, 7)
    starts_key, whole_key = jax.random.split(key)
    column_keys = jax.random.split(starts_key, COLS)
    orders = jax.vmap(lambda one_key: jax.random.permutation(one_key, L - 1))(column_keys)
    marked = orders.T < 3
    starts = jnp.concatenate([jnp.zeros((1, COLS), dtype=bool), marked], axis=0)
    chosen = jax.random.randint(whole_key, (COLS // SEQ_DEV,), 0, SEQ_DEV)
    column = jnp.arange(COLS)
    single = column % SEQ_DEV == jnp.repeat(chosen, SEQ_DEV)
    flags = jnp.where(jnp.logical_not(single)[None, :], starts, False)
    return jnp.cumsum(flags.astype(jnp.int32), axis=0).astype(jnp.int32)


def steps_of(key, dims, shards, low, largest):
    def one(position, parts):
        heights = jax.random.uniform(jax.random.fold_in(jax.random.fold_in(key, 6), position), (parts,), jnp.float32, low / len(shards), largest / len(shards))
        return jnp.repeat(jnp.exp(heights), dims[position] // parts).reshape((-1,) + (1,) * (len(dims) - position - 1))

    level = one(*shards[0])
    for cut in shards[1:]:
        level = level * one(*cut)
    return level


def scatter_about(own_key, extent, scale, reach, pieces=(), kind=jnp.bfloat16):
    loudness = steps_of(own_key, extent, pieces, -0.22, 0.18) if pieces else 1.0
    values = jax.random.normal(own_key, extent, jnp.float32) * scale * loudness
    return jnp.minimum(jnp.maximum(values, -reach), reach).astype(kind)


def setup_inputs(seed: int = 0) -> dict:
    key_list = jax.random.split(jax.random.key(seed), 14)
    x_post = scatter_about(key_list[0], (L, COLS, D), 1.0, 6.0, ((0, 4), (1, 8)))
    x_dual = scatter_about(key_list[1], (L, COLS, D), 1.0, 6.0, ((0, 4), (1, 8)))
    cot_post = scatter_about(key_list[2], (L, COLS, D), 1.0, 6.0, ((0, 4), (1, 8)))
    cot_dual = scatter_about(key_list[3], (L, COLS, D), 1.0, 6.0, ((0, 4), (1, 8)))
    segment_ids = draw_segment_ids(jax.random.fold_in(key_list[13], 71), 0)
    w_qkv = scatter_about(key_list[5], (3, D, D), (D // 2) ** -0.5, 0.375, ((2, 4),))
    w_out = scatter_about(key_list[6], (D, D), (D // 4) ** -0.5, 0.5, ((0, 4),))
    w_up = scatter_about(key_list[7], (D, FF), D ** -0.5, 0.25, ((1, 4),))
    w_down = scatter_about(key_list[8], (FF, D), FF ** -0.5, 0.125, ((0, 4),))
    gain_one = jnp.clip(1.0 + 0.18 * jax.random.normal(key_list[9], (D,), jnp.float32), 0.1, 1.9)
    bias_one = scatter_about(key_list[10], (D,), 0.3, 4.0, (), jnp.float32)
    gain_two = jnp.clip(1.0 + 0.18 * jax.random.normal(key_list[11], (D,), jnp.float32), 0.1, 1.9)
    bias_two = scatter_about(key_list[12], (D,), 0.3, 4.0, (), jnp.float32)
    return {"x_post": x_post, "x_dual": x_dual, "cot_post": cot_post, "cot_dual": cot_dual, "segment_ids": segment_ids, "w_qkv": w_qkv, "w_out": w_out, "w_up": w_up, "w_down": w_down, "gain_one": gain_one, "bias_one": bias_one, "gain_two": gain_two, "bias_two": bias_two}


EPSILON = 1e-05
HIGH = lax.Precision.HIGHEST

@jax.custom_vjp
def low(v):
    return lax.optimization_barrier(v.astype(jnp.bfloat16)).astype(jnp.float32)

@jax.custom_vjp
def low_back(v):
    return v

def low_keep(v):
    return (low(v), None)

def low_pass(kept, grad):
    return (grad,)

def back_keep(v):
    return (v, None)

def back_low(kept, grad):
    return (low(grad),)
low.defvjp(low_keep, low_pass)
low_back.defvjp(back_keep, back_low)

def layer_norm(total, gain, bias):
    centre = total - lax.optimization_barrier(jnp.mean(total, axis=-1, keepdims=True))
    spread = lax.optimization_barrier(jnp.mean(centre * centre, axis=-1, keepdims=True))
    return centre * lax.rsqrt(spread + EPSILON) * gain + bias

def layer(post, dual, w_qkv, w_out, w_up, w_down, gain_one, bias_one, gain_two, bias_two, labels):
    length, columns, width = post.shape
    projected = low_back(low(jnp.einsum('lbd,cdf->clbf', post, w_qkv, precision=HIGH)))
    split = projected.reshape(3, length, columns, HEADS, width // HEADS)
    query, keys, values = (split[0], split[1], split[2])
    scores = low_back(jnp.einsum('qbhe,kbhe->bhqk', query, keys, precision=HIGH) * 0.125)
    marks = labels.T
    same = (marks[:, :, None] == marks[:, None, :])[:, None]
    scores = jnp.where(same, scores, -1e+30)
    top = lax.optimization_barrier(jnp.max(scores, axis=-1, keepdims=True))
    raised = jnp.exp(scores - top)
    probs = low(raised / lax.optimization_barrier(jnp.sum(raised, axis=-1, keepdims=True)))
    mixed = jnp.einsum('bhqk,kbhe->qbhe', probs, values, precision=HIGH)
    mixed = low_back(low(mixed)).reshape(length, columns, width)
    branch_one = low_back(jnp.einsum('lbf,fd->lbd', mixed, w_out, precision=HIGH))
    middle = layer_norm(post + branch_one, gain_one, bias_one)
    inner = low_back(jnp.einsum('lbd,df->lbf', low(middle), w_up, precision=HIGH))
    hidden = low(jax.nn.gelu(inner))
    branch_two = low_back(jnp.einsum('lbf,fd->lbd', hidden, w_down, precision=HIGH))
    post_out = layer_norm(middle + branch_two, gain_two, bias_two)
    return (post_out, dual + branch_one + branch_two)

def reference(x_post, x_dual, cot_post, cot_dual, segment_ids, w_qkv, w_out, w_up, w_down, gain_one, bias_one, gain_two, bias_two):
    length, total, width = x_post.shape
    groups = total // 4
    params = (w_qkv.astype(jnp.float32), w_out.astype(jnp.float32), w_up.astype(jnp.float32), w_down.astype(jnp.float32), gain_one.astype(jnp.float32), bias_one.astype(jnp.float32), gain_two.astype(jnp.float32), bias_two.astype(jnp.float32))

    def split_cols(array):
        return jnp.swapaxes(array.reshape((length, groups, 4) + array.shape[2:]), 0, 1)

    def join_cols(array):
        return jnp.swapaxes(array, 0, 1).reshape((length, total) + array.shape[3:])

    def advance(carry, item):
        post, dual, cot_one, cot_two, labels = item

        def forward(post_in, wq, wo, wu, wd, g_one, c_one, g_two, c_two):
            return layer(post_in, dual, wq, wo, wu, wd, g_one, c_one, g_two, c_two, labels)
        outs, pull = jax.vjp(forward, post, params[0], params[1], params[2], params[3], params[4], params[5], params[6], params[7])
        grads = pull((cot_one, cot_two))
        carry = tuple((old + new for old, new in zip(carry, grads[1:])))
        return (carry, (outs[0], outs[1], grads[0]))
    start = tuple((jnp.zeros_like(param) for param in params))
    items = (split_cols(x_post.astype(jnp.float32)), split_cols(x_dual.astype(jnp.float32)), split_cols(cot_post.astype(jnp.float32)), split_cols(cot_dual.astype(jnp.float32)), split_cols(segment_ids))
    sums, (posts, duals, grad_posts) = lax.scan(advance, start, items)
    return (join_cols(posts), join_cols(duals), join_cols(grad_posts), sums[0], sums[1], sums[2], sums[3], sums[4], sums[5], sums[6], sums[7])
```

```python
import functools

import jax
import jax.numpy as jnp
from jax import lax
from jax.experimental import pallas as pl
from jax.experimental.pallas import tpu as pltpu
from jax.sharding import PartitionSpec as P

E = 64
EPSILON = 1e-05
NEGATIVE = -1e30
GELU_A = 0.7978845608028654
GELU_B = 0.044715
F32 = jnp.float32
BF16 = jnp.bfloat16
VMEM_BYTES = 60 * 1024 * 1024


def dot_nn(a, b):
    return lax.dot_general(a, b, (((1,), (0,)), ((), ())), preferred_element_type=F32)


def dot_nt(a, b):
    return lax.dot_general(a, b, (((1,), (1,)), ((), ())), preferred_element_type=F32)


def dot_tn(a, b):
    return lax.dot_general(a, b, (((0,), (0,)), ((), ())), preferred_element_type=F32)


def row_mean(a):
    return jnp.mean(a, axis=-1, keepdims=True)


def norm_forward(total):
    centre = total - row_mean(total)
    factor = lax.rsqrt(row_mean(centre * centre) + EPSILON)
    return centre * factor, factor


def norm_backward(upstream, normed, factor, gain):
    scaled = upstream * gain
    inner = scaled - row_mean(scaled) - normed * row_mean(scaled * normed)
    return factor * inner


def mask_bias(seg_keys, seg_own, column, bias_ref):
    lanes = lax.broadcasted_iota(jnp.int32, seg_keys.shape, 1)
    keys = jnp.sum(jnp.where(lanes == column, seg_keys, 0.0), axis=1, keepdims=True)
    bias_ref[...] = jnp.where(keys == seg_own, 0.0, NEGATIVE)


def half_rows(block, half):
    zeros = jnp.zeros((E, block.shape[1]), block.dtype)
    if half == 0:
        return jnp.concatenate([block[:E], zeros], axis=0)
    return jnp.concatenate([zeros, block[E:]], axis=0)


def forward_kernel(
    seg_ref,
    seg_own_ref,
    x_all_ref,
    x_own_ref,
    dual_in_ref,
    cot_post_ref,
    cot_dual_ref,
    w_qkv_ref,
    w_out_ref,
    w_up_ref,
    w_down_ref,
    norms_ref,
    post_ref,
    dual_ref,
    d_one_ref,
    q_ref,
    k_ref,
    v_ref,
    do_ref,
    lse_ref,
    delta_ref,
    g_down_ref,
    g_up_ref,
    g_out_ref,
    g_norm_ref,
    bias_ref,
    qt_ref,
    vt_ref,
    ot_ref,
    hidden_ref,
    slope_ref,
    grad_inner_ref,
    up_two_ref,
    middle_ref,
    up_one_ref,
    mixed_ref,
):
    tensors, columns, rows, width = x_all_ref.shape
    length = tensors * rows
    heads = width // E
    pairs = heads // 2
    gain_one, bias_one = norms_ref[0:1, :], norms_ref[1:2, :]
    gain_two, bias_two = norms_ref[2:3, :], norms_ref[3:4, :]
    g_norm_ref[...] = jnp.zeros_like(g_norm_ref)

    @pl.loop(0, columns)
    def _(c):
        mask_bias(seg_ref[...], seg_own_ref[pl.ds(c, 1), :], c, bias_ref)
        x_own = x_own_ref[c]
        query = dot_nn(x_own, w_qkv_ref[0]).astype(BF16) * jnp.bfloat16(0.125)
        q_ref[c] = query
        qt_ref[...] = query.astype(F32).T.astype(BF16)

        @pl.loop(0, tensors)
        def _(t):
            block = x_all_ref[t, c]
            at = pl.ds(pl.multiple_of(t * rows, rows), rows)
            k_ref[c, at, :] = dot_nn(block, w_qkv_ref[1]).astype(BF16)
            v_ref[c, at, :] = dot_nn(block, w_qkv_ref[2]).astype(BF16)

        vt_ref[...] = v_ref[c].T

        @pl.loop(0, pairs)
        def _(j):
            at = pl.ds(pl.multiple_of(j * 2 * E, 2 * E), 2 * E)
            keys = k_ref[c, :, at]
            queries = qt_ref[at, :]
            for half in range(2):
                scores = dot_nn(keys, half_rows(queries, half)) + bias_ref[...]
                top = jnp.max(scores, axis=0, keepdims=True)
                raised = jnp.exp(scores - top)
                denom = jnp.sum(raised, axis=0, keepdims=True)
                at_head = pl.ds(pl.multiple_of((2 * j + half) * E, E), E)
                result = dot_nn(vt_ref[at_head, :], raised.astype(BF16))
                ot_ref[at_head, :] = result * (1.0 / denom)
                lse_ref[c, pl.ds(2 * j + half, 1), :] = top + jnp.log(denom)

        tokens = pl.ds(pl.multiple_of(c * rows, rows), rows)
        mixed = ot_ref[...].T.astype(BF16)
        mixed_ref[tokens, :] = mixed
        branch_one = dot_nn(mixed, w_out_ref[...])
        normed_one, factor_one = norm_forward(x_own.astype(F32) + branch_one)
        middle = normed_one * gain_one + bias_one
        middle_low = middle.astype(BF16)
        middle_ref[tokens, :] = middle_low
        branch_two = jnp.zeros((rows, width), F32)
        for t in range(tensors):
            inner = dot_nn(middle_low, w_up_ref[t])
            square = inner * inner
            bend = jnp.tanh(GELU_A * (inner + GELU_B * (square * inner)))
            hidden = (0.5 * inner * (1.0 + bend)).astype(BF16)
            slope_ref[t] = 0.5 * (1.0 + bend) + (0.5 * GELU_A) * inner * (1.0 - bend * bend) * (
                1.0 + (3.0 * GELU_B) * square
            )
            hidden_ref[t, tokens, :] = hidden
            branch_two = branch_two + dot_nn(hidden, w_down_ref[t])
        normed_two, factor_two = norm_forward(middle + branch_two)
        post_ref[c] = normed_two * gain_two + bias_two
        dual_ref[c] = dual_in_ref[c].astype(F32) + branch_one + branch_two
        cot_dual = cot_dual_ref[c].astype(F32)
        upstream = cot_post_ref[c].astype(F32)
        d_two = norm_backward(upstream, normed_two, factor_two, gain_two)
        g_norm_ref[2:3, :] += jnp.sum(upstream * normed_two, axis=0, keepdims=True)
        g_norm_ref[3:4, :] += jnp.sum(upstream, axis=0, keepdims=True)
        up_two = (d_two + cot_dual).astype(BF16)
        up_two_ref[tokens, :] = up_two
        grad_middle = d_two
        for t in range(tensors):
            grad_hidden = dot_nt(up_two, w_down_ref[t])
            grad_inner = (grad_hidden * slope_ref[t]).astype(BF16)
            grad_inner_ref[t, tokens, :] = grad_inner
            grad_middle = grad_middle + dot_nt(grad_inner, w_up_ref[t])
        d_one = norm_backward(grad_middle, normed_one, factor_one, gain_one)
        g_norm_ref[0:1, :] += jnp.sum(grad_middle * normed_one, axis=0, keepdims=True)
        g_norm_ref[1:2, :] += jnp.sum(grad_middle, axis=0, keepdims=True)
        d_one_ref[c] = d_one
        up_one = (d_one + cot_dual).astype(BF16)
        up_one_ref[tokens, :] = up_one
        grad_mixed = dot_nt(up_one, w_out_ref[...]).astype(BF16)
        do_ref[c] = grad_mixed
        product = grad_mixed.astype(F32).T * ot_ref[...]
        delta_ref[c] = jnp.sum(product.reshape(heads, E, rows), axis=1)

    @pl.loop(0, tensors)
    def _(t):
        g_down_ref[t] = dot_tn(up_two_ref[...], hidden_ref[t]).astype(BF16)
        g_up_ref[t] = dot_tn(middle_ref[...], grad_inner_ref[t]).astype(BF16)

    g_out_ref[...] = dot_tn(up_one_ref[...], mixed_ref[...]).astype(BF16)


def backward_kernel(
    seg_ref,
    seg_own_ref,
    x_all_ref,
    x_own_ref,
    w_qkv_ref,
    d_one_ref,
    q_ref,
    k_ref,
    v_ref,
    do_ref,
    lse_ref,
    delta_ref,
    base_ref,
    part_ref,
    g_qkv_ref,
    bias_ref,
    qt_ref,
    dot_ref,
    kt_ref,
    dk_ref,
    dv_ref,
    dqt_ref,
    acc_ref,
):
    tensors, columns, rows, width = x_all_ref.shape
    heads = width // E
    pairs = heads // 2
    acc_ref[...] = jnp.zeros_like(acc_ref)

    @pl.loop(0, columns)
    def _(c):
        mask_bias(seg_ref[...], seg_own_ref[pl.ds(c, 1), :], c, bias_ref)
        qt_ref[...] = q_ref[c].T
        dot_ref[...] = do_ref[c].T
        kt_ref[...] = k_ref[c].T

        @pl.loop(0, pairs)
        def _(j):
            at = pl.ds(pl.multiple_of(j * 2 * E, 2 * E), 2 * E)
            keys, values = k_ref[c, :, at], v_ref[c, :, at]
            queries, ups = q_ref[c, :, at], do_ref[c, :, at]
            sums = []
            for half in range(2):
                scores = dot_nn(keys, half_rows(qt_ref[at, :], half)) + bias_ref[...]
                probs = jnp.exp(scores - lse_ref[c, pl.ds(2 * j + half, 1), :])
                pushed = dot_nn(values, half_rows(dot_ref[at, :], half))
                delta = (probs * (pushed - delta_ref[c, pl.ds(2 * j + half, 1), :])).astype(BF16)
                at_head = pl.ds(pl.multiple_of((2 * j + half) * E, E), E)
                dqt_ref[at_head, :] = dot_nn(kt_ref[at_head, :], delta)
                sums.append((dot_nn(delta, queries), dot_nn(probs.astype(BF16), ups)))
            low_half = lax.broadcasted_iota(jnp.int32, sums[0][0].shape, 1) < E
            dk_ref[:, at] = jnp.where(low_half, sums[0][0], sums[1][0]).astype(BF16)
            dv_ref[:, at] = jnp.where(low_half, sums[0][1], sums[1][1]).astype(BF16)

        grad_query = (dqt_ref[...] * 0.125).T.astype(BF16)
        base_ref[c] = d_one_ref[c] + dot_nt(grad_query, w_qkv_ref[0])
        acc_ref[0] += dot_tn(x_own_ref[c], grad_query)

        @pl.loop(0, tensors)
        def _(t):
            at = pl.ds(pl.multiple_of(t * rows, rows), rows)
            grad_keys, grad_values = dk_ref[at, :], dv_ref[at, :]
            part = dot_nt(grad_keys, w_qkv_ref[1]) + dot_nt(grad_values, w_qkv_ref[2])
            part_ref[t, c] = part.astype(BF16)
            block = x_all_ref[t, c]
            acc_ref[1] += dot_tn(block, grad_keys)
            acc_ref[2] += dot_tn(block, grad_values)

    for i in range(3):
        g_qkv_ref[i] = acc_ref[i].astype(BF16)


def body(
    x_post,
    x_dual,
    cot_post,
    cot_dual,
    segment_ids,
    w_qkv,
    w_out,
    w_up,
    w_down,
    gain_one,
    bias_one,
    gain_two,
    bias_two,
):
    tensors = lax.axis_size("tensor")
    rows, columns, width = x_post.shape
    length = tensors * rows
    heads = width // E
    share = w_up.shape[1]
    me = lax.axis_index("tensor")
    x_own = jnp.swapaxes(x_post, 0, 1)
    x_all = lax.all_gather(x_own, "tensor", axis=0)
    all_qkv = lax.all_gather(w_qkv, "tensor", axis=2, tiled=True)
    all_out = lax.all_gather(w_out, "tensor", axis=0, tiled=True)
    all_up = lax.all_gather(w_up, "tensor", axis=0)
    all_down = lax.all_gather(w_down, "tensor", axis=0)
    norms = jnp.stack([gain_one, bias_one, gain_two, bias_two])
    seg = segment_ids.astype(F32)
    seg_own = lax.dynamic_slice_in_dim(seg.T, me * rows, rows, axis=1)
    in_vmem = pl.BlockSpec(memory_space=pltpu.VMEM)
    params = pltpu.CompilerParams(vmem_limit_bytes=VMEM_BYTES)
    shape = jax.ShapeDtypeStruct
    tokens = columns * rows
    forward = pl.pallas_call(
        forward_kernel,
        out_shape=(
            shape((columns, rows, width), F32),
            shape((columns, rows, width), F32),
            shape((columns, rows, width), F32),
            shape((columns, rows, width), BF16),
            shape((columns, length, width), BF16),
            shape((columns, length, width), BF16),
            shape((columns, rows, width), BF16),
            shape((columns, heads, rows), F32),
            shape((columns, heads, rows), F32),
            shape((tensors, width, share), BF16),
            shape((tensors, width, share), BF16),
            shape((width, width), BF16),
            shape((4, width), F32),
        ),
        in_specs=[in_vmem] * 12,
        out_specs=(in_vmem,) * 13,
        scratch_shapes=[
            pltpu.VMEM((length, rows), F32),
            pltpu.VMEM((width, rows), BF16),
            pltpu.VMEM((width, length), BF16),
            pltpu.VMEM((width, rows), F32),
            pltpu.VMEM((tensors, tokens, share), BF16),
            pltpu.VMEM((tensors, rows, share), F32),
            pltpu.VMEM((tensors, tokens, share), BF16),
            pltpu.VMEM((tokens, width), BF16),
            pltpu.VMEM((tokens, width), BF16),
            pltpu.VMEM((tokens, width), BF16),
            pltpu.VMEM((tokens, width), BF16),
        ],
        compiler_params=params,
        name="forward",
    )
    (
        post_out,
        dual_out,
        d_one,
        query,
        keys,
        values,
        grad_mixed,
        lse,
        delta,
        g_down,
        g_up,
        g_out,
        g_norm,
    ) = forward(
        seg, seg_own, x_all, x_own,
        jnp.swapaxes(x_dual, 0, 1), jnp.swapaxes(cot_post, 0, 1), jnp.swapaxes(cot_dual, 0, 1),
        all_qkv, all_out, all_up, all_down, norms,
    )
    backward = pl.pallas_call(
        backward_kernel,
        out_shape=(
            shape((columns, rows, width), F32),
            shape((tensors, columns, rows, width), BF16),
            shape((3, width, width), BF16),
        ),
        in_specs=[in_vmem] * 12,
        out_specs=(in_vmem,) * 3,
        scratch_shapes=[
            pltpu.VMEM((length, rows), F32),
            pltpu.VMEM((width, rows), BF16),
            pltpu.VMEM((width, rows), BF16),
            pltpu.VMEM((width, length), BF16),
            pltpu.VMEM((length, width), BF16),
            pltpu.VMEM((length, width), BF16),
            pltpu.VMEM((width, rows), F32),
            pltpu.VMEM((3, width, width), F32),
        ],
        compiler_params=params,
        name="backward",
    )
    base, part, g_qkv = backward(
        seg, seg_own, x_all, x_own, all_qkv, d_one, query, keys, values, grad_mixed, lse, delta
    )
    grad_post = base + lax.psum_scatter(part, "tensor", scatter_dimension=0, tiled=False).astype(F32)

    def over_dp(array, dim):
        return lax.psum_scatter(array, "dp", scatter_dimension=dim, tiled=True)

    own = width // tensors
    r_qkv = lax.psum_scatter(over_dp(g_qkv, 1), "tensor", scatter_dimension=2, tiled=True)
    r_out = lax.psum_scatter(over_dp(g_out, 0), "tensor", scatter_dimension=1, tiled=True)
    r_up = lax.psum_scatter(over_dp(g_up, 1), "tensor", scatter_dimension=0, tiled=False)
    r_down = lax.psum_scatter(over_dp(g_down, 1), "tensor", scatter_dimension=0, tiled=False)
    norm_parts = lax.psum_scatter(g_norm, ("dp", "tensor"), scatter_dimension=1, tiled=True)
    return (
        jnp.swapaxes(post_out, 0, 1),
        jnp.swapaxes(dual_out, 0, 1),
        jnp.swapaxes(grad_post, 0, 1),
        r_qkv.astype(F32),
        r_out.astype(F32).T,
        r_up.astype(F32),
        r_down.astype(F32).T,
        norm_parts[0],
        norm_parts[1],
        norm_parts[2],
        norm_parts[3],
    )


def solution(mesh):
    placed = (
        P("tensor", "dp", None),
        P("tensor", "dp", None),
        P("tensor", "dp", None),
        P("tensor", "dp", None),
        P(None, "dp"),
        P(None, None, "tensor"),
        P("tensor", None),
        P(None, "tensor"),
        P("tensor", None),
        P(),
        P(),
        P(),
        P(),
    )
    return jax.shard_map(
        body,
        mesh=mesh,
        in_specs=placed,
        out_specs=(
            P("tensor", "dp", None),
            P("tensor", "dp", None),
            P("tensor", "dp", None),
            P(None, "dp", "tensor"),
            P("tensor", "dp"),
            P("dp", "tensor"),
            P("tensor", "dp"),
            P(("dp", "tensor")),
            P(("dp", "tensor")),
            P(("dp", "tensor")),
            P(("dp", "tensor")),
        ),
        check_vma=False,
    )
```

```python
import functools
import itertools

import jax
import jax.numpy as jnp
from jax import lax
from jax.experimental import pallas as pl
from jax.experimental.pallas import tpu as pltpu
from jax.sharding import PartitionSpec as P

E = 64
EPSILON = 1e-05
NEGATIVE = -1e30
GELU_A = 0.7978845608028654
GELU_B = 0.044715
F32 = jnp.float32
BF16 = jnp.bfloat16
VMEM_BYTES = 63 * 1024 * 1024
LINKS = 256


def dot_nn(a, b):
    return lax.dot_general(a, b, (((1,), (0,)), ((), ())), preferred_element_type=F32)


def dot_nt(a, b):
    return lax.dot_general(a, b, (((1,), (1,)), ((), ())), preferred_element_type=F32)


def dot_tn(a, b):
    return lax.dot_general(a, b, (((0,), (0,)), ((), ())), preferred_element_type=F32)


def row_mean(a):
    return jnp.mean(a, axis=-1, keepdims=True)


def norm_forward(total):
    centre = total - row_mean(total)
    factor = lax.rsqrt(row_mean(centre * centre) + EPSILON)
    return centre * factor, factor


def norm_backward(upstream, normed, factor, gain):
    scaled = upstream * gain
    inner = scaled - row_mean(scaled) - normed * row_mean(scaled * normed)
    return factor * inner


def half_rows(block, half):
    zeros = jnp.zeros((E, block.shape[1]), block.dtype)
    if half == 0:
        return jnp.concatenate([block[:E], zeros], axis=0)
    return jnp.concatenate([zeros, block[E:]], axis=0)


MESH = pl.DeviceIdType.MESH


def bit_of(index, bit):
    return (index // (1 << bit)) % 2


def flip(index, mask):
    for bit in range(mask.bit_length()):
        if (mask >> bit) % 2:
            index = index + (1 - 2 * bit_of(index, bit)) * (1 << bit)
    return index


def log2(count):
    return count.bit_length() - 1


class Links:
    def __init__(self, send_sem, recv_sem):
        self.send_sem, self.recv_sem, self.used = send_sem, recv_sem, 0

    def take(self, count):
        first = self.used
        self.used += count
        assert self.used <= self.send_sem.shape[0]
        return first

    def copy(self, src, dst, slot, axis, partner):
        return pltpu.make_async_remote_copy(
            src_ref=src,
            dst_ref=dst,
            send_sem=self.send_sem.at[slot],
            recv_sem=self.recv_sem.at[slot],
            device_id={axis: partner},
            device_id_type=MESH,
        )


def start(copies):
    for copy in copies:
        copy.start()


def finish(copies):
    for copy in copies:
        copy.wait_recv()
        copy.wait_send()


def greet(dp_bits, tensors):
    dp, me = lax.axis_index("dp"), lax.axis_index("tensor")
    barrier = pltpu.get_barrier_semaphore()
    for bit in range(dp_bits):
        pl.semaphore_signal(barrier, inc=1, device_id={"dp": flip(dp, 1 << bit)}, device_id_type=MESH)
    for step in range(1, tensors):
        pl.semaphore_signal(
            barrier, inc=1, device_id={"tensor": (me + step) % tensors}, device_id_type=MESH
        )
    pl.semaphore_wait(barrier, dp_bits + tensors - 1)


class WeightGather:
    def __init__(self, links, src, dst, lead, cut_bits, dp_bits, first):
        tensors = dst.shape[0]
        dp, me = lax.axis_index("dp"), lax.axis_index("tensor")
        bits = list(range(dp_bits - 1, dp_bits - 1 - cut_bits, -1))
        self.src, self.dst, self.own = src, dst, me
        inner = [()] if lead == 0 else [(i,) for i in range(src.shape[0])]
        self.across = []
        for step in range(1, tensors):
            piece = (slice(None),) * lead + tuple(bit_of(dp, bit) for bit in bits)
            self.across.append(
                links.copy(
                    src.at[piece],
                    dst.at[(me,) + piece],
                    links.take(1),
                    "tensor",
                    (me + step) % tensors,
                )
            )
        low = [bit for bit in bits if bit == 0]
        high = [bit for bit in bits if bit != 0]
        orders = (high[::-1] + low, high + low)
        self.phases = [[] for _ in bits]
        count = first
        for step in range(1, tensors):
            source = (me + tensors - step) % tensors
            for i in inner:
                order = orders[count % 2]
                count += 1
                for phase, bit in enumerate(order):
                    done = order[:phase]
                    region = (source,) + i + tuple(
                        slice(None) if other in done else bit_of(dp, other) for other in bits
                    )
                    self.phases[phase].append(
                        links.copy(
                            dst.at[region],
                            dst.at[region],
                            links.take(1),
                            "dp",
                            flip(dp, 1 << bit),
                        )
                    )

    def own_copy(self, sem):
        return pltpu.make_async_copy(self.src, self.dst.at[self.own], sem)


class GradScatter:
    def __init__(self, links, grad, lands, across):
        self.links, self.grad, self.lands, self.across = links, grad, lands, across
        self.tensors = grad.shape[0]
        self.dp, self.me = lax.axis_index("dp"), lax.axis_index("tensor")
        dp_bits = len(lands)
        high = list(range(dp_bits - 1, 0, -1))
        middle = self.tensors // 2
        first = links.take(1)
        copies = [
            [
                links.copy(
                    grad.at[(slice(None),) * dp_bits + (1 - bit_of(self.dp, 0),)],
                    lands[0],
                    first,
                    "dp",
                    flip(self.dp, 1),
                )
            ]
        ]
        sums = [[(0, self.tensors, grad, dp_bits - 1, bit_of(self.dp, 0), lands[0])]]
        for step in range(1, dp_bits):
            copies.append([])
            sums.append([])
        for begin, order in ((0, high[::-1]), (middle, high)):
            left = list(high)
            for step, bit in enumerate(order, 1):
                place = left.index(bit)
                left.remove(bit)
                part = pl.ds(begin, middle)
                index = (part,) + (slice(None),) * place + (1 - bit_of(self.dp, bit),)
                copies[step].append(
                    links.copy(
                        lands[step - 1].at[index],
                        lands[step].at[part],
                        links.take(1),
                        "dp",
                        flip(self.dp, 1 << bit),
                    )
                )
                sums[step].append(
                    (begin, middle, lands[step - 1], place, bit_of(self.dp, bit), lands[step])
                )
        last = []
        for step in range(1, self.tensors):
            other = (self.me + step) % self.tensors
            last.append(
                links.copy(
                    lands[-1].at[other], across.at[step - 1], links.take(1), "tensor", other
                )
            )
        copies.append(last)
        self.copies, self.sums = copies, sums

    def begin(self):
        start(self.copies[0])

    def advance(self, step):
        finish(self.copies[step])
        for first, count, source, place, own, land in self.sums[step]:

            @pl.loop(first, first + count)
            def _(t):
                for spot in itertools.product((0, 1), repeat=len(land.shape) - 3):
                    whole = (t,) + spot[:place] + (own,) + spot[place:]
                    here = (t,) + spot
                    land[here] = (land[here].astype(F32) + source[whole].astype(F32)).astype(BF16)

        start(self.copies[step + 1])

    def result(self):
        finish(self.copies[-1])
        total = self.lands[-1][self.me].astype(F32)
        for step in range(self.tensors - 1):
            total = total + self.across[step].astype(F32)
        return total


class NormSum:
    def __init__(self, links, total, land, dp_bits, tensors):
        dp, me = lax.axis_index("dp"), lax.axis_index("tensor")
        self.total, self.land = total, land
        self.copies = [
            [links.copy(total, land.at[bit], links.take(1), "dp", flip(dp, 1 << bit))]
            for bit in range(dp_bits)
        ]
        self.copies.append(
            [
                links.copy(
                    total,
                    land.at[dp_bits + step - 1],
                    links.take(1),
                    "tensor",
                    (me + step) % tensors,
                )
                for step in range(1, tensors)
            ]
        )

    def begin(self):
        start(self.copies[0])

    def advance(self, step):
        finish(self.copies[step])
        self.total[...] += self.land[step]
        start(self.copies[step + 1])

    def result(self):
        finish(self.copies[-1])
        total = self.total[...]
        for step in range(len(self.copies) - 1, self.land.shape[0]):
            total = total + self.land[step]
        return total


def layer_kernel(
    dp_bits,
    columns,
    seg_ref,
    x_ref,
    dual_in_ref,
    cot_post_ref,
    cot_dual_ref,
    w_qkv_ref,
    w_out_ref,
    w_up_ref,
    w_down_ref,
    norms_ref,
    post_ref,
    dual_ref,
    grad_post_ref,
    r_qkv_ref,
    r_ffn_ref,
    r_norm_ref,
    x_col_ref,
    all_qkv_ref,
    all_out_ref,
    all_up_ref,
    all_down_ref,
    mixed_ref,
    do_ref,
    input_land_ref,
    g_ffn_ref,
    g_qkv_ref,
    ffn_lands,
    ffn_across_ref,
    qkv_lands,
    qkv_across_ref,
    norm_ref,
    norm_land_ref,
    q_ref,
    k_ref,
    v_ref,
    qt_ref,
    kt_ref,
    xt_ref,
    ot_ref,
    lse_ref,
    base_ref,
    stage_ref,
    bias_ref,
    send_sem,
    recv_sem,
    local_sem,
):
    tensors, rows, width = x_col_ref.shape
    owners = tensors // columns
    lanes = mixed_ref.shape[-1]
    heads = lanes // E
    pairs = heads // 2
    share = all_up_ref.shape[-1]
    shard = width // tensors
    last = tensors - 1
    length = tensors * rows
    tokens = columns * rows
    me = lax.axis_index("tensor")
    me_low = me % owners
    links = Links(send_sem, recv_sem)

    def slot_copies(sources, land):
        first = links.take(last)

        def one(slot, partner):
            source = sources.at[slot, :, pl.ds(0, land.shape[-1])]
            return links.copy(source, land.at[slot], first + slot, "tensor", partner)

        return one

    def partner_of(slot):
        mask = last - slot
        index = me
        for bit in range(log2(tensors)):
            index = index + bit_of(mask, bit) * (1 - 2 * bit_of(me, bit)) * (1 << bit)
        return index

    def gather(src, dst, lead, first):
        return WeightGather(links, src, dst, lead, len(src.shape) - lead - 2, dp_bits, first)

    qkv = gather(w_qkv_ref, all_qkv_ref, 1, 0)
    others = [
        gather(w_out_ref, all_out_ref, 0, 0),
        gather(w_up_ref, all_up_ref, 0, 0),
        gather(w_down_ref, all_down_ref, 0, 1),
    ]
    others_across = [copy for one in others for copy in one.across]
    others_phases = [
        [copy for one in others if len(one.phases) > phase for copy in one.phases[phase]]
        for phase in range(dp_bits)
    ]
    x_first = links.take(last)

    def x_copy(slot):
        partner = partner_of(slot)
        return links.copy(
            x_ref.at[partner // owners], x_col_ref.at[slot], x_first + slot, "tensor", partner
        )

    mixed_copy = slot_copies(stage_ref, mixed_ref)
    do_copy = slot_copies(stage_ref, do_ref)
    input_copy = slot_copies(stage_ref, input_land_ref)
    ffn_scatter = GradScatter(links, g_ffn_ref, ffn_lands, ffn_across_ref)
    qkv_scatter = GradScatter(links, g_qkv_ref, qkv_lands, qkv_across_ref)
    norm_sum = NormSum(links, norm_ref, norm_land_ref, dp_bits, tensors)

    local = [pltpu.make_async_copy(x_ref.at[me // owners], x_col_ref.at[last], local_sem.at[0])] + [
        one.own_copy(local_sem.at[1 + i]) for i, one in enumerate([qkv] + others)
    ]
    greet(dp_bits, tensors)
    start(qkv.across)
    start([x_copy(slot) for slot in range(last)])
    start(local)
    norm_ref[...] = jnp.zeros_like(norm_ref)
    if owners > 1:
        g_qkv_ref[...] = jnp.zeros_like(g_qkv_ref)
    finish(qkv.across)
    for copies in qkv.phases:
        start(copies)
        finish(copies)
    for copy in local:
        copy.wait()
    start(others_across)

    own_shards = pl.ds(me_low * (tensors // owners), tensors // owners)

    def w_t(i):
        return all_qkv_ref[own_shards, i].reshape(lanes, width)

    @pl.loop(0, tensors)
    def _(turn):
        slot = last - turn

        @pl.when(slot < last)
        def _():
            x_copy(slot).wait_recv()

        block = x_col_ref[slot]
        at = pl.ds(pl.multiple_of(slot * rows, rows), rows)
        q_ref[at, :] = dot_nt(block, w_t(0)).astype(BF16) * jnp.bfloat16(0.125)
        k_ref[at, :] = dot_nt(block, w_t(1)).astype(BF16)
        v_ref[at, :] = dot_nt(block, w_t(2)).astype(BF16)
        qt_ref[:, at] = dot_nt(w_t(0), block).astype(BF16) * jnp.bfloat16(0.125)
        kt_ref[:, at] = dot_nt(w_t(1), block).astype(BF16)
        xt_ref[:, at] = block.T

    seg_columns = seg_ref[...].T

    def bias_of(q_slot, k_slot):
        lane = lax.broadcasted_iota(jnp.int32, seg_columns.shape, 1)
        keys = jnp.sum(jnp.where(lane == k_slot, seg_columns, 0.0), axis=1, keepdims=True)
        return jnp.where(keys == seg_ref[pl.ds(q_slot, 1), :], 0.0, NEGATIVE)

    def forward_phase(
        vt_ref,
        hidden_ref,
        slope_ref,
        grad_inner_ref,
        up_two_ref,
        middle_ref,
        up_one_ref,
        home_ref,
        out_stage_ref,
    ):
        @pl.loop(0, tensors)
        def _(slot):
            at = pl.ds(pl.multiple_of(slot * rows, rows), rows)
            vt_ref[:, at] = dot_nt(w_t(2), x_col_ref[slot]).astype(BF16)

        @pl.loop(0, tensors)
        def _(slot):
            at_rows = pl.ds(pl.multiple_of(slot * rows, rows), rows)
            for k_slot in range(tensors):
                bias_ref[k_slot * rows : (k_slot + 1) * rows, :] = bias_of(slot, k_slot)

            @pl.loop(0, pairs)
            def _(j):
                @pl.when(slot == 0)
                def _():
                    for phase in range(dp_bits):

                        @pl.when(j == min(phase, pairs - 1))
                        def _():
                            finish(others_phases[phase - 1] if phase else others_across)
                            start(others_phases[phase])

                at = pl.ds(pl.multiple_of(j * 2 * E, 2 * E), 2 * E)
                keys = k_ref[:, at]
                queries = qt_ref[at, at_rows]
                for half in range(2):
                    scores = dot_nn(keys, half_rows(queries, half)) + bias_ref[...]
                    top = jnp.max(scores, axis=0, keepdims=True)
                    raised = jnp.exp(scores - top)
                    denom = jnp.sum(raised, axis=0, keepdims=True)
                    at_head = pl.ds(pl.multiple_of((2 * j + half) * E, E), E)
                    result = dot_nn(vt_ref[at_head, :], raised.astype(BF16))
                    ot_ref[slot, at_head, :] = result * (1.0 / denom)
                    lse_ref[slot, pl.ds(2 * j + half, 1), :] = top + jnp.log(denom)

            block = ot_ref[slot].T.astype(BF16)

            @pl.when(slot < last)
            def _():
                stage_ref[slot, :, :lanes] = block
                mixed_copy(slot, partner_of(slot)).start()

            @pl.when(slot == last)
            def _():
                mixed_ref[last] = block

        finish(others_phases[-1])
        gain_one, bias_one = norms_ref[0:1, :], norms_ref[1:2, :]
        gain_two, bias_two = norms_ref[2:3, :], norms_ref[3:4, :]

        @pl.loop(0, columns)
        def _(i):
            column = partner_of(owners * i) // owners
            loads = [
                pltpu.make_async_copy(ref.at[column], home_ref.at[n], local_sem.at[n])
                for n, ref in enumerate((x_ref, dual_in_ref, cot_post_ref, cot_dual_ref))
            ]
            start(loads)
            for r in range(owners):

                @pl.when(owners * i + r < last)
                def _():
                    mixed_copy(owners * i + r, partner_of(owners * i + r)).wait()

            def slot_of(h):
                return last - owners * (columns - 1 - i) - flip(me_low, h)

            mixed = jnp.concatenate([mixed_ref[slot_of(h)] for h in range(owners)], axis=1)
            at = pl.ds(pl.multiple_of(i * rows, rows), rows)
            branch_one = dot_nn(mixed, all_out_ref[...].reshape(width, width))
            for copy in loads:
                copy.wait()
            normed_one, factor_one = norm_forward(home_ref[0].astype(F32) + branch_one)
            middle = normed_one * gain_one + bias_one
            middle_low = middle.astype(BF16)
            middle_ref[:, at] = middle_low.T
            branch_two = jnp.zeros((rows, width), F32)
            for t in range(tensors):
                inner = dot_nn(middle_low, all_up_ref[t].reshape(width, share))
                square = inner * inner
                bend = jnp.tanh(GELU_A * (inner + GELU_B * (square * inner)))
                hidden = (0.5 * inner * (1.0 + bend)).astype(BF16)
                slope_ref[t] = 0.5 * (1.0 + bend) + (0.5 * GELU_A) * inner * (
                    1.0 - bend * bend
                ) * (1.0 + (3.0 * GELU_B) * square)
                hidden_ref[t, at, :] = hidden
                branch_two = branch_two + dot_nn(hidden, all_down_ref[t].reshape(share, width))
            normed_two, factor_two = norm_forward(middle + branch_two)
            stores = [
                pltpu.make_async_copy(out_stage_ref.at[n], ref.at[column], local_sem.at[4 + n])
                for n, ref in enumerate((post_ref, dual_ref))
            ]

            @pl.when(i > 0)
            def _():
                for copy in stores:
                    copy.wait()

            out_stage_ref[0] = normed_two * gain_two + bias_two
            out_stage_ref[1] = home_ref[1].astype(F32) + branch_one + branch_two
            start(stores)
            cot_dual = home_ref[3].astype(F32)
            upstream = home_ref[2].astype(F32)
            d_two = norm_backward(upstream, normed_two, factor_two, gain_two)
            norm_ref[2:3, :] += jnp.sum(upstream * normed_two, axis=0, keepdims=True)
            norm_ref[3:4, :] += jnp.sum(upstream, axis=0, keepdims=True)
            up_two = (d_two + cot_dual).astype(BF16)
            up_two_ref[:, at] = up_two.T
            grad_middle = d_two
            for t in range(tensors):
                grad_hidden = dot_nt(up_two, all_down_ref[t].reshape(share, width))
                grad_inner = (grad_hidden * slope_ref[t]).astype(BF16)
                grad_inner_ref[t, at, :] = grad_inner
                grad_middle = grad_middle + dot_nt(grad_inner, all_up_ref[t].reshape(width, share))
            d_one = norm_backward(grad_middle, normed_one, factor_one, gain_one)
            norm_ref[0:1, :] += jnp.sum(grad_middle * normed_one, axis=0, keepdims=True)
            norm_ref[1:2, :] += jnp.sum(grad_middle, axis=0, keepdims=True)
            base_ref[column] = d_one
            up_one = (d_one + cot_dual).astype(BF16)
            up_one_ref[:, at] = up_one.T
            grad_mixed = dot_nt(up_one, all_out_ref[...].reshape(width, width)).astype(BF16)
            for h in range(owners):
                slot = slot_of(h)
                piece = grad_mixed[:, h * lanes : (h + 1) * lanes]

                @pl.when(slot < last)
                def _():
                    stage_ref[slot, :, :lanes] = piece
                    do_copy(slot, partner_of(slot)).start()

                @pl.when(slot == last)
                def _():
                    do_ref[last] = piece

            @pl.when(i == columns - 1)
            def _():
                for copy in stores:
                    copy.wait()

        norm_sum.begin()
        cut = (2,) * dp_bits + (width >> dp_bits, share)

        @pl.loop(0, tensors)
        def _(t):
            g_down = dot_nn(up_two_ref[...], hidden_ref[t]).astype(BF16)
            g_up = dot_nn(middle_ref[...], grad_inner_ref[t]).astype(BF16)
            at_t = (t,) + (slice(None),) * (dp_bits + 1)
            g_ffn_ref[at_t + (slice(0, share),)] = g_down.reshape(cut)
            g_ffn_ref[at_t + (slice(share, 2 * share),)] = g_up.reshape(cut)

        def mixed_of(i):
            def slot_of(h):
                return last - owners * (columns - 1 - i) - flip(me_low, h)

            return jnp.concatenate([mixed_ref[slot_of(h)] for h in range(owners)], axis=1)

        all_mixed = jnp.concatenate([mixed_of(i) for i in range(columns)], axis=0)
        g_out = dot_nn(up_one_ref[...], all_mixed).astype(BF16)
        for t in range(tensors):
            g_ffn_ref[
                (t,) + (slice(None),) * (dp_bits + 1) + (slice(2 * share, 2 * share + shard),)
            ] = g_out[:, t * shard : (t + 1) * shard].reshape(cut[:-1] + (shard,))
        ffn_scatter.begin()

    pl.run_scoped(
        forward_phase,
        pltpu.VMEM((lanes, length), BF16),
        pltpu.VMEM((tensors, tokens, share), BF16),
        pltpu.VMEM((tensors, rows, share), F32),
        pltpu.VMEM((tensors, tokens, share), BF16),
        pltpu.VMEM((width, tokens), BF16),
        pltpu.VMEM((width, tokens), BF16),
        pltpu.VMEM((width, tokens), BF16),
        pltpu.VMEM((4, rows, width), BF16),
        pltpu.VMEM((2, rows, width), F32),
    )

    def backward_phase(dot_ref, delta_ref, dq_ref, dk_ref, dv_ref, grads_ref):
        dq_ref[...] = jnp.zeros_like(dq_ref)
        dk_ref[...] = jnp.zeros_like(dk_ref)
        dv_ref[...] = jnp.zeros_like(dv_ref)

        @pl.loop(0, tensors)
        def _(slot):
            @pl.when(slot < last)
            def _():
                do_copy(slot, partner_of(slot)).wait()

            at = pl.ds(pl.multiple_of(slot * rows, rows), rows)
            turned = do_ref[slot].T
            dot_ref[:, at] = turned
            product = turned.astype(F32) * ot_ref[slot]
            delta_ref[slot, :heads] = jnp.sum(product.reshape(heads, E, rows), axis=1)

        def pair_of(q_slot, k_slot):
            at_q = pl.ds(pl.multiple_of(q_slot * rows, rows), rows)
            at_k = pl.ds(pl.multiple_of(k_slot * rows, rows), rows)
            bias_ref[:rows, :] = bias_of(q_slot, k_slot)

            @pl.loop(0, pairs)
            def _(j):
                at = pl.ds(pl.multiple_of(j * 2 * E, 2 * E), 2 * E)
                keys, values = k_ref[at_k, at], v_ref[at_k, at]
                queries, ups = q_ref[at_q, at], do_ref[q_slot, :, at]
                sums = []
                for half in range(2):
                    row = pl.ds(2 * j + half, 1)
                    scores = dot_nn(keys, half_rows(qt_ref[at, at_q], half)) + bias_ref[:rows, :]
                    probs = jnp.exp(scores - lse_ref[q_slot, row, :])
                    pushed = dot_nn(values, half_rows(dot_ref[at, at_q], half))
                    delta = (probs * (pushed - delta_ref[q_slot, row, :])).astype(BF16)
                    at_head = pl.ds(pl.multiple_of((2 * j + half) * E, E), E)
                    dq_ref[at_head, at_q] += dot_nn(kt_ref[at_head, at_k], delta)
                    sums.append((dot_nn(delta, queries), dot_nn(probs.astype(BF16), ups)))
                low_half = lax.broadcasted_iota(jnp.int32, sums[0][0].shape, 1) < E
                dk_ref[at_k, at] += jnp.where(low_half, sums[0][0], sums[1][0])
                dv_ref[at_k, at] += jnp.where(low_half, sums[0][1], sums[1][1])

        @pl.loop(0, tensors)
        def _(wave):
            for step in range(1, dp_bits):

                @pl.when(wave == step)
                def _():
                    ffn_scatter.advance(step)
                    norm_sum.advance(step)

            @pl.loop(wave, tensors)
            def _(k_slot):
                @pl.when((wave == 0) & (k_slot == 1))
                def _():
                    ffn_scatter.advance(0)
                    norm_sum.advance(0)

                pair_of(wave, k_slot)

            @pl.loop(wave + 1, tensors)
            def _(q_slot):
                pair_of(q_slot, wave)

            at = pl.ds(pl.multiple_of(wave * rows, rows), rows)
            grads = (
                (dq_ref[:, at] * 0.125).T.astype(BF16),
                dk_ref[at, :].astype(BF16),
                dv_ref[at, :].astype(BF16),
            )
            part = jnp.zeros((rows, width), F32)
            for i in range(3):
                grads_ref[i, at, :] = grads[i]
                part = part + dot_nn(grads[i], w_t(i))

            @pl.when(wave < last)
            def _():
                stage_ref[wave] = part.astype(BF16)
                input_copy(wave, partner_of(wave)).start()

            @pl.when(wave == last)
            def _():
                base_ref[me // owners] += part

        for i in range(3):
            g = dot_nn(xt_ref[...], grads_ref[i]).astype(BF16)
            for t in range(tensors // owners):
                index = (me_low * (tensors // owners) + t,) + (slice(None),) * (dp_bits + 1)
                g_qkv_ref[index + (slice(i * shard, (i + 1) * shard),)] = g[
                    :, t * shard : (t + 1) * shard
                ].reshape((2,) * dp_bits + (width >> dp_bits, shard))

    pl.run_scoped(
        backward_phase,
        pltpu.VMEM((lanes, length), BF16),
        pltpu.VMEM((tensors, max(heads, 8), rows), F32),
        pltpu.VMEM((lanes, length), F32),
        pltpu.VMEM((length, lanes), F32),
        pltpu.VMEM((length, lanes), F32),
        pltpu.VMEM((3, length, lanes), BF16),
    )

    qkv_scatter.begin()
    for slot in range(last):
        x_copy(slot).wait_send()

    @pl.loop(0, last)
    def _(slot):
        input_copy(slot, partner_of(slot)).wait()
        base_ref[partner_of(slot) // owners] += input_land_ref[slot].astype(F32)

    stored = pltpu.make_async_copy(base_ref, grad_post_ref, local_sem.at[0])
    stored.start()
    qkv_scatter.advance(0)
    r_ffn_ref[...] = ffn_scatter.result()
    r_norm_ref[...] = norm_sum.result()
    for step in range(1, dp_bits):
        qkv_scatter.advance(step)
    r_qkv_ref[...] = qkv_scatter.result()
    stored.wait()


def body(
    x_post,
    x_dual,
    cot_post,
    cot_dual,
    segment_ids,
    w_qkv,
    w_out,
    w_up,
    w_down,
    gain_one,
    bias_one,
    gain_two,
    bias_two,
):
    tensors, devices = lax.axis_size("tensor"), lax.axis_size("dp")
    dp_bits = log2(devices)
    rows, columns, width = x_post.shape
    length = tensors * rows
    owners = tensors // columns
    lanes = width // owners
    share, shard = w_up.shape[1], w_out.shape[0]
    piece = width // devices
    heads = lanes // E
    me = lax.axis_index("tensor")
    norms = jnp.stack([gain_one, bias_one, gain_two, bias_two])

    def cut(array, dim):
        bits = min(dp_bits, log2(array.shape[dim] // 16))
        shape = array.shape[:dim] + (2,) * bits + (array.shape[dim] >> bits,) + array.shape[dim + 1 :]
        return array.reshape(shape)

    shards = [cut(jnp.swapaxes(w_qkv, 1, 2), 1), cut(w_out, 0), cut(w_up, 0), cut(w_down, 0)]
    own = lax.dynamic_slice_in_dim(segment_ids.T, me // owners, 1, axis=0).reshape(tensors, rows)
    seg = jnp.stack(
        [
            lax.dynamic_index_in_dim(own, flip(me, tensors - 1 - slot), 0, keepdims=False)
            for slot in range(tensors)
        ]
    ).astype(F32)
    seg = jnp.pad(seg, ((0, -tensors % 8), (0, 0)))
    in_vmem = pl.BlockSpec(memory_space=pltpu.VMEM)
    in_place = pl.BlockSpec(memory_space=pl.ANY)
    shape = jax.ShapeDtypeStruct
    bits = (2,) * dp_bits
    ffn_lanes = 2 * share + shard

    def lands(lane_count):
        return [
            pltpu.VMEM((tensors,) + bits[: dp_bits - 1 - step] + (piece, lane_count), BF16)
            for step in range(dp_bits)
        ]

    layer = pl.pallas_call(
        functools.partial(layer_kernel, dp_bits, columns),
        out_shape=(
            shape((columns, rows, width), F32),
            shape((columns, rows, width), F32),
            shape((columns, rows, width), F32),
            shape((piece, 3 * shard), F32),
            shape((piece, ffn_lanes), F32),
            shape((8, width), F32),
        ),
        in_specs=[in_vmem] + [in_place] * 8 + [in_vmem],
        out_specs=(in_place,) * 3 + (in_vmem,) * 3,
        scratch_shapes=[pltpu.VMEM((tensors, rows, width), BF16)]
        + [pltpu.VMEM((tensors,) + one.shape, BF16) for one in shards]
        + [
            pltpu.VMEM((tensors, rows, lanes), BF16),
            pltpu.VMEM((tensors, rows, lanes), BF16),
            pltpu.VMEM((tensors - 1, rows, width), BF16),
            pltpu.VMEM((tensors,) + bits + (piece, ffn_lanes), BF16),
            pltpu.VMEM((tensors,) + bits + (piece, 3 * shard), BF16),
            lands(ffn_lanes),
            pltpu.VMEM((tensors - 1, piece, ffn_lanes), BF16),
            lands(3 * shard),
            pltpu.VMEM((tensors - 1, piece, 3 * shard), BF16),
            pltpu.VMEM((8, width), F32),
            pltpu.VMEM((dp_bits + tensors - 1, 8, width), F32),
            pltpu.VMEM((length, lanes), BF16),
            pltpu.VMEM((length, lanes), BF16),
            pltpu.VMEM((length, lanes), BF16),
            pltpu.VMEM((lanes, length), BF16),
            pltpu.VMEM((lanes, length), BF16),
            pltpu.VMEM((width, length), BF16),
            pltpu.VMEM((tensors, lanes, rows), F32),
            pltpu.VMEM((tensors, max(heads, 8), rows), F32),
            pltpu.VMEM((columns, rows, width), F32),
            pltpu.VMEM((tensors - 1, rows, width), BF16),
            pltpu.VMEM((length, rows), F32),
            pltpu.SemaphoreType.DMA((LINKS,)),
            pltpu.SemaphoreType.DMA((LINKS,)),
            pltpu.SemaphoreType.DMA((8,)),
        ],
        compiler_params=pltpu.CompilerParams(
            vmem_limit_bytes=VMEM_BYTES, collective_id=0, has_side_effects=True
        ),
        name="layer",
    )
    post_out, dual_out, grad_post, r_qkv, r_ffn, r_norm = layer(
        seg,
        jnp.swapaxes(x_post, 0, 1),
        jnp.swapaxes(x_dual, 0, 1),
        jnp.swapaxes(cot_post, 0, 1),
        jnp.swapaxes(cot_dual, 0, 1),
        *shards,
        norms,
    )
    count = width // (tensors * devices)
    own_norms = lax.dynamic_slice_in_dim(
        r_norm, (lax.axis_index("dp") * tensors + me) * count, count, axis=1
    )
    return (
        jnp.swapaxes(post_out, 0, 1),
        jnp.swapaxes(dual_out, 0, 1),
        jnp.swapaxes(grad_post, 0, 1),
        jnp.swapaxes(r_qkv.reshape(piece, 3, shard), 0, 1),
        r_ffn[:, 2 * share :].T,
        r_ffn[:, share : 2 * share],
        r_ffn[:, :share].T,
        own_norms[0],
        own_norms[1],
        own_norms[2],
        own_norms[3],
    )


def solution(mesh):
    placed = (
        P("tensor", "dp", None),
        P("tensor", "dp", None),
        P("tensor", "dp", None),
        P("tensor", "dp", None),
        P(None, "dp"),
        P(None, None, "tensor"),
        P("tensor", None),
        P(None, "tensor"),
        P("tensor", None),
        P(),
        P(),
        P(),
        P(),
    )
    return jax.shard_map(
        body,
        mesh=mesh,
        in_specs=placed,
        out_specs=(
            P("tensor", "dp", None),
            P("tensor", "dp", None),
            P("tensor", "dp", None),
            P(None, "dp", "tensor"),
            P("tensor", "dp"),
            P("dp", "tensor"),
            P("tensor", "dp"),
            P(("dp", "tensor")),
            P(("dp", "tensor")),
            P(("dp", "tensor")),
            P(("dp", "tensor")),
        ),
        check_vma=False,
    )
```

```python
import functools
import itertools

import jax
import jax.numpy as jnp
from jax import lax
from jax.experimental import pallas as pl
from jax.experimental.pallas import tpu as pltpu
from jax.sharding import PartitionSpec as P

E = 64
EPSILON = 1e-05
NEGATIVE = -1e30
DOCUMENTS = 4
DOWN_DUES = (0.06, 0.35, 0.75)
UP_DUES = (0.10, 0.5, 0.9)
GATHER_DUE, GATHER_LEVEL, GATHER_STEP = 6, 4, 3
PARTS = 3
GELU_A = 0.7978845608028654
GELU_B = 0.044715
F32 = jnp.float32
BF16 = jnp.bfloat16
VMEM_BYTES = 63 * 1024 * 1024
LINKS = 320


def dot_nn(a, b):
    return lax.dot_general(a, b, (((1,), (0,)), ((), ())), preferred_element_type=F32)


def dot_nt(a, b):
    return lax.dot_general(a, b, (((1,), (1,)), ((), ())), preferred_element_type=F32)


def dot_tn(a, b):
    return lax.dot_general(a, b, (((0,), (0,)), ((), ())), preferred_element_type=F32)


def row_mean(a):
    return jnp.mean(a, axis=-1, keepdims=True)


def norm_forward(total):
    centre = total - row_mean(total)
    factor = lax.rsqrt(row_mean(centre * centre) + EPSILON)
    return centre * factor, factor


def norm_backward(upstream, normed, factor, gain):
    scaled = upstream * gain
    inner = scaled - row_mean(scaled) - normed * row_mean(scaled * normed)
    return factor * inner


def with_marks(block, marks):
    return jnp.concatenate([block, marks], axis=0)


def with_row(marks, row):
    line = lax.broadcasted_iota(jnp.int32, (16, row.shape[1]), 0)
    top = marks[:16].astype(F32)
    rest = -row
    for part in range(PARTS):
        term = rest.astype(BF16).astype(F32)
        rest = rest - term
        top = jnp.where(line == DOCUMENTS + part, term, top)
    return jnp.concatenate([top.astype(BF16), marks[16:]], axis=0)


def half_rows(block, half):
    zeros = jnp.zeros((E, block.shape[1]), block.dtype)
    if half == 0:
        return jnp.concatenate([block[:E], zeros], axis=0)
    return jnp.concatenate([zeros, block[E:]], axis=0)


MESH = pl.DeviceIdType.MESH


def bit_of(index, bit):
    return (index // (1 << bit)) % 2


def flip(index, mask):
    for bit in range(mask.bit_length()):
        if (mask >> bit) % 2:
            index = index + (1 - 2 * bit_of(index, bit)) * (1 << bit)
    return index


def log2(count):
    return count.bit_length() - 1


class Links:
    def __init__(self, send_sem, recv_sem):
        self.send_sem, self.recv_sem, self.used = send_sem, recv_sem, 0

    def take(self, count):
        first = self.used
        self.used += count
        assert self.used <= self.send_sem.shape[0]
        return first

    def copy(self, src, dst, slot, axis, partner):
        return pltpu.make_async_remote_copy(
            src_ref=src,
            dst_ref=dst,
            send_sem=self.send_sem.at[slot],
            recv_sem=self.recv_sem.at[slot],
            device_id={axis: partner},
            device_id_type=MESH,
        )


def start(copies):
    for copy in copies:
        copy.start()


def finish(copies):
    for copy in copies:
        copy.wait_recv()
        copy.wait_send()


def greet(dp_bits, tensors):
    dp, me = lax.axis_index("dp"), lax.axis_index("tensor")
    barrier = pltpu.get_barrier_semaphore()
    for bit in range(dp_bits):
        pl.semaphore_signal(barrier, inc=1, device_id={"dp": flip(dp, 1 << bit)}, device_id_type=MESH)
    for step in range(1, tensors):
        pl.semaphore_signal(
            barrier, inc=1, device_id={"tensor": (me + step) % tensors}, device_id_type=MESH
        )


def greeted(dp_bits, tensors):
    pl.semaphore_wait(pltpu.get_barrier_semaphore(), dp_bits + tensors - 1)


class WeightGather:
    def __init__(self, links, src, dst, lead, cut_bits, dp_bits, first, direct):
        tensors = dst.shape[0]
        dp, me = lax.axis_index("dp"), lax.axis_index("tensor")
        bits = list(range(dp_bits - 1, dp_bits - 1 - cut_bits, -1))
        if src is None:
            src = dst.at[me]
        self.src, self.dst, self.own = src, dst, me
        inner = [()] if lead == 0 else [(i,) for i in range(dst.shape[1])]
        piece = (slice(None),) * lead + tuple(bit_of(dp, bit) for bit in bits)
        low = [bit for bit in bits if bit == 0]
        high = [bit for bit in bits if bit != 0]
        orders = (high[::-1] + low, high + low)
        count = first
        self.stages = {}
        for mask in range(1, tensors):
            near = mask if direct else mask & -mask
            block = flip(me, mask - near)
            stages = [[] for _ in range(1 + dp_bits)]
            stages[0].append(
                links.copy(
                    dst.at[(block,) + piece] if mask != near else src.at[piece],
                    dst.at[(block,) + piece],
                    links.take(1),
                    "tensor",
                    flip(me, near),
                )
            )
            source = flip(me, mask)
            for i in inner:
                order = orders[count % 2]
                count += 1
                for phase, bit in enumerate(order):
                    done = order[:phase]
                    region = (source,) + i + tuple(
                        slice(None) if other in done else bit_of(dp, other) for other in bits
                    )
                    stages[1 + phase].append(
                        links.copy(
                            dst.at[region],
                            dst.at[region],
                            links.take(1),
                            "dp",
                            flip(dp, 1 << bit),
                        )
                    )
            self.stages[mask] = stages

    def own_copy(self, sem):
        return pltpu.make_async_copy(self.src, self.dst.at[self.own], sem)


class Stages:
    def __init__(self, weights, masks):
        count = len(weights[0].stages[masks[0]])
        self.copies = [
            [copy for one in weights for mask in masks for copy in one.stages[mask][stage]]
            for stage in range(count)
        ]
        self.count = count

    def begin(self):
        start(self.copies[0])

    def advance(self, stage):
        finish(self.copies[stage])
        if stage + 1 < self.count:
            start(self.copies[stage + 1])


class GradScatter:
    def __init__(self, links, grad, lands, across, direct):
        self.links, self.grad, self.lands, self.across = links, grad, lands, across
        self.tensors = grad.shape[0]
        self.dp, self.me = lax.axis_index("dp"), lax.axis_index("tensor")
        dp_bits = len(lands)
        high = list(range(dp_bits - 1, 0, -1))
        middle = self.tensors // 2
        first = links.take(1)
        copies = [
            [
                links.copy(
                    grad.at[(slice(None),) * dp_bits + (1 - bit_of(self.dp, 0),)],
                    lands[0],
                    first,
                    "dp",
                    flip(self.dp, 1),
                )
            ]
        ]
        sums = [[(0, self.tensors, grad, dp_bits - 1, bit_of(self.dp, 0), lands[0])]]
        for step in range(1, dp_bits):
            copies.append([])
            sums.append([])
        for begin, order in ((0, high[::-1]), (middle, high)):
            left = list(high)
            for step, bit in enumerate(order, 1):
                place = left.index(bit)
                left.remove(bit)
                part = pl.ds(begin, middle)
                index = (part,) + (slice(None),) * place + (1 - bit_of(self.dp, bit),)
                copies[step].append(
                    links.copy(
                        lands[step - 1].at[index],
                        lands[step].at[part],
                        links.take(1),
                        "dp",
                        flip(self.dp, 1 << bit),
                    )
                )
                sums[step].append(
                    (begin, middle, lands[step - 1], place, bit_of(self.dp, bit), lands[step])
                )
        place = 0
        self.joins = []
        for bit in range(0 if direct else log2(self.tensors)):
            step, found, joins = 1 << bit, [], []
            for high in range(self.tensors >> (bit + 1)):
                mask = high * 2 * step
                found.append(
                    links.copy(
                        lands[-1].at[flip(self.me, mask + step)],
                        across.at[place],
                        links.take(1),
                        "tensor",
                        flip(self.me, step),
                    )
                )
                joins.append((mask, place))
                place += 1
            copies.append(found)
            self.joins.append(joins)
        if direct:
            copies.append(
                [
                    links.copy(
                        lands[-1].at[flip(self.me, step)],
                        across.at[step - 1],
                        links.take(1),
                        "tensor",
                        flip(self.me, step),
                    )
                    for step in range(1, self.tensors)
                ]
            )
            self.joins = [[(0, step) for step in range(self.tensors - 1)]]
        self.copies, self.sums = copies, sums + [[] for _ in self.joins[1:]]
        self.steps = len(copies) - 1

    def begin(self):
        start(self.copies[0])

    def advance(self, step):
        finish(self.copies[step])
        for first, count, source, place, own, land in self.sums[step]:

            @pl.loop(first, first + count)
            def _(t):
                for spot in itertools.product((0, 1), repeat=len(land.shape) - 3):
                    whole = (t,) + spot[:place] + (own,) + spot[place:]
                    here = (t,) + spot
                    land[here] = (land[here].astype(F32) + source[whole].astype(F32)).astype(BF16)

        if step >= len(self.lands):
            for mask, place in self.joins[step - len(self.lands)]:
                spot = flip(self.me, mask)
                total = self.lands[-1][spot].astype(F32) + self.across[place].astype(F32)
                self.lands[-1][spot] = total.astype(BF16)
        start(self.copies[step + 1])

    def result(self):
        finish(self.copies[-1])
        total = self.lands[-1][self.me].astype(F32)
        for _, place in self.joins[-1]:
            total = total + self.across[place].astype(F32)
        return total


class NormSum:
    def __init__(self, links, total, land, dp_bits, tensors):
        dp, me = lax.axis_index("dp"), lax.axis_index("tensor")
        self.total, self.land = total, land
        self.copies = [
            [links.copy(total, land.at[bit], links.take(1), "dp", flip(dp, 1 << bit))]
            for bit in range(dp_bits)
        ]
        self.copies.append(
            [
                links.copy(
                    total,
                    land.at[dp_bits + step - 1],
                    links.take(1),
                    "tensor",
                    (me + step) % tensors,
                )
                for step in range(1, tensors)
            ]
        )

    def begin(self):
        start(self.copies[0])

    def advance(self, step):
        if step + 1 < len(self.copies):
            finish(self.copies[step])
            self.total[...] += self.land[step]
            start(self.copies[step + 1])

    def result(self):
        finish(self.copies[-1])
        total = self.total[...]
        for step in range(len(self.copies) - 1, self.land.shape[0]):
            total = total + self.land[step]
        return total


def layer_kernel(
    dp_bits,
    columns,
    seg_ref,
    x_ref,
    dual_in_ref,
    cot_post_ref,
    cot_dual_ref,
    w_qkv_ref,
    w_out_ref,
    w_up_ref,
    w_down_ref,
    gain_one_ref,
    bias_one_ref,
    gain_two_ref,
    bias_two_ref,
    post_ref,
    dual_ref,
    grad_post_ref,
    r_qkv_ref,
    r_down_ref,
    r_up_ref,
    r_norm_ref,
    home_ref,
    x_col_ref,
    all_qkv_ref,
    all_out_ref,
    all_up_ref,
    all_down_ref,
    mixed_ref,
    do_ref,
    input_land_ref,
    g_down_ref,
    g_up_ref,
    g_qkv_ref,
    down_lands,
    down_across_ref,
    up_lands,
    up_across_ref,
    qkv_lands,
    qkv_across_ref,
    norm_ref,
    norm_land_ref,
    q_ref,
    k_ref,
    v_ref,
    qt_ref,
    kt_ref,
    xt_ref,
    ot_ref,
    lse_ref,
    results_ref,
    stage_ref,
    key_marks_ref,
    query_marks_ref,
    own_seg_ref,
    seg_line_ref,
    send_sem,
    recv_sem,
    local_sem,
):
    tensors, rows, width = x_col_ref.shape
    owners = tensors // columns
    lanes = mixed_ref.shape[-1]
    heads = lanes // E
    pairs = heads // 2
    share = all_up_ref.shape[-1]
    shard = width // tensors
    last = tensors - 1
    length = tensors * rows
    tokens = columns * rows
    tensor_bits = log2(tensors)
    me = lax.axis_index("tensor")
    me_low = me % owners
    links = Links(send_sem, recv_sem)

    def slot_copies(sources, land):
        first = links.take(last)

        def one(slot, partner):
            source = sources.at[slot, :, pl.ds(0, land.shape[-1])]
            return links.copy(source, land.at[slot], first + slot, "tensor", partner)

        return one

    def partner_of(slot):
        mask = last - slot
        index = me
        for bit in range(log2(tensors)):
            index = index + bit_of(mask, bit) * (1 - 2 * bit_of(me, bit)) * (1 << bit)
        return index

    def gather(src, dst, lead, first, direct):
        cut_bits = len(dst.shape) - lead - 3
        return WeightGather(links, src, dst, lead, cut_bits, dp_bits, first, direct)

    masks = range(1, tensors)
    qkv = Stages([gather(None, all_qkv_ref, 1, 0, True)], masks)
    ffn = [
        gather(w_out_ref, all_out_ref, 0, 0, False),
        gather(w_up_ref, all_up_ref, 0, 0, False),
        gather(w_down_ref, all_down_ref, 0, 1, False),
    ]
    levels = [[mask for mask in masks if mask.bit_count() == n + 1] for n in range(tensor_bits)]
    near_ffn = Stages(ffn, [1])
    far_ffn = [Stages(ffn, [mask for mask in level if mask != 1]) for level in levels]
    x_first = links.take(last)

    def x_copy(slot):
        partner = partner_of(slot)
        return links.copy(
            home_ref.at[0, partner // owners], x_col_ref.at[slot], x_first + slot, "tensor", partner
        )

    mixed_copy = slot_copies(stage_ref, mixed_ref)
    do_copy = slot_copies(stage_ref, do_ref)
    input_copy = slot_copies(stage_ref, input_land_ref)
    down_scatter = GradScatter(links, g_down_ref, down_lands, down_across_ref, False)
    up_scatter = GradScatter(links, g_up_ref, up_lands, up_across_ref, False)
    qkv_scatters = [
        GradScatter(links, g_qkv_ref.at[i], [land.at[i] for land in qkv_lands], qkv_across_ref.at[i], True)
        for i in range(3)
    ]
    norm_sum = NormSum(links, norm_ref, norm_land_ref, dp_bits, tensors)

    def next_x(slot):
        x_copy(slot).wait_send()
        if slot + 1 < last - 1:
            x_copy(slot + 1).start()

    gain_one, bias_one = gain_one_ref[...], bias_one_ref[...]
    gain_two, bias_two = gain_two_ref[...], bias_two_ref[...]
    shard_copies = [one.own_copy(local_sem.at[5 + i]) for i, one in enumerate(ffn)]

    def start_phase(raw_ref, raw_qkv_ref):
        loads = [
            pltpu.make_async_copy(ref, raw_ref.at[n], local_sem.at[n])
            for n, ref in enumerate((x_ref, dual_in_ref, cot_post_ref, cot_dual_ref))
        ]
        load_qkv = pltpu.make_async_copy(w_qkv_ref, raw_qkv_ref, local_sem.at[4])
        start(loads[:1] + [load_qkv] + loads[1:] + shard_copies)
        greet(dp_bits, tensors)
        load_qkv.wait()
        for i in range(3):
            all_qkv_ref[me, i] = raw_qkv_ref[i].T.reshape(all_qkv_ref.shape[2:])
        loads[0].wait()
        home_ref[0] = jnp.swapaxes(raw_ref[0], 0, 1)
        greeted(dp_bits, tensors)
        qkv.begin()
        x_copy(0).start()
        if last > 1:
            x_copy(last - 1).start()
        near_ffn.begin()
        x_col_ref[last] = home_ref[0, me // owners]
        norm_ref[...] = jnp.zeros_like(norm_ref)
        own_seg_ref[...] = jnp.zeros_like(own_seg_ref)
        seg_row = lax.broadcasted_iota(jnp.int32, seg_ref.shape, 0)
        own_seg = jnp.where(seg_row == me // owners, seg_ref[...], 0).astype(F32)
        seg_line_ref[0:1, :] = jnp.sum(own_seg, axis=0, keepdims=True)
        for slot in range(tensors):
            spot = pl.ds(pl.multiple_of(partner_of(slot) * rows, rows), rows)
            own_seg_ref[slot : slot + 1, :] = seg_line_ref[0:1, spot]
        seg_columns = own_seg_ref[...].T
        for slot in range(tensors):
            at = slice(slot * rows, (slot + 1) * rows)
            lane = lax.broadcasted_iota(jnp.int32, (rows, 2 * E), 1)
            same = seg_columns[:, slot : slot + 1] == lane.astype(F32)
            marks = jnp.where(lane < DOCUMENTS, same.astype(F32), 0.0)
            ones = jnp.where((lane >= DOCUMENTS) & (lane < DOCUMENTS + PARTS), 1.0, marks)
            key_marks_ref[at, :] = ones.astype(BF16)
            line = lax.broadcasted_iota(jnp.int32, (2 * E, rows), 0)
            other = own_seg_ref[slot : slot + 1, :] != line.astype(F32)
            bias = jnp.where((line < DOCUMENTS) & other, NEGATIVE, 0.0)
            query_marks_ref[:, at] = bias.astype(BF16)
        if owners > 1:
            g_qkv_ref[...] = jnp.zeros_like(g_qkv_ref)
        turned = 1
        for stage in range(qkv.count):
            if turned < 4:
                loads[turned].wait()
                home_ref[turned] = jnp.swapaxes(raw_ref[turned], 0, 1)
                turned += 1
            if stage == qkv.count - 1:
                next_x(0)
                near_ffn.advance(0)
            qkv.advance(stage)
        for copy in shard_copies:
            copy.wait()

    pl.run_scoped(
        start_phase,
        pltpu.VMEM((4, rows, columns, width), BF16),
        pltpu.VMEM(w_qkv_ref.shape, BF16),
    )
    own_shards = pl.ds(me_low * (tensors // owners), tensors // owners)

    def w_t(i):
        return all_qkv_ref[own_shards, i].reshape(lanes, width)

    def forward_phase(
        vt_ref,
        hidden_ref,
        slope_ref,
        grad_inner_ref,
        up_two_ref,
        middle_ref,
        up_one_ref,
    ):
        order = [last, last - 1] + list(range(last - 1)) if last > 1 else [last, 0]
        for turn, slot in enumerate(order):
            if slot < last:
                x_copy(slot).wait_recv()
            if 0 < slot < last - 1:
                next_x(slot)
            if turn + 1 == tensors:
                far_ffn[0].begin()
            block = x_col_ref[slot]
            at = slice(slot * rows, (slot + 1) * rows)
            q_ref[at, :] = dot_nt(block, w_t(0)).astype(BF16) * jnp.bfloat16(0.125)
            k_ref[at, :] = dot_nt(block, w_t(1)).astype(BF16)
            v_ref[at, :] = dot_nt(block, w_t(2)).astype(BF16)
            qt_ref[:, at] = dot_nt(w_t(0), block).astype(BF16) * jnp.bfloat16(0.125)
            kt_ref[:, at] = dot_nt(w_t(1), block).astype(BF16)
            vt_ref[:, at] = dot_nt(w_t(2), block).astype(BF16)
            xt_ref[:, at] = block.T
            if 0 < turn < near_ffn.count:
                near_ffn.advance(turn)
        for stage in range(tensors, near_ffn.count):
            near_ffn.advance(stage)

        def gather_step(level, stage):
            def run():
                far_ffn[level].advance(stage)
                if stage == 0 and level + 1 < len(far_ffn):
                    far_ffn[level + 1].begin()

            return run

        steps = tensors * pairs
        gather_events = sorted(
            (
                (GATHER_DUE + GATHER_LEVEL * level + GATHER_STEP * stage, level, stage)
                for level in range(tensor_bits)
                for stage in range(1 + dp_bits)
            ),
        )
        late = [gather_step(*which) for due, *which in gather_events if due >= 16]
        gather_events = [
            (due * steps // 16, gather_step(*which)) for due, *which in gather_events if due < 16
        ]

        @pl.loop(0, tensors)
        def _(slot):
            at_rows = pl.ds(pl.multiple_of(slot * rows, rows), rows)
            @pl.loop(0, pairs)
            def _(j):
                for due, one in gather_events:

                    @pl.when(slot * pairs + j == due)
                    def _():
                        one()

                at = pl.ds(pl.multiple_of(j * 2 * E, 2 * E), 2 * E)
                keys = jnp.concatenate([k_ref[:, at], key_marks_ref[...]], axis=1)
                queries = qt_ref[at, at_rows]
                marks = query_marks_ref[:, at_rows]
                for half in range(2):
                    scores = dot_nn(keys, with_marks(half_rows(queries, half), marks))
                    top = jnp.max(scores, axis=0, keepdims=True)
                    raised = jnp.exp(scores - top)
                    denom = jnp.sum(raised, axis=0, keepdims=True)
                    at_head = pl.ds(pl.multiple_of((2 * j + half) * E, E), E)
                    result = dot_nn(vt_ref[at_head, :], raised.astype(BF16))
                    ot_ref[slot, at_head, :] = result * (1.0 / denom)
                    lse_ref[slot, pl.ds(2 * j + half, 1), :] = top + jnp.log(denom)

            block = ot_ref[slot].T.astype(BF16)

            @pl.when(slot < last)
            def _():
                stage_ref[slot, :, :lanes] = block
                mixed_copy(slot, partner_of(slot)).start()

            @pl.when(slot == last)
            def _():
                mixed_ref[last] = block

        for one in late:
            one()

        @pl.loop(0, columns)
        def _(i):
            column = partner_of(owners * i) // owners
            for r in range(owners):

                @pl.when(owners * i + r < last)
                def _():
                    mixed_copy(owners * i + r, partner_of(owners * i + r)).wait()

            def slot_of(h):
                return last - owners * (columns - 1 - i) - flip(me_low, h)

            mixed = jnp.concatenate([mixed_ref[slot_of(h)] for h in range(owners)], axis=1)
            at = pl.ds(pl.multiple_of(i * rows, rows), rows)
            branch_one = dot_nn(mixed, all_out_ref[...].reshape(width, width))
            normed_one, factor_one = norm_forward(home_ref[0, column].astype(F32) + branch_one)
            middle = normed_one * gain_one + bias_one
            middle_low = middle.astype(BF16)
            middle_ref[:, at] = middle_low.T
            branch_two = jnp.zeros((rows, width), F32)

            for t in range(tensors):
                inner = dot_nn(middle_low, all_up_ref[t].reshape(width, share))
                square = inner * inner
                bend = jnp.tanh(GELU_A * (inner + GELU_B * (square * inner)))
                hidden = (0.5 * inner * (1.0 + bend)).astype(BF16)
                slope_ref[t] = 0.5 * (1.0 + bend) + (0.5 * GELU_A) * inner * (
                    1.0 - bend * bend
                ) * (1.0 + (3.0 * GELU_B) * square)
                hidden_ref[t, at, :] = hidden
                branch_two = branch_two + dot_nn(hidden, all_down_ref[t].reshape(share, width))
            normed_two, factor_two = norm_forward(middle + branch_two)
            results_ref[0, column] = normed_two * gain_two + bias_two
            results_ref[1, column] = home_ref[1, column].astype(F32) + branch_one + branch_two
            cot_dual = home_ref[3, column].astype(F32)
            upstream = home_ref[2, column].astype(F32)
            d_two = norm_backward(upstream, normed_two, factor_two, gain_two)
            norm_ref[2:3, :] += jnp.sum(upstream * normed_two, axis=0, keepdims=True)
            norm_ref[3:4, :] += jnp.sum(upstream, axis=0, keepdims=True)
            up_two = (d_two + cot_dual).astype(BF16)
            up_two_ref[:, at] = up_two.T
            grad_middle = d_two
            for t in range(tensors):
                grad_hidden = dot_nt(up_two, all_down_ref[t].reshape(share, width))
                grad_inner = (grad_hidden * slope_ref[t]).astype(BF16)
                grad_inner_ref[t, at, :] = grad_inner
                grad_middle = grad_middle + dot_nt(grad_inner, all_up_ref[t].reshape(width, share))
            d_one = norm_backward(grad_middle, normed_one, factor_one, gain_one)
            norm_ref[0:1, :] += jnp.sum(grad_middle * normed_one, axis=0, keepdims=True)
            norm_ref[1:2, :] += jnp.sum(grad_middle, axis=0, keepdims=True)
            results_ref[2, column] = d_one
            up_one = (d_one + cot_dual).astype(BF16)
            up_one_ref[:, at] = up_one.T
            grad_mixed = dot_nt(up_one, all_out_ref[...].reshape(width, width)).astype(BF16)
            for h in range(owners):
                slot = slot_of(h)
                piece = grad_mixed[:, h * lanes : (h + 1) * lanes]

                @pl.when(slot < last)
                def _():
                    stage_ref[slot, :, :lanes] = piece
                    do_copy(slot, partner_of(slot)).start()

                @pl.when(slot == last)
                def _():
                    do_ref[last] = piece

        norm_sum.begin()
        cut = (2,) * dp_bits + (width >> dp_bits,)

        @pl.loop(0, tensors)
        def _(t):
            g_down = dot_nn(up_two_ref[...], hidden_ref[t]).astype(BF16)
            g_down_ref[t] = g_down.reshape(cut + (share,))

        down_scatter.begin()
        every = (slice(None),) * (dp_bits + 1)

        @pl.loop(0, tensors)
        def _(t):
            g_up = dot_nn(middle_ref[...], grad_inner_ref[t]).astype(BF16)
            g_up_ref[(t,) + every + (slice(0, share),)] = g_up.reshape(cut + (share,))

        def mixed_of(i):
            def slot_of(h):
                return last - owners * (columns - 1 - i) - flip(me_low, h)

            return jnp.concatenate([mixed_ref[slot_of(h)] for h in range(owners)], axis=1)

        all_mixed = jnp.concatenate([mixed_of(i) for i in range(columns)], axis=0)
        g_out = dot_nn(up_one_ref[...], all_mixed).astype(BF16)
        for t in range(tensors):
            g_up_ref[(t,) + every + (slice(share, share + shard),)] = g_out[
                :, t * shard : (t + 1) * shard
            ].reshape(cut + (shard,))
        up_scatter.begin()

    pl.run_scoped(
        forward_phase,
        pltpu.VMEM((lanes, length), BF16),
        pltpu.VMEM((tensors, tokens, share), BF16),
        pltpu.VMEM((tensors, rows, share), F32),
        pltpu.VMEM((tensors, tokens, share), BF16),
        pltpu.VMEM((width, tokens), BF16),
        pltpu.VMEM((width, tokens), BF16),
        pltpu.VMEM((width, tokens), BF16),
    )

    def backward_phase(dot_ref, delta_ref, dq_ref, dk_ref, dv_ref, grads_ref):
        dq_ref[...] = jnp.zeros_like(dq_ref)
        dk_ref[...] = jnp.zeros_like(dk_ref)
        dv_ref[...] = jnp.zeros_like(dv_ref)

        def receive(slot):
            if slot < last:
                do_copy(slot, partner_of(slot)).wait()
            at = slice(slot * rows, (slot + 1) * rows)
            turned = do_ref[slot].T
            dot_ref[:, at] = turned
            product = turned.astype(F32) * ot_ref[slot]
            delta_ref[slot, :heads] = jnp.sum(product.reshape(heads, E, rows), axis=1)

        def advance(scatter, step):
            def run():
                scatter.advance(step)
                if scatter is up_scatter:
                    norm_sum.advance(step)

            return run

        counts = [
            count for wave in range(tensors) for count in (tensors - wave, last - wave) if count
        ]
        begins, done = [], 0
        for count in counts:
            for j in range(pairs):
                begins.append((done + count * j / pairs) / (tensors * tensors))
            done += count
        count = down_scatter.steps
        wishes = []
        for scatter, dues in ((down_scatter, DOWN_DUES), (up_scatter, UP_DUES)):
            wishes.append((dues[0], advance(scatter, 0)))
            for step in range(1, count):
                due = dues[1] + (dues[2] - dues[1]) * (step - 1) / max(count - 2, 1)
                wishes.append((due, advance(scatter, step)))
        wishes = [(next(n for n, at in enumerate(begins) if at >= wish), one) for wish, one in wishes]

        def block_of(number, q_slot, q_count, k_slot, k_count):
            at_q = slice(q_slot * rows, (q_slot + q_count) * rows)
            at_k = slice(k_slot * rows, (k_slot + k_count) * rows)

            @pl.loop(0, pairs)
            def _(j):
                for place, one in wishes:
                    if place // pairs == number:

                        @pl.when(j == place % pairs)
                        def _():
                            one()

                at = pl.ds(pl.multiple_of(j * 2 * E, 2 * E), 2 * E)
                key_marks = key_marks_ref[at_k, :]
                keys = jnp.concatenate([k_ref[at_k, at], key_marks], axis=1)
                values = jnp.concatenate([v_ref[at_k, at], key_marks], axis=1)
                query_marks = query_marks_ref[:, at_q]
                no_marks = jnp.zeros_like(query_marks)
                queries = q_ref[at_q, at]
                ups = do_ref[q_slot : q_slot + q_count, :, at].reshape(q_count * rows, 2 * E)
                sums = []
                for half in range(2):

                    def row_of(ref):
                        row = pl.ds(2 * j + half, 1)
                        slots = range(q_slot, q_slot + q_count)
                        return jnp.concatenate([ref[slot, row, :] for slot in slots], axis=1)

                    minus_lse = with_row(query_marks, row_of(lse_ref))
                    minus_delta = with_row(no_marks, row_of(delta_ref))
                    probs = jnp.exp(dot_nn(keys, with_marks(half_rows(qt_ref[at, at_q], half), minus_lse)))
                    pushed = dot_nn(values, with_marks(half_rows(dot_ref[at, at_q], half), minus_delta))
                    delta = (probs * pushed).astype(BF16)
                    at_head = pl.ds(pl.multiple_of((2 * j + half) * E, E), E)
                    dq_ref[at_head, at_q] += dot_nn(kt_ref[at_head, at_k], delta)
                    sums.append((dot_nn(delta, queries), dot_nn(probs.astype(BF16), ups)))
                low_half = lax.broadcasted_iota(jnp.int32, sums[0][0].shape, 1) < E
                dk_ref[at_k, at] += jnp.where(low_half, sums[0][0], sums[1][0])
                dv_ref[at_k, at] += jnp.where(low_half, sums[0][1], sums[1][1])

        for wave in range(tensors):
            if wave == 0:
                receive(0)
            block_of(2 * wave, wave, 1, wave, tensors - wave)
            if wave == 0:
                for slot in range(1, tensors):
                    receive(slot)
            if wave < last:
                block_of(2 * wave + 1, wave + 1, last - wave, wave, 1)
            at = slice(wave * rows, (wave + 1) * rows)
            grads = (
                (dq_ref[:, at] * 0.125).T.astype(BF16),
                dk_ref[at, :].astype(BF16),
                dv_ref[at, :].astype(BF16),
            )
            part = jnp.zeros((rows, width), F32)
            for i in range(3):
                grads_ref[i, at, :] = grads[i]
                part = part + dot_nn(grads[i], w_t(i))

            if wave < last:
                stage_ref[wave] = part.astype(BF16)
                input_copy(wave, partner_of(wave)).start()
            else:
                results_ref[2, me // owners] += part

        for i in range(3):
            g = dot_nn(xt_ref[...], grads_ref[i]).astype(BF16)
            for t in range(tensors // owners):
                g_qkv_ref[i, me_low * (tensors // owners) + t] = g[
                    :, t * shard : (t + 1) * shard
                ].reshape((2,) * dp_bits + (width >> dp_bits, shard))
            qkv_scatters[i].begin()
            if i:
                qkv_scatters[i - 1].advance(0)

    pl.run_scoped(
        backward_phase,
        pltpu.VMEM((lanes, length), BF16),
        pltpu.VMEM((tensors, max(heads, 8), rows), F32),
        pltpu.VMEM((lanes, length), F32),
        pltpu.VMEM((length, lanes), F32),
        pltpu.VMEM((length, lanes), F32),
        pltpu.VMEM((3, length, lanes), BF16),
    )


    def end_phase(turned_ref):
        stores = [
            pltpu.make_async_copy(turned_ref.at[n], ref, local_sem.at[n])
            for n, ref in enumerate((post_ref, dual_ref, grad_post_ref))
        ]

        def store(n):
            turned_ref[n] = jnp.swapaxes(results_ref[n], 0, 1)
            stores[n].start()

        def advance(step):
            for one in qkv_scatters:
                one.advance(step)

        store(0)
        qkv_scatters[2].advance(0)
        store(1)
        if dp_bits > 1:
            advance(1)
        if last > 1:
            x_copy(last - 1).wait_send()
        for slot in range(last):
            input_copy(slot, partner_of(slot)).wait()
            results_ref[2, partner_of(slot) // owners] += input_land_ref[slot].astype(F32)
        store(2)
        for step in range(2, dp_bits):
            advance(step)
        r_down_ref[...] = down_scatter.result()
        r_up_ref[...] = up_scatter.result()
        count = width // (tensors << dp_bits)
        first = (lax.axis_index("dp") * tensors + me) * count
        r_norm_ref[...] = pltpu.roll(norm_sum.result(), width - first, 1)[:, : r_norm_ref.shape[1]]
        for i in range(3):
            r_qkv_ref[i] = qkv_scatters[i].result()
        for copy in stores:
            copy.wait()

    pl.run_scoped(end_phase, pltpu.VMEM((3, rows, columns, width), F32))


def hand_over_kernel(*refs):
    sources, results = refs[:7], refs[7:]
    for n in range(3):
        results[n][...] = sources[n][...]

    @pl.when(pl.program_id(0) == 0)
    def _():
        grad_qkv, grad_down, grad_up_out, grad_norm = sources[3:]
        share = results[4].shape[1]
        results[3][...] = grad_qkv[...]
        results[4][...] = grad_down[...]
        results[5][...] = grad_up_out[:, :share]
        results[6][...] = grad_up_out[:, share:]
        for n in range(4):
            results[7 + n][...] = grad_norm[n : n + 1, : results[7 + n].shape[1]]


def body(
    x_post,
    x_dual,
    cot_post,
    cot_dual,
    segment_ids,
    w_qkv,
    w_out,
    w_up,
    w_down,
    gain_one,
    bias_one,
    gain_two,
    bias_two,
):
    tensors, devices = lax.axis_size("tensor"), lax.axis_size("dp")
    dp_bits = log2(devices)
    rows, columns, width = x_post.shape
    length = tensors * rows
    owners = tensors // columns
    lanes = width // owners
    share, shard = w_up.shape[1], w_out.shape[0]
    piece = width // devices
    heads = lanes // E
    me = lax.axis_index("tensor")
    def cut(array, dim):
        bits = min(dp_bits, log2(array.shape[dim] // 16))
        shape = array.shape[:dim] + (2,) * bits + (array.shape[dim] >> bits,) + array.shape[dim + 1 :]
        return array.reshape(shape)

    shards = [cut(w_out, 0), cut(w_up, 0), cut(w_down, 0)]
    qkv_shape = jax.eval_shape(lambda w: cut(jnp.swapaxes(w, 1, 2), 1), w_qkv).shape
    in_vmem = pl.BlockSpec(memory_space=pltpu.VMEM)
    in_place = pl.BlockSpec(memory_space=pl.ANY)
    shape = jax.ShapeDtypeStruct
    bits = (2,) * dp_bits

    def lands(lane_count, *lead):
        return [
            pltpu.VMEM(lead + (tensors,) + bits[: dp_bits - 1 - step] + (piece, lane_count), BF16)
            for step in range(dp_bits)
        ]

    layer = pl.pallas_call(
        functools.partial(layer_kernel, dp_bits, columns),
        out_shape=(
            shape((rows, columns, width), F32),
            shape((rows, columns, width), F32),
            shape((rows, columns, width), F32),
            shape((3, piece, shard), F32),
            shape((piece, share), F32),
            shape((piece, share + shard), F32),
            shape((8, 128), F32),
        ),
        in_specs=[in_vmem] + [in_place] * 8 + [in_vmem] * 4,
        out_specs=(in_place,) * 3 + (in_vmem,) * 4,
        scratch_shapes=[
            pltpu.VMEM((4, columns, rows, width), BF16),
            pltpu.VMEM((tensors, rows, width), BF16),
            pltpu.VMEM((tensors,) + qkv_shape, BF16),
        ]
        + [pltpu.VMEM((tensors,) + one.shape, BF16) for one in shards]
        + [
            pltpu.VMEM((tensors, rows, lanes), BF16),
            pltpu.VMEM((tensors, rows, lanes), BF16),
            pltpu.VMEM((tensors - 1, rows, width), BF16),
            pltpu.VMEM((tensors,) + bits + (piece, share), BF16),
            pltpu.VMEM((tensors,) + bits + (piece, share + shard), BF16),
            pltpu.VMEM((3, tensors) + bits + (piece, shard), BF16),
            lands(share),
            pltpu.VMEM((tensors - 1, piece, share), BF16),
            lands(share + shard),
            pltpu.VMEM((tensors - 1, piece, share + shard), BF16),
            lands(shard, 3),
            pltpu.VMEM((3, tensors - 1, piece, shard), BF16),
            pltpu.VMEM((8, width), F32),
            pltpu.VMEM((dp_bits + tensors - 1, 8, width), F32),
            pltpu.VMEM((length, lanes), BF16),
            pltpu.VMEM((length, lanes), BF16),
            pltpu.VMEM((length, lanes), BF16),
            pltpu.VMEM((lanes, length), BF16),
            pltpu.VMEM((lanes, length), BF16),
            pltpu.VMEM((width, length), BF16),
            pltpu.VMEM((tensors, lanes, rows), F32),
            pltpu.VMEM((tensors, max(heads, 8), rows), F32),
            pltpu.VMEM((3, columns, rows, width), F32),
            pltpu.VMEM((tensors - 1, rows, width), BF16),
            pltpu.VMEM((length, 2 * E), BF16),
            pltpu.VMEM((2 * E, length), BF16),
            pltpu.VMEM((max(tensors, 8), rows), F32),
            pltpu.VMEM((8, length), F32),
            pltpu.SemaphoreType.DMA((LINKS,)),
            pltpu.SemaphoreType.DMA((LINKS,)),
            pltpu.SemaphoreType.DMA((8,)),
        ],
        compiler_params=pltpu.CompilerParams(
            vmem_limit_bytes=VMEM_BYTES, collective_id=0, has_side_effects=True
        ),
        name="layer",
    )
    made = layer(
        segment_ids.T,
        x_post,
        x_dual,
        cot_post,
        cot_dual,
        w_qkv,
        *shards,
        *(one.reshape(1, width) for one in (gain_one, bias_one, gain_two, bias_two)),
    )
    count = width // (tensors * devices)
    blocks = 2
    block_spec = pl.BlockSpec((rows // blocks, columns, width), lambda i: (i, 0, 0))

    def whole_spec(one):
        return pl.BlockSpec(one.shape, lambda i: (0,) * len(one.shape))

    small = (
        shape((3, piece, shard), F32),
        shape((piece, share), F32),
        shape((piece, share), F32),
        shape((piece, shard), F32),
    ) + (shape((1, count), F32),) * 4
    results = pl.pallas_call(
        hand_over_kernel,
        out_shape=tuple(shape(one.shape, F32) for one in made[:3]) + small,
        grid=(blocks,),
        in_specs=[block_spec] * 3 + [whole_spec(one) for one in made[3:]],
        out_specs=(block_spec,) * 3 + tuple(whole_spec(one) for one in small),
        name="hand_over",
    )(*made)
    post_out, dual_out, grad_post, g_qkv, g_down, g_up, g_out = results[:7]
    norms = tuple(one.reshape(count) for one in results[7:])
    return (post_out, dual_out, grad_post, g_qkv, g_out.T, g_up, g_down.T) + norms


def solution(mesh):
    placed = (
        P("tensor", "dp", None),
        P("tensor", "dp", None),
        P("tensor", "dp", None),
        P("tensor", "dp", None),
        P(None, "dp"),
        P(None, None, "tensor"),
        P("tensor", None),
        P(None, "tensor"),
        P("tensor", None),
        P(),
        P(),
        P(),
        P(),
    )
    return jax.shard_map(
        body,
        mesh=mesh,
        in_specs=placed,
        out_specs=(
            P("tensor", "dp", None),
            P("tensor", "dp", None),
            P("tensor", "dp", None),
            P(None, "dp", "tensor"),
            P("tensor", "dp"),
            P("dp", "tensor"),
            P("tensor", "dp"),
            P(("dp", "tensor")),
            P(("dp", "tensor")),
            P(("dp", "tensor")),
            P(("dp", "tensor")),
        ),
        check_vma=False,
    )
```

```python
import functools
import itertools

import jax
import jax.numpy as jnp
from jax import lax
from jax.experimental import pallas as pl
from jax.experimental.pallas import tpu as pltpu
from jax.sharding import PartitionSpec as P

E = 64
EPSILON = 1e-05
NEGATIVE = -1e30
DOCUMENTS = 4
DOWN_DUES = (0.06, 0.35, 0.75)
UP_DUES = (0.10, 0.5, 0.9)
GATHER_DUE, GATHER_LEVEL, GATHER_STEP = 6, 4, 3
NEAR_DUE = 1
PARTS = 3
GELU_A = 0.7978845608028654
GELU_B = 0.044715
F32 = jnp.float32
BF16 = jnp.bfloat16
VMEM_BYTES = 63 * 1024 * 1024


def dot_nn(a, b):
    return lax.dot_general(a, b, (((1,), (0,)), ((), ())), preferred_element_type=F32)


def dot_nt(a, b):
    return lax.dot_general(a, b, (((1,), (1,)), ((), ())), preferred_element_type=F32)


def dot_tn(a, b):
    return lax.dot_general(a, b, (((0,), (0,)), ((), ())), preferred_element_type=F32)


def row_mean(a):
    return jnp.mean(a, axis=-1, keepdims=True)


def norm_forward(total):
    centre = total - row_mean(total)
    factor = lax.rsqrt(row_mean(centre * centre) + EPSILON)
    return centre * factor, factor


def norm_backward(upstream, normed, factor, gain):
    scaled = upstream * gain
    inner = scaled - row_mean(scaled) - normed * row_mean(scaled * normed)
    return factor * inner


def with_marks(block, marks):
    return jnp.concatenate([block, marks], axis=0)


def with_row(marks, row):
    line = lax.broadcasted_iota(jnp.int32, (16, row.shape[1]), 0)
    top = marks[:16].astype(F32)
    rest = -row
    for part in range(PARTS):
        term = rest.astype(BF16).astype(F32)
        rest = rest - term
        top = jnp.where(line == DOCUMENTS + part, term, top)
    return jnp.concatenate([top.astype(BF16), marks[16:]], axis=0)


def half_rows(block, half):
    zeros = jnp.zeros((E, block.shape[1]), block.dtype)
    if half == 0:
        return jnp.concatenate([block[:E], zeros], axis=0)
    return jnp.concatenate([zeros, block[E:]], axis=0)


MESH = pl.DeviceIdType.MESH


def bit_of(index, bit):
    return (index // (1 << bit)) % 2


def flip(index, mask):
    for bit in range(mask.bit_length()):
        if (mask >> bit) % 2:
            index = index + (1 - 2 * bit_of(index, bit)) * (1 << bit)
    return index


def log2(count):
    return count.bit_length() - 1


class Links:
    def __init__(self, send_sem, recv_sem):
        self.send_sem, self.recv_sem, self.used, self.pooled = send_sem, recv_sem, 0, 0

    def take(self, count):
        first = self.used
        self.used += count
        assert self.used <= self.recv_sem.shape[0]
        return first

    def pool(self, count):
        first = self.pooled
        self.pooled += count
        assert self.pooled <= self.send_sem.shape[0]
        return first

    def copy(self, src, dst, slot, send_slot, axis, partner):
        return pltpu.make_async_remote_copy(
            src_ref=src,
            dst_ref=dst,
            send_sem=self.send_sem.at[send_slot],
            recv_sem=self.recv_sem.at[slot],
            device_id={axis: partner},
            device_id_type=MESH,
        )

    def stages(self, stages):
        first = self.pool(max(len(stage) for stage in stages))
        return [
            [
                self.copy(src, dst, self.take(1), first + n, axis, partner)
                for n, (src, dst, axis, partner) in enumerate(stage)
            ]
            for stage in stages
        ]


def link_counts(tensors, dp_bits, cuts):
    others = tensors - 1
    levels = [0] * log2(tensors)
    for mask in range(2, tensors):
        levels[mask.bit_count() - 1] += 1
    receive = 4 * others + others * (1 + 3 * cuts[0]) + sum(others * (1 + cut) for cut in cuts[1:])
    receive += 5 * (1 + 2 * (dp_bits - 1) + others) + dp_bits + others
    send = 2 * others + 3 * others + 3 + 3 * sum(levels)
    send += 2 * max(2, tensors // 2) + 3 * max(2, others) + others
    return receive, send


def start(copies):
    for copy in copies:
        copy.start()


def finish(copies):
    for copy in copies:
        copy.wait_recv()
        copy.wait_send()


def greet(dp_bits, tensors):
    dp, me = lax.axis_index("dp"), lax.axis_index("tensor")
    barrier = pltpu.get_barrier_semaphore()
    for bit in range(dp_bits):
        pl.semaphore_signal(barrier, inc=1, device_id={"dp": flip(dp, 1 << bit)}, device_id_type=MESH)
    for step in range(1, tensors):
        pl.semaphore_signal(
            barrier, inc=1, device_id={"tensor": (me + step) % tensors}, device_id_type=MESH
        )


def greeted(dp_bits, tensors):
    pl.semaphore_wait(pltpu.get_barrier_semaphore(), dp_bits + tensors - 1)


class WeightGather:
    def __init__(self, src, dst, lead, cut_bits, dp_bits, first, direct=False):
        tensors = dst.shape[0]
        dp, me = lax.axis_index("dp"), lax.axis_index("tensor")
        bits = list(range(dp_bits - 1, dp_bits - 1 - cut_bits, -1))
        if src is None:
            src = dst.at[me]
        self.src, self.dst, self.own = src, dst, me
        inner = [()] if lead == 0 else [(i,) for i in range(dst.shape[1])]
        piece = (slice(None),) * lead + tuple(bit_of(dp, bit) for bit in bits)
        low = [bit for bit in bits if bit == 0]
        high = [bit for bit in bits if bit != 0]
        orders = (high[::-1] + low, high + low)
        count = first
        self.stages = {}
        for mask in range(1, tensors):
            near = mask if direct else mask & -mask
            block = flip(me, mask - near)
            stages = [[] for _ in range(1 + dp_bits)]
            stages[0].append(
                (
                    dst.at[(block,) + piece] if mask != near else src.at[piece],
                    dst.at[(block,) + piece],
                    "tensor",
                    flip(me, near),
                )
            )
            source = flip(me, mask)
            for i in inner:
                order = orders[count % 2]
                count += 1
                for phase, bit in enumerate(order):
                    done = order[:phase]
                    region = (source,) + i + tuple(
                        slice(None) if other in done else bit_of(dp, other) for other in bits
                    )
                    stages[1 + phase].append(
                        (dst.at[region], dst.at[region], "dp", flip(dp, 1 << bit))
                    )
            self.stages[mask] = stages

    def own_copy(self, sem):
        return pltpu.make_async_copy(self.src, self.dst.at[self.own], sem)


class Stages:
    def __init__(self, links, stages):
        self.copies = links.stages(stages)
        self.count = len(stages)

    def begin(self):
        start(self.copies[0])

    def advance(self, stage):
        finish(self.copies[stage])
        if stage + 1 < self.count:
            start(self.copies[stage + 1])


def shard_stages(weights, masks):
    count = len(weights[0].stages[masks[0]])
    return [
        [copy for one in weights for mask in masks for copy in one.stages[mask][stage]]
        for stage in range(count)
    ]


class GradScatter:
    def __init__(self, links, grad, lands, across, direct):
        self.links, self.grad, self.lands, self.across = links, grad, lands, across
        self.tensors = grad.shape[0]
        self.dp, self.me = lax.axis_index("dp"), lax.axis_index("tensor")
        dp_bits = len(lands)
        high = list(range(dp_bits - 1, 0, -1))
        middle = self.tensors // 2
        copies = [
            [
                (
                    grad.at[(slice(None),) * dp_bits + (1 - bit_of(self.dp, 0),)],
                    lands[0],
                    "dp",
                    flip(self.dp, 1),
                )
            ]
        ]
        sums = [[(0, self.tensors, grad, dp_bits - 1, bit_of(self.dp, 0), lands[0])]]
        for step in range(1, dp_bits):
            copies.append([])
            sums.append([])
        for begin, order in ((0, high[::-1]), (middle, high)):
            left = list(high)
            for step, bit in enumerate(order, 1):
                place = left.index(bit)
                left.remove(bit)
                part = pl.ds(begin, middle)
                index = (part,) + (slice(None),) * place + (1 - bit_of(self.dp, bit),)
                copies[step].append(
                    (
                        lands[step - 1].at[index],
                        lands[step].at[part],
                        "dp",
                        flip(self.dp, 1 << bit),
                    )
                )
                sums[step].append(
                    (begin, middle, lands[step - 1], place, bit_of(self.dp, bit), lands[step])
                )
        place = 0
        self.joins = []
        for bit in range(0 if direct else log2(self.tensors)):
            step, found, joins = 1 << bit, [], []
            for high in range(self.tensors >> (bit + 1)):
                mask = high * 2 * step
                found.append(
                    (
                        lands[-1].at[flip(self.me, mask + step)],
                        across.at[place],
                        "tensor",
                        flip(self.me, step),
                    )
                )
                joins.append((mask, place))
                place += 1
            copies.append(found)
            self.joins.append(joins)
        if direct:
            copies.append(
                [
                    (
                        lands[-1].at[flip(self.me, step)],
                        across.at[step - 1],
                        "tensor",
                        flip(self.me, step),
                    )
                    for step in range(1, self.tensors)
                ]
            )
            self.joins = [[(0, step) for step in range(self.tensors - 1)]]
        self.copies = links.stages(copies)
        self.sums = sums + [[] for _ in self.joins[1:]]
        self.steps = len(copies) - 1

    def begin(self):
        start(self.copies[0])

    def advance(self, step):
        finish(self.copies[step])
        for first, count, source, place, own, land in self.sums[step]:

            @pl.loop(first, first + count)
            def _(t):
                for spot in itertools.product((0, 1), repeat=len(land.shape) - 3):
                    whole = (t,) + spot[:place] + (own,) + spot[place:]
                    here = (t,) + spot
                    land[here] = (land[here].astype(F32) + source[whole].astype(F32)).astype(BF16)

        if step >= len(self.lands):
            for mask, place in self.joins[step - len(self.lands)]:
                spot = flip(self.me, mask)
                total = self.lands[-1][spot].astype(F32) + self.across[place].astype(F32)
                self.lands[-1][spot] = total.astype(BF16)
        start(self.copies[step + 1])

    def result(self):
        finish(self.copies[-1])
        total = self.lands[-1][self.me].astype(F32)
        for _, place in self.joins[-1]:
            total = total + self.across[place].astype(F32)
        return total


class NormSum:
    def __init__(self, links, total, land, dp_bits, tensors):
        dp, me = lax.axis_index("dp"), lax.axis_index("tensor")
        self.total, self.land = total, land
        copies = [
            [(total, land.at[bit], "dp", flip(dp, 1 << bit))] for bit in range(dp_bits)
        ]
        copies.append(
            [
                (total, land.at[dp_bits + step - 1], "tensor", flip(me, step))
                for step in range(1, tensors)
            ]
        )
        self.copies = links.stages(copies)

    def begin(self):
        start(self.copies[0])

    def advance(self, step):
        if step + 1 < len(self.copies):
            finish(self.copies[step])
            self.total[...] += self.land[step]
            start(self.copies[step + 1])

    def result(self):
        finish(self.copies[-1])
        total = self.total[...]
        for step in range(len(self.copies) - 1, self.land.shape[0]):
            total = total + self.land[step]
        return total


def layer_kernel(
    dp_bits,
    columns,
    seg_ref,
    x_ref,
    dual_in_ref,
    cot_post_ref,
    cot_dual_ref,
    w_qkv_ref,
    w_out_ref,
    w_up_ref,
    w_down_ref,
    gain_one_ref,
    bias_one_ref,
    gain_two_ref,
    bias_two_ref,
    post_ref,
    dual_ref,
    grad_post_ref,
    r_qkv_ref,
    r_down_ref,
    r_up_ref,
    r_norm_ref,
    home_ref,
    x_col_ref,
    all_qkv_ref,
    all_out_ref,
    all_up_ref,
    all_down_ref,
    mixed_ref,
    do_ref,
    input_land_ref,
    g_down_ref,
    g_up_ref,
    g_qkv_ref,
    down_lands,
    down_across_ref,
    up_lands,
    up_across_ref,
    qkv_lands,
    qkv_across_ref,
    norm_ref,
    norm_land_ref,
    q_ref,
    k_ref,
    v_ref,
    qt_ref,
    kt_ref,
    xt_ref,
    o_ref,
    lse_ref,
    results_ref,
    stage_ref,
    key_marks_ref,
    key_marks_t_ref,
    query_marks_ref,
    query_marks_n_ref,
    lse_columns_ref,
    own_seg_ref,
    seg_line_ref,
    seg_in_ref,
    norms_ref,
    small_refs,
    send_sem,
    recv_sem,
    local_sem,
):
    tensors, rows, width = x_col_ref.shape
    owners = tensors // columns
    lanes = mixed_ref.shape[-1]
    heads = lanes // E
    pairs = heads // 2
    share = all_up_ref.shape[-1]
    shard = width // tensors
    last = tensors - 1
    length = tensors * rows
    tokens = columns * rows
    tensor_bits = log2(tensors)
    me = lax.axis_index("tensor")
    me_low = me % owners
    links = Links(send_sem, recv_sem)

    exchange_pool = links.pool(last)

    def slot_copies(sources, land):
        first = links.take(last)

        def one(slot, partner):
            source = sources.at[slot, :, pl.ds(0, land.shape[-1])]
            return links.copy(
                source, land.at[slot], first + slot, exchange_pool + slot, "tensor", partner
            )

        return one

    def partner_of(slot):
        mask = last - slot
        index = me
        for bit in range(log2(tensors)):
            index = index + bit_of(mask, bit) * (1 - 2 * bit_of(me, bit)) * (1 << bit)
        return index

    def gather(src, dst, lead, first, direct=False):
        return WeightGather(src, dst, lead, len(dst.shape) - lead - 3, dp_bits, first, direct)

    masks = list(range(1, tensors))
    levels = [[mask for mask in masks if mask.bit_count() == n + 1] for n in range(tensor_bits)]
    qkv = Stages(links, shard_stages([gather(None, all_qkv_ref, 1, 0, True)], masks))
    ffn = [
        gather(w_out_ref, all_out_ref, 0, 0),
        gather(w_up_ref, all_up_ref, 0, 0),
        gather(w_down_ref, all_down_ref, 0, 1),
    ]
    near_ffn = Stages(links, shard_stages(ffn, [1]))
    far_ffn = [
        Stages(links, shard_stages(ffn, [mask for mask in level if mask != 1])) for level in levels
    ]
    x_pool = links.pool(last)
    x_first = links.take(last)

    def x_copy(slot):
        partner = partner_of(slot)
        return links.copy(
            home_ref.at[0, partner // owners],
            x_col_ref.at[slot],
            x_first + slot,
            x_pool + slot,
            "tensor",
            partner,
        )

    mixed_copy = slot_copies(stage_ref, mixed_ref)
    do_copy = slot_copies(stage_ref, do_ref)
    input_copy = slot_copies(stage_ref, input_land_ref)
    down_scatter = GradScatter(links, g_down_ref, down_lands, down_across_ref, False)
    up_scatter = GradScatter(links, g_up_ref, up_lands, up_across_ref, False)
    qkv_scatters = [
        GradScatter(links, g_qkv_ref.at[i], [land.at[i] for land in qkv_lands], qkv_across_ref.at[i], True)
        for i in range(3)
    ]
    norm_sum = NormSum(links, norm_ref, norm_land_ref, dp_bits, tensors)

    def next_x(slot):
        x_copy(slot).wait_send()
        if slot + 1 < last - 1:
            x_copy(slot + 1).start()

    shard_copies = [one.own_copy(local_sem.at[5 + i]) for i, one in enumerate(ffn)]

    def start_phase(raw_ref, raw_qkv_ref):
        loads = [
            pltpu.make_async_copy(ref, raw_ref.at[n], local_sem.at[n])
            for n, ref in enumerate((x_ref, dual_in_ref, cot_post_ref, cot_dual_ref))
        ]
        load_qkv = pltpu.make_async_copy(w_qkv_ref, raw_qkv_ref, local_sem.at[4])
        small_loads = [pltpu.make_async_copy(seg_ref, seg_in_ref, local_sem.at[8])] + [
            pltpu.make_async_copy(ref, norms_ref.at[pl.ds(n, 1)], local_sem.at[9 + n])
            for n, ref in enumerate((gain_one_ref, bias_one_ref, gain_two_ref, bias_two_ref))
        ]
        start(loads[:1] + [load_qkv] + loads[1:] + small_loads + shard_copies)
        greet(dp_bits, tensors)
        load_qkv.wait()
        for i in range(3):
            all_qkv_ref[me, i] = raw_qkv_ref[i].T.reshape(all_qkv_ref.shape[2:])
        loads[0].wait()
        home_ref[0] = jnp.swapaxes(raw_ref[0], 0, 1)
        greeted(dp_bits, tensors)
        qkv.begin()
        x_copy(0).start()
        if last > 1:
            x_copy(last - 1).start()
        x_col_ref[last] = home_ref[0, me // owners]
        norm_ref[...] = jnp.zeros_like(norm_ref)
        lse_columns_ref[...] = jnp.zeros_like(lse_columns_ref)
        own_seg_ref[...] = jnp.zeros_like(own_seg_ref)
        for copy in small_loads:
            copy.wait()
        seg_row = lax.broadcasted_iota(jnp.int32, seg_in_ref.shape, 0)
        own_seg = jnp.where(seg_row == me // owners, seg_in_ref[...], 0).astype(F32)
        seg_line_ref[0:1, :] = jnp.sum(own_seg, axis=0, keepdims=True)
        for slot in range(tensors):
            spot = pl.ds(pl.multiple_of(partner_of(slot) * rows, rows), rows)
            own_seg_ref[slot : slot + 1, :] = seg_line_ref[0:1, spot]
        seg_columns = own_seg_ref[...].T
        for slot in range(tensors):
            at = slice(slot * rows, (slot + 1) * rows)
            lane = lax.broadcasted_iota(jnp.int32, (rows, 2 * E), 1)
            same = seg_columns[:, slot : slot + 1] == lane.astype(F32)
            marks = jnp.where(lane < DOCUMENTS, same.astype(F32), 0.0)
            ones = jnp.where((lane >= DOCUMENTS) & (lane < DOCUMENTS + PARTS), 1.0, marks)
            key_marks_ref[at, :] = ones.astype(BF16)
            key_marks_t_ref[:, at] = ones.T.astype(BF16)
            line = lax.broadcasted_iota(jnp.int32, (2 * E, rows), 0)
            other = own_seg_ref[slot : slot + 1, :] != line.astype(F32)
            bias = jnp.where((line < DOCUMENTS) & other, NEGATIVE, 0.0)
            query_marks_ref[:, at] = bias.astype(BF16)
            query_marks_n_ref[at, :] = bias.T.astype(BF16)
        if owners > 1:
            g_qkv_ref[...] = jnp.zeros_like(g_qkv_ref)
        turned = 1
        for stage in range(qkv.count):
            if turned < 4:
                loads[turned].wait()
                home_ref[turned] = jnp.swapaxes(raw_ref[turned], 0, 1)
                turned += 1
            if stage == qkv.count - 1:
                next_x(0)
                near_ffn.begin()
            qkv.advance(stage)
        for copy in shard_copies:
            copy.wait()

    pl.run_scoped(
        start_phase,
        pltpu.VMEM((4, rows, columns, width), BF16),
        pltpu.VMEM(w_qkv_ref.shape, BF16),
    )
    own_shards = pl.ds(me_low * (tensors // owners), tensors // owners)

    def w_t(i):
        return all_qkv_ref[own_shards, i].reshape(lanes, width)

    def forward_phase(
        hidden_ref,
        slope_ref,
        grad_inner_ref,
        up_two_ref,
        middle_ref,
        up_one_ref,
    ):
        order = [last, last - 1] + list(range(last - 1)) if last > 1 else [last, 0]
        for turn, slot in enumerate(order):
            if slot < last:
                x_copy(slot).wait_recv()
            if 0 < slot < last - 1:
                next_x(slot)
            if turn + 1 == tensors:
                far_ffn[0].begin()
            block = x_col_ref[slot]
            at = slice(slot * rows, (slot + 1) * rows)
            q_ref[at, :] = dot_nt(block, w_t(0)).astype(BF16) * jnp.bfloat16(0.125)
            k_ref[at, :] = dot_nt(block, w_t(1)).astype(BF16)
            v_ref[at, :] = dot_nt(block, w_t(2)).astype(BF16)
            qt_ref[:, at] = dot_nt(w_t(0), block).astype(BF16) * jnp.bfloat16(0.125)
            kt_ref[:, at] = dot_nt(w_t(1), block).astype(BF16)
            xt_ref[:, at] = block.T
            if turn == min(2, last):
                near_ffn.advance(0)

        def gather_step(level, stage):
            def run():
                far_ffn[level].advance(stage)
                if stage == 0 and level + 1 < len(far_ffn):
                    far_ffn[level + 1].begin()

            return run

        steps = tensors * pairs
        def near_step(stage):
            return lambda: near_ffn.advance(stage)

        near_events = [
            (NEAR_DUE + GATHER_STEP * (stage - 1), near_step(stage))
            for stage in range(1, near_ffn.count)
        ]
        gather_events = sorted(
            (
                (GATHER_DUE + GATHER_LEVEL * level + GATHER_STEP * stage, level, stage)
                for level in range(tensor_bits)
                for stage in range(1 + dp_bits)
            ),
        )
        late = [gather_step(*which) for due, *which in gather_events if due >= 16]
        gather_events = [
            (due * steps // 16, gather_step(*which)) for due, *which in gather_events if due < 16
        ] + [(due * steps // 16, one) for due, one in near_events]

        @pl.loop(0, tensors)
        def _(slot):
            at_rows = pl.ds(pl.multiple_of(slot * rows, rows), rows)
            @pl.loop(0, pairs)
            def _(j):
                for due, one in gather_events:

                    @pl.when(slot * pairs + j == due)
                    def _():
                        one()

                at = pl.ds(pl.multiple_of(j * 2 * E, 2 * E), 2 * E)
                keys = with_marks(kt_ref[at, :], key_marks_t_ref[...])
                values = jnp.concatenate([v_ref[:, at], key_marks_ref[...]], axis=1)
                queries = q_ref[at_rows, at]
                marks = query_marks_n_ref[at_rows, :]
                lane = lax.broadcasted_iota(jnp.int32, queries.shape, 1)
                results = []
                for half in range(2):
                    own = (lane < E) if half == 0 else (lane >= E)
                    own_queries = jnp.where(own, queries, jnp.zeros_like(queries))
                    scores = dot_nn(jnp.concatenate([own_queries, marks], axis=1), keys)
                    top = jnp.max(scores, axis=1, keepdims=True)
                    raised = jnp.exp(scores - top).astype(BF16)
                    result = dot_nn(raised, values)
                    denom = result[:, 2 * E + DOCUMENTS : 2 * E + DOCUMENTS + 1]
                    results.append(result[:, : 2 * E] * (1.0 / denom))
                    lse = top + jnp.log(denom)
                    lse_columns_ref[...] = jnp.where(
                        lane == 2 * j + half, lse, lse_columns_ref[...]
                    )
                block = jnp.where(lane < E, results[0], results[1])
                o_ref[slot, :, at] = block

                @pl.when(slot < last)
                def _():
                    stage_ref[slot, :, at] = block.astype(BF16)

                @pl.when(slot == last)
                def _():
                    mixed_ref[last, :, at] = block.astype(BF16)

            lse_ref[slot] = lse_columns_ref[...].T[: lse_ref.shape[1]]

            @pl.when(slot < last)
            def _():
                mixed_copy(slot, partner_of(slot)).start()

        for one in late:
            one()

        gain_one, bias_one = norms_ref[0:1, :], norms_ref[1:2, :]
        gain_two, bias_two = norms_ref[2:3, :], norms_ref[3:4, :]

        @pl.loop(0, columns)
        def _(i):
            column = partner_of(owners * i) // owners
            for r in range(owners):

                @pl.when(owners * i + r < last)
                def _():
                    mixed_copy(owners * i + r, partner_of(owners * i + r)).wait()

            def slot_of(h):
                return last - owners * (columns - 1 - i) - flip(me_low, h)

            mixed = jnp.concatenate([mixed_ref[slot_of(h)] for h in range(owners)], axis=1)
            at = pl.ds(pl.multiple_of(i * rows, rows), rows)
            branch_one = dot_nn(mixed, all_out_ref[...].reshape(width, width))
            normed_one, factor_one = norm_forward(home_ref[0, column].astype(F32) + branch_one)
            middle = normed_one * gain_one + bias_one
            middle_low = middle.astype(BF16)
            middle_ref[:, at] = middle_low.T
            branch_two = jnp.zeros((rows, width), F32)

            for t in range(tensors):
                inner = dot_nn(middle_low, all_up_ref[t].reshape(width, share))
                square = inner * inner
                bend = jnp.tanh(GELU_A * (inner + GELU_B * (square * inner)))
                hidden = (0.5 * inner * (1.0 + bend)).astype(BF16)
                slope_ref[t] = 0.5 * (1.0 + bend) + (0.5 * GELU_A) * inner * (
                    1.0 - bend * bend
                ) * (1.0 + (3.0 * GELU_B) * square)
                hidden_ref[t, at, :] = hidden
                branch_two = branch_two + dot_nn(hidden, all_down_ref[t].reshape(share, width))
            normed_two, factor_two = norm_forward(middle + branch_two)
            results_ref[0, column] = normed_two * gain_two + bias_two
            results_ref[1, column] = home_ref[1, column].astype(F32) + branch_one + branch_two
            cot_dual = home_ref[3, column].astype(F32)
            upstream = home_ref[2, column].astype(F32)
            d_two = norm_backward(upstream, normed_two, factor_two, gain_two)
            norm_ref[2:3, :] += jnp.sum(upstream * normed_two, axis=0, keepdims=True)
            norm_ref[3:4, :] += jnp.sum(upstream, axis=0, keepdims=True)
            up_two = (d_two + cot_dual).astype(BF16)
            up_two_ref[:, at] = up_two.T
            grad_middle = d_two
            for t in range(tensors):
                grad_hidden = dot_nt(up_two, all_down_ref[t].reshape(share, width))
                grad_inner = (grad_hidden * slope_ref[t]).astype(BF16)
                grad_inner_ref[t, at, :] = grad_inner
                grad_middle = grad_middle + dot_nt(grad_inner, all_up_ref[t].reshape(width, share))
            d_one = norm_backward(grad_middle, normed_one, factor_one, gain_one)
            norm_ref[0:1, :] += jnp.sum(grad_middle * normed_one, axis=0, keepdims=True)
            norm_ref[1:2, :] += jnp.sum(grad_middle, axis=0, keepdims=True)
            results_ref[2, column] = d_one
            up_one = (d_one + cot_dual).astype(BF16)
            up_one_ref[:, at] = up_one.T
            grad_mixed = dot_nt(up_one, all_out_ref[...].reshape(width, width)).astype(BF16)
            for h in range(owners):
                slot = slot_of(h)
                piece = grad_mixed[:, h * lanes : (h + 1) * lanes]

                @pl.when(slot < last)
                def _():
                    stage_ref[slot, :, :lanes] = piece
                    do_copy(slot, partner_of(slot)).start()

                @pl.when(slot == last)
                def _():
                    do_ref[last] = piece

        norm_sum.begin()
        cut = (2,) * dp_bits + (width >> dp_bits,)

        @pl.loop(0, tensors)
        def _(t):
            g_down = dot_nn(up_two_ref[...], hidden_ref[t]).astype(BF16)
            g_down_ref[t] = g_down.reshape(cut + (share,))

        down_scatter.begin()
        every = (slice(None),) * (dp_bits + 1)

        @pl.loop(0, tensors)
        def _(t):
            g_up = dot_nn(middle_ref[...], grad_inner_ref[t]).astype(BF16)
            g_up_ref[(t,) + every + (slice(0, share),)] = g_up.reshape(cut + (share,))

        def mixed_of(i):
            def slot_of(h):
                return last - owners * (columns - 1 - i) - flip(me_low, h)

            return jnp.concatenate([mixed_ref[slot_of(h)] for h in range(owners)], axis=1)

        all_mixed = jnp.concatenate([mixed_of(i) for i in range(columns)], axis=0)
        g_out = dot_nn(up_one_ref[...], all_mixed).astype(BF16)
        for t in range(tensors):
            g_up_ref[(t,) + every + (slice(share, share + shard),)] = g_out[
                :, t * shard : (t + 1) * shard
            ].reshape(cut + (shard,))
        up_scatter.begin()

    pl.run_scoped(
        forward_phase,
        pltpu.VMEM((tensors, tokens, share), BF16),
        pltpu.VMEM((tensors, rows, share), F32),
        pltpu.VMEM((tensors, tokens, share), BF16),
        pltpu.VMEM((width, tokens), BF16),
        pltpu.VMEM((width, tokens), BF16),
        pltpu.VMEM((width, tokens), BF16),
    )

    def backward_phase(dot_ref, delta_ref, dq_ref, dk_ref, dv_ref, grads_ref):
        dq_ref[...] = jnp.zeros_like(dq_ref)
        dk_ref[...] = jnp.zeros_like(dk_ref)
        dv_ref[...] = jnp.zeros_like(dv_ref)

        def receive(slot):
            if slot < last:
                do_copy(slot, partner_of(slot)).wait()
            at = slice(slot * rows, (slot + 1) * rows)
            dot_ref[:, at] = do_ref[slot].T
            product = (do_ref[slot].astype(F32) * o_ref[slot]).T
            delta_ref[slot, :heads] = jnp.sum(product.reshape(heads, E, rows), axis=1)

        def advance(scatter, step):
            def run():
                scatter.advance(step)
                if scatter is up_scatter:
                    norm_sum.advance(step)

            return run

        counts = [
            count for wave in range(tensors) for count in (tensors - wave, last - wave) if count
        ]
        begins, done = [], 0
        for count in counts:
            for j in range(pairs):
                begins.append((done + count * j / pairs) / (tensors * tensors))
            done += count
        count = down_scatter.steps
        wishes = []
        for scatter, dues in ((down_scatter, DOWN_DUES), (up_scatter, UP_DUES)):
            wishes.append((dues[0], advance(scatter, 0)))
            for step in range(1, count):
                due = dues[1] + (dues[2] - dues[1]) * (step - 1) / max(count - 2, 1)
                wishes.append((due, advance(scatter, step)))
        wishes = [(next(n for n, at in enumerate(begins) if at >= wish), one) for wish, one in wishes]

        def block_of(number, q_slot, q_count, k_slot, k_count):
            at_q = slice(q_slot * rows, (q_slot + q_count) * rows)
            at_k = slice(k_slot * rows, (k_slot + k_count) * rows)

            @pl.loop(0, pairs)
            def _(j):
                for place, one in wishes:
                    if place // pairs == number:

                        @pl.when(j == place % pairs)
                        def _():
                            one()

                at = pl.ds(pl.multiple_of(j * 2 * E, 2 * E), 2 * E)
                key_marks = key_marks_ref[at_k, :]
                keys = jnp.concatenate([k_ref[at_k, at], key_marks], axis=1)
                values = jnp.concatenate([v_ref[at_k, at], key_marks], axis=1)
                query_marks = query_marks_ref[:, at_q]
                no_marks = jnp.zeros_like(query_marks)
                queries = q_ref[at_q, at]
                ups = do_ref[q_slot : q_slot + q_count, :, at].reshape(q_count * rows, 2 * E)
                sums = []
                for half in range(2):

                    def row_of(ref):
                        row = pl.ds(2 * j + half, 1)
                        slots = range(q_slot, q_slot + q_count)
                        return jnp.concatenate([ref[slot, row, :] for slot in slots], axis=1)

                    minus_lse = with_row(query_marks, row_of(lse_ref))
                    minus_delta = with_row(no_marks, row_of(delta_ref))
                    probs = jnp.exp(dot_nn(keys, with_marks(half_rows(qt_ref[at, at_q], half), minus_lse)))
                    pushed = dot_nn(values, with_marks(half_rows(dot_ref[at, at_q], half), minus_delta))
                    delta = (probs * pushed).astype(BF16)
                    at_head = pl.ds(pl.multiple_of((2 * j + half) * E, E), E)
                    dq_ref[at_head, at_q] += dot_nn(kt_ref[at_head, at_k], delta)
                    sums.append((dot_nn(delta, queries), dot_nn(probs.astype(BF16), ups)))
                low_half = lax.broadcasted_iota(jnp.int32, sums[0][0].shape, 1) < E
                dk_ref[at_k, at] += jnp.where(low_half, sums[0][0], sums[1][0])
                dv_ref[at_k, at] += jnp.where(low_half, sums[0][1], sums[1][1])

        for wave in range(tensors):
            if wave == 0:
                receive(0)
            block_of(2 * wave, wave, 1, wave, tensors - wave)
            if wave == 0:
                for slot in range(1, tensors):
                    receive(slot)
            if wave < last:
                block_of(2 * wave + 1, wave + 1, last - wave, wave, 1)
            at = slice(wave * rows, (wave + 1) * rows)
            grads = (
                (dq_ref[:, at] * 0.125).T.astype(BF16),
                dk_ref[at, :].astype(BF16),
                dv_ref[at, :].astype(BF16),
            )
            part = jnp.zeros((rows, width), F32)
            for i in range(3):
                grads_ref[i, at, :] = grads[i]
                part = part + dot_nn(grads[i], w_t(i))

            if wave < last:
                stage_ref[wave] = part.astype(BF16)
                input_copy(wave, partner_of(wave)).start()
            else:
                results_ref[2, me // owners] += part

        for i in range(3):
            g = dot_nn(xt_ref[...], grads_ref[i]).astype(BF16)
            for t in range(tensors // owners):
                g_qkv_ref[i, me_low * (tensors // owners) + t] = g[
                    :, t * shard : (t + 1) * shard
                ].reshape((2,) * dp_bits + (width >> dp_bits, shard))
            qkv_scatters[i].begin()
            if i:
                qkv_scatters[i - 1].advance(0)

    pl.run_scoped(
        backward_phase,
        pltpu.VMEM((lanes, length), BF16),
        pltpu.VMEM((tensors, max(heads, 8), rows), F32),
        pltpu.VMEM((lanes, length), F32),
        pltpu.VMEM((length, lanes), F32),
        pltpu.VMEM((length, lanes), F32),
        pltpu.VMEM((3, length, lanes), BF16),
    )


    def end_phase(turned_ref):
        stores = [
            pltpu.make_async_copy(turned_ref.at[n], ref, local_sem.at[n])
            for n, ref in enumerate((post_ref, dual_ref, grad_post_ref))
        ]

        def store(n):
            turned_ref[n] = jnp.swapaxes(results_ref[n], 0, 1)
            stores[n].start()

        def advance(step):
            for one in qkv_scatters:
                one.advance(step)

        store(0)
        qkv_scatters[2].advance(0)
        store(1)
        if dp_bits > 1:
            advance(1)
        if last > 1:
            x_copy(last - 1).wait_send()
        for slot in range(last):
            input_copy(slot, partner_of(slot)).wait()
            results_ref[2, partner_of(slot) // owners] += input_land_ref[slot].astype(F32)
        store(2)
        for step in range(2, dp_bits):
            advance(step)
        small = [
            pltpu.make_async_copy(small_refs[n], ref, local_sem.at[8 + n])
            for n, ref in enumerate((r_qkv_ref, r_down_ref, r_up_ref, r_norm_ref))
        ]
        small_refs[1][...] = down_scatter.result()
        small_refs[2][...] = up_scatter.result()
        count = width // (tensors << dp_bits)
        first = (lax.axis_index("dp") * tensors + me) * count
        small_refs[3][...] = pltpu.roll(norm_sum.result(), width - first, 1)[:, :128]
        start(small[1:])
        for i in range(3):
            small_refs[0][i] = qkv_scatters[i].result()
        small[0].start()
        for copy in small:
            copy.wait()
        for copy in stores:
            copy.wait()

    pl.run_scoped(end_phase, pltpu.VMEM((3, rows, columns, width), F32))


def hand_over_kernel(*refs):
    sources, results = refs[:7], refs[7:]
    for n in range(3):
        results[n][...] = sources[n][...]

    @pl.when(pl.program_id(0) == 0)
    def _():
        grad_qkv, grad_down, grad_up_out, grad_norm = sources[3:]
        share = results[4].shape[1]
        results[3][...] = grad_qkv[...]
        results[4][...] = grad_down[...]
        results[5][...] = grad_up_out[:, :share]
        results[6][...] = grad_up_out[:, share:]
        for n in range(4):
            results[7 + n][...] = grad_norm[n : n + 1, : results[7 + n].shape[1]]


def body(
    x_post,
    x_dual,
    cot_post,
    cot_dual,
    segment_ids,
    w_qkv,
    w_out,
    w_up,
    w_down,
    gain_one,
    bias_one,
    gain_two,
    bias_two,
):
    tensors, devices = lax.axis_size("tensor"), lax.axis_size("dp")
    dp_bits = log2(devices)
    rows, columns, width = x_post.shape
    length = tensors * rows
    owners = tensors // columns
    lanes = width // owners
    share, shard = w_up.shape[1], w_out.shape[0]
    piece = width // devices
    heads = lanes // E
    me = lax.axis_index("tensor")
    def cut(array, dim):
        bits = min(dp_bits, log2(array.shape[dim] // 16))
        shape = array.shape[:dim] + (2,) * bits + (array.shape[dim] >> bits,) + array.shape[dim + 1 :]
        return array.reshape(shape)

    shards = [cut(w_out, 0), cut(w_up, 0), cut(w_down, 0)]
    qkv_shape = jax.eval_shape(lambda w: cut(jnp.swapaxes(w, 1, 2), 1), w_qkv).shape
    in_place = pl.BlockSpec(memory_space=pl.ANY)
    shape = jax.ShapeDtypeStruct
    bits = (2,) * dp_bits

    def lands(lane_count, *lead):
        return [
            pltpu.VMEM(lead + (tensors,) + bits[: dp_bits - 1 - step] + (piece, lane_count), BF16)
            for step in range(dp_bits)
        ]

    small_out = (
        shape((3, piece, shard), F32),
        shape((piece, share), F32),
        shape((piece, share + shard), F32),
        shape((8, 128), F32),
    )
    cuts = [len(qkv_shape) - 3] + [len(one.shape) - 2 for one in shards]
    links = link_counts(tensors, dp_bits, cuts)
    layer = pl.pallas_call(
        functools.partial(layer_kernel, dp_bits, columns),
        out_shape=(
            shape((rows, columns, width), F32),
            shape((rows, columns, width), F32),
            shape((rows, columns, width), F32),
        )
        + small_out,
        in_specs=[in_place] * 13,
        out_specs=(in_place,) * 7,
        scratch_shapes=[
            pltpu.VMEM((4, columns, rows, width), BF16),
            pltpu.VMEM((tensors, rows, width), BF16),
            pltpu.VMEM((tensors,) + qkv_shape, BF16),
        ]
        + [pltpu.VMEM((tensors,) + one.shape, BF16) for one in shards]
        + [
            pltpu.VMEM((tensors, rows, lanes), BF16),
            pltpu.VMEM((tensors, rows, lanes), BF16),
            pltpu.VMEM((tensors - 1, rows, width), BF16),
            pltpu.VMEM((tensors,) + bits + (piece, share), BF16),
            pltpu.VMEM((tensors,) + bits + (piece, share + shard), BF16),
            pltpu.VMEM((3, tensors) + bits + (piece, shard), BF16),
            lands(share),
            pltpu.VMEM((tensors - 1, piece, share), BF16),
            lands(share + shard),
            pltpu.VMEM((tensors - 1, piece, share + shard), BF16),
            lands(shard, 3),
            pltpu.VMEM((3, tensors - 1, piece, shard), BF16),
            pltpu.VMEM((8, width), F32),
            pltpu.VMEM((dp_bits + tensors - 1, 8, width), F32),
            pltpu.VMEM((length, lanes), BF16),
            pltpu.VMEM((length, lanes), BF16),
            pltpu.VMEM((length, lanes), BF16),
            pltpu.VMEM((lanes, length), BF16),
            pltpu.VMEM((lanes, length), BF16),
            pltpu.VMEM((width, length), BF16),
            pltpu.VMEM((tensors, rows, lanes), F32),
            pltpu.VMEM((tensors, max(heads, 8), rows), F32),
            pltpu.VMEM((3, columns, rows, width), F32),
            pltpu.VMEM((tensors - 1, rows, width), BF16),
            pltpu.VMEM((length, 2 * E), BF16),
            pltpu.VMEM((2 * E, length), BF16),
            pltpu.VMEM((2 * E, length), BF16),
            pltpu.VMEM((length, 2 * E), BF16),
            pltpu.VMEM((rows, 2 * E), F32),
            pltpu.VMEM((max(tensors, 8), rows), F32),
            pltpu.VMEM((8, length), F32),
            pltpu.VMEM((columns, length), jnp.int32),
            pltpu.VMEM((8, width), F32),
            [pltpu.VMEM(one.shape, F32) for one in small_out],
            pltpu.SemaphoreType.DMA((links[1],)),
            pltpu.SemaphoreType.DMA((links[0],)),
            pltpu.SemaphoreType.DMA((16,)),
        ],
        compiler_params=pltpu.CompilerParams(
            vmem_limit_bytes=VMEM_BYTES, collective_id=0, has_side_effects=True
        ),
        name="layer",
    )
    made = layer(
        segment_ids.T,
        x_post,
        x_dual,
        cot_post,
        cot_dual,
        w_qkv,
        *shards,
        *(one.reshape(1, width) for one in (gain_one, bias_one, gain_two, bias_two)),
    )
    count = width // (tensors * devices)
    blocks = 2
    block_spec = pl.BlockSpec((rows // blocks, columns, width), lambda i: (i, 0, 0))

    def whole_spec(one):
        return pl.BlockSpec(one.shape, lambda i: (0,) * len(one.shape))

    small = (
        shape((3, piece, shard), F32),
        shape((piece, share), F32),
        shape((piece, share), F32),
        shape((piece, shard), F32),
    ) + (shape((1, count), F32),) * 4
    results = pl.pallas_call(
        hand_over_kernel,
        out_shape=tuple(shape(one.shape, F32) for one in made[:3]) + small,
        grid=(blocks,),
        in_specs=[block_spec] * 3 + [whole_spec(one) for one in made[3:]],
        out_specs=(block_spec,) * 3 + tuple(whole_spec(one) for one in small),
        name="hand_over",
    )(*made)
    post_out, dual_out, grad_post, g_qkv, g_down, g_up, g_out = results[:7]
    norms = tuple(one.reshape(count) for one in results[7:])
    return (post_out, dual_out, grad_post, g_qkv, g_out.T, g_up, g_down.T) + norms


def solution(mesh):
    placed = (
        P("tensor", "dp", None),
        P("tensor", "dp", None),
        P("tensor", "dp", None),
        P("tensor", "dp", None),
        P(None, "dp"),
        P(None, None, "tensor"),
        P("tensor", None),
        P(None, "tensor"),
        P("tensor", None),
        P(),
        P(),
        P(),
        P(),
    )
    return jax.shard_map(
        body,
        mesh=mesh,
        in_specs=placed,
        out_specs=(
            P("tensor", "dp", None),
            P("tensor", "dp", None),
            P("tensor", "dp", None),
            P(None, "dp", "tensor"),
            P("tensor", "dp"),
            P("dp", "tensor"),
            P("tensor", "dp"),
            P(("dp", "tensor")),
            P(("dp", "tensor")),
            P(("dp", "tensor")),
            P(("dp", "tensor")),
        ),
        check_vma=False,
    )
```

```python
import functools
import itertools

import jax
import jax.numpy as jnp
from jax import lax
from jax.experimental import pallas as pl
from jax.experimental.pallas import tpu as pltpu
from jax.sharding import PartitionSpec as P

E = 64
EPSILON = 1e-05
NEGATIVE = -1e30
DOCUMENTS = 4
DOWN_DUES = (0.06, 0.35, 0.75)
UP_DUES = (0.10, 0.5, 0.9)
GATHER_DUE, GATHER_LEVEL, GATHER_STEP = 1, 4, 4
NEAR_DUE = 1
GROUP = 1
PARTS = 3
GELU_A = 0.7978845608028654
GELU_B = 0.044715
F32 = jnp.float32
BF16 = jnp.bfloat16
VMEM_BYTES = 63 * 1024 * 1024


def dot_nn(a, b):
    return lax.dot_general(a, b, (((1,), (0,)), ((), ())), preferred_element_type=F32)


def dot_nt(a, b):
    return lax.dot_general(a, b, (((1,), (1,)), ((), ())), preferred_element_type=F32)


def dot_tn(a, b):
    return lax.dot_general(a, b, (((0,), (0,)), ((), ())), preferred_element_type=F32)


def row_mean(a):
    return jnp.mean(a, axis=-1, keepdims=True)


def norm_forward(total):
    centre = total - row_mean(total)
    factor = lax.rsqrt(row_mean(centre * centre) + EPSILON)
    return centre * factor, factor


def norm_backward(upstream, normed, factor, gain):
    scaled = upstream * gain
    inner = scaled - row_mean(scaled) - normed * row_mean(scaled * normed)
    return factor * inner


def with_marks(block, marks):
    return jnp.concatenate([block, marks], axis=0)


def with_row(marks, row):
    line = lax.broadcasted_iota(jnp.int32, (16, row.shape[1]), 0)
    top = marks[:16].astype(F32)
    rest = -row
    for part in range(PARTS):
        term = rest.astype(BF16).astype(F32)
        rest = rest - term
        top = jnp.where(line == DOCUMENTS + part, term, top)
    return jnp.concatenate([top.astype(BF16), marks[16:]], axis=0)


def half_rows(block, half):
    zeros = jnp.zeros((E, block.shape[1]), block.dtype)
    if half == 0:
        return jnp.concatenate([block[:E], zeros], axis=0)
    return jnp.concatenate([zeros, block[E:]], axis=0)


MESH = pl.DeviceIdType.MESH


def bit_of(index, bit):
    return (index // (1 << bit)) % 2


def flip(index, mask):
    for bit in range(mask.bit_length()):
        if (mask >> bit) % 2:
            index = index + (1 - 2 * bit_of(index, bit)) * (1 << bit)
    return index


def log2(count):
    return count.bit_length() - 1


class Links:
    def __init__(self, send_sem, recv_sem):
        self.send_sem, self.recv_sem, self.used, self.pooled = send_sem, recv_sem, 0, 0

    def take(self, count):
        first = self.used
        self.used += count
        assert self.used <= self.recv_sem.shape[0]
        return first

    def pool(self, count):
        first = self.pooled
        self.pooled += count
        assert self.pooled <= self.send_sem.shape[0]
        return first

    def copy(self, src, dst, slot, send_slot, axis, partner):
        return pltpu.make_async_remote_copy(
            src_ref=src,
            dst_ref=dst,
            send_sem=self.send_sem.at[send_slot],
            recv_sem=self.recv_sem.at[slot],
            device_id={axis: partner},
            device_id_type=MESH,
        )

    def stages(self, stages):
        first = self.pool(max(len(stage) for stage in stages))
        return [
            [
                self.copy(src, dst, self.take(1), first + n, axis, partner)
                for n, (src, dst, axis, partner) in enumerate(stage)
            ]
            for stage in stages
        ]


def link_counts(tensors, dp_bits, cuts):
    others = tensors - 1
    levels = [0] * log2(tensors)
    for mask in range(2, tensors):
        levels[mask.bit_count() - 1] += 1
    receive = 4 * others + others * (1 + 3 * cuts[0]) + sum(others * (1 + cut) for cut in cuts[1:])
    receive += 5 * (1 + 2 * (dp_bits - 1) + others) + dp_bits + others
    send = 2 * others + 3 * others + 3 + 3 * sum(levels)
    send += 2 * max(2, tensors // 2) + 3 * max(2, others) + others
    return receive, send


def start(copies):
    for copy in copies:
        copy.start()


def finish(copies):
    for copy in copies:
        copy.wait_recv()
        copy.wait_send()


def greet(dp_bits, tensors):
    dp, me = lax.axis_index("dp"), lax.axis_index("tensor")
    barrier = pltpu.get_barrier_semaphore()
    for bit in range(dp_bits):
        pl.semaphore_signal(barrier, inc=1, device_id={"dp": flip(dp, 1 << bit)}, device_id_type=MESH)
    for step in range(1, tensors):
        pl.semaphore_signal(
            barrier, inc=1, device_id={"tensor": (me + step) % tensors}, device_id_type=MESH
        )


def greeted(dp_bits, tensors):
    pl.semaphore_wait(pltpu.get_barrier_semaphore(), dp_bits + tensors - 1)


class WeightGather:
    def __init__(self, src, dst, lead, cut_bits, dp_bits, first, direct=False):
        tensors = dst.shape[0]
        dp, me = lax.axis_index("dp"), lax.axis_index("tensor")
        bits = list(range(dp_bits - 1, dp_bits - 1 - cut_bits, -1))
        if src is None:
            src = dst.at[me]
        self.src, self.dst, self.own = src, dst, me
        inner = [()] if lead == 0 else [(i,) for i in range(dst.shape[1])]
        piece = (slice(None),) * lead + tuple(bit_of(dp, bit) for bit in bits)
        low = [bit for bit in bits if bit == 0]
        high = [bit for bit in bits if bit != 0]
        orders = (high[::-1] + low, high + low)
        count = first
        self.stages = {}
        for mask in range(1, tensors):
            near = mask if direct else mask & -mask
            block = flip(me, mask - near)
            stages = [[] for _ in range(1 + dp_bits)]
            stages[0].append(
                (
                    dst.at[(block,) + piece] if mask != near else src.at[piece],
                    dst.at[(block,) + piece],
                    "tensor",
                    flip(me, near),
                )
            )
            source = flip(me, mask)
            for i in inner:
                order = orders[count % 2]
                count += 1
                for phase, bit in enumerate(order):
                    done = order[:phase]
                    region = (source,) + i + tuple(
                        slice(None) if other in done else bit_of(dp, other) for other in bits
                    )
                    stages[1 + phase].append(
                        (dst.at[region], dst.at[region], "dp", flip(dp, 1 << bit))
                    )
            self.stages[mask] = stages

    def own_copy(self, sem):
        return pltpu.make_async_copy(self.src, self.dst.at[self.own], sem)


class Stages:
    def __init__(self, links, stages):
        self.copies = links.stages(stages)
        self.count = len(stages)

    def begin(self):
        start(self.copies[0])

    def advance(self, stage):
        finish(self.copies[stage])
        if stage + 1 < self.count:
            start(self.copies[stage + 1])


def shard_stages(weights, masks):
    count = len(weights[0].stages[masks[0]])
    return [
        [copy for one in weights for mask in masks for copy in one.stages[mask][stage]]
        for stage in range(count)
    ]


class GradScatter:
    def __init__(self, links, grad, lands, across, direct):
        self.links, self.grad, self.lands, self.across = links, grad, lands, across
        self.tensors = grad.shape[0]
        self.dp, self.me = lax.axis_index("dp"), lax.axis_index("tensor")
        dp_bits = len(lands)
        high = list(range(dp_bits - 1, 0, -1))
        middle = self.tensors // 2
        copies = [
            [
                (
                    grad.at[(slice(None),) * dp_bits + (1 - bit_of(self.dp, 0),)],
                    lands[0],
                    "dp",
                    flip(self.dp, 1),
                )
            ]
        ]
        sums = [[(0, self.tensors, grad, dp_bits - 1, bit_of(self.dp, 0), lands[0])]]
        for step in range(1, dp_bits):
            copies.append([])
            sums.append([])
        for begin, order in ((0, high[::-1]), (middle, high)):
            left = list(high)
            for step, bit in enumerate(order, 1):
                place = left.index(bit)
                left.remove(bit)
                part = pl.ds(begin, middle)
                index = (part,) + (slice(None),) * place + (1 - bit_of(self.dp, bit),)
                copies[step].append(
                    (
                        lands[step - 1].at[index],
                        lands[step].at[part],
                        "dp",
                        flip(self.dp, 1 << bit),
                    )
                )
                sums[step].append(
                    (begin, middle, lands[step - 1], place, bit_of(self.dp, bit), lands[step])
                )
        place = 0
        self.joins = []
        for bit in range(0 if direct else log2(self.tensors)):
            step, found, joins = 1 << bit, [], []
            for high in range(self.tensors >> (bit + 1)):
                mask = high * 2 * step
                found.append(
                    (
                        lands[-1].at[flip(self.me, mask + step)],
                        across.at[place],
                        "tensor",
                        flip(self.me, step),
                    )
                )
                joins.append((mask, place))
                place += 1
            copies.append(found)
            self.joins.append(joins)
        if direct:
            copies.append(
                [
                    (
                        lands[-1].at[flip(self.me, step)],
                        across.at[step - 1],
                        "tensor",
                        flip(self.me, step),
                    )
                    for step in range(1, self.tensors)
                ]
            )
            self.joins = [[(0, step) for step in range(self.tensors - 1)]]
        self.copies = links.stages(copies)
        self.sums = sums + [[] for _ in self.joins[1:]]
        self.steps = len(copies) - 1

    def begin(self):
        start(self.copies[0])

    def advance(self, step):
        finish(self.copies[step])
        for first, count, source, place, own, land in self.sums[step]:

            @pl.loop(first, first + count)
            def _(t):
                for spot in itertools.product((0, 1), repeat=len(land.shape) - 3):
                    whole = (t,) + spot[:place] + (own,) + spot[place:]
                    here = (t,) + spot
                    land[here] = (land[here].astype(F32) + source[whole].astype(F32)).astype(BF16)

        if step >= len(self.lands):
            for mask, place in self.joins[step - len(self.lands)]:
                spot = flip(self.me, mask)
                total = self.lands[-1][spot].astype(F32) + self.across[place].astype(F32)
                self.lands[-1][spot] = total.astype(BF16)
        start(self.copies[step + 1])

    def result(self):
        finish(self.copies[-1])
        total = self.lands[-1][self.me].astype(F32)
        for _, place in self.joins[-1]:
            total = total + self.across[place].astype(F32)
        return total


class NormSum:
    def __init__(self, links, total, land, dp_bits, tensors):
        dp, me = lax.axis_index("dp"), lax.axis_index("tensor")
        self.total, self.land = total, land
        copies = [
            [(total, land.at[bit], "dp", flip(dp, 1 << bit))] for bit in range(dp_bits)
        ]
        copies.append(
            [
                (total, land.at[dp_bits + step - 1], "tensor", flip(me, step))
                for step in range(1, tensors)
            ]
        )
        self.copies = links.stages(copies)

    def begin(self):
        start(self.copies[0])

    def advance(self, step):
        if step + 1 < len(self.copies):
            finish(self.copies[step])
            self.total[...] += self.land[step]
            start(self.copies[step + 1])

    def result(self):
        finish(self.copies[-1])
        total = self.total[...]
        for step in range(len(self.copies) - 1, self.land.shape[0]):
            total = total + self.land[step]
        return total


def layer_kernel(
    dp_bits,
    columns,
    seg_ref,
    x_ref,
    dual_in_ref,
    cot_post_ref,
    cot_dual_ref,
    w_qkv_ref,
    w_out_ref,
    w_up_ref,
    w_down_ref,
    gain_one_ref,
    bias_one_ref,
    gain_two_ref,
    bias_two_ref,
    post_ref,
    dual_ref,
    grad_post_ref,
    r_qkv_ref,
    r_down_ref,
    r_up_ref,
    r_norm_ref,
    home_ref,
    x_col_ref,
    all_qkv_ref,
    all_out_ref,
    all_up_ref,
    all_down_ref,
    mixed_ref,
    do_ref,
    input_land_ref,
    g_down_ref,
    g_up_ref,
    g_qkv_ref,
    down_lands,
    down_across_ref,
    up_lands,
    up_across_ref,
    qkv_lands,
    qkv_across_ref,
    norm_ref,
    norm_land_ref,
    q_ref,
    k_ref,
    v_ref,
    qt_ref,
    kt_ref,
    xt_ref,
    o_ref,
    lse_ref,
    base_ref,
    stage_ref,
    key_marks_ref,
    key_marks_t_ref,
    query_marks_ref,
    query_marks_n_ref,
    lse_columns_ref,
    own_seg_ref,
    seg_line_ref,
    seg_in_ref,
    norms_ref,
    small_refs,
    send_sem,
    recv_sem,
    local_sem,
):
    tensors, rows, width = x_col_ref.shape
    owners = tensors // columns
    lanes = mixed_ref.shape[-1]
    heads = lanes // E
    pairs = heads // 2
    share = all_up_ref.shape[-1]
    shard = width // tensors
    last = tensors - 1
    length = tensors * rows
    tokens = columns * rows
    tensor_bits = log2(tensors)
    me = lax.axis_index("tensor")
    me_low = me % owners
    links = Links(send_sem, recv_sem)

    exchange_pool = links.pool(last)

    def slot_copies(sources, land):
        first = links.take(last)

        def one(slot, partner):
            source = sources.at[slot, :, pl.ds(0, land.shape[-1])]
            return links.copy(
                source, land.at[slot], first + slot, exchange_pool + slot, "tensor", partner
            )

        return one

    def partner_of(slot):
        mask = last - slot
        index = me
        for bit in range(log2(tensors)):
            index = index + bit_of(mask, bit) * (1 - 2 * bit_of(me, bit)) * (1 << bit)
        return index

    def gather(src, dst, lead, first, direct=False):
        return WeightGather(src, dst, lead, len(dst.shape) - lead - 3, dp_bits, first, direct)

    masks = list(range(1, tensors))
    levels = [[mask for mask in masks if mask.bit_count() == n + 1] for n in range(tensor_bits)]
    qkv = Stages(links, shard_stages([gather(None, all_qkv_ref, 1, 0, True)], masks))
    ffn = [
        gather(w_out_ref, all_out_ref, 0, 0),
        gather(w_up_ref, all_up_ref, 0, 0),
        gather(w_down_ref, all_down_ref, 0, 1),
    ]
    near_ffn = Stages(links, shard_stages(ffn, [1]))
    far_ffn = [
        Stages(links, shard_stages(ffn, [mask for mask in level if mask != 1])) for level in levels
    ]
    x_pool = links.pool(last)
    x_first = links.take(last)

    def x_copy(slot):
        partner = partner_of(slot)
        return links.copy(
            home_ref.at[0, partner // owners],
            x_col_ref.at[slot],
            x_first + slot,
            x_pool + slot,
            "tensor",
            partner,
        )

    mixed_copy = slot_copies(stage_ref, mixed_ref)
    do_copy = slot_copies(stage_ref, do_ref)
    input_copy = slot_copies(stage_ref, input_land_ref)
    down_scatter = GradScatter(links, g_down_ref, down_lands, down_across_ref, False)
    up_scatter = GradScatter(links, g_up_ref, up_lands, up_across_ref, False)
    qkv_scatters = [
        GradScatter(links, g_qkv_ref.at[i], [land.at[i] for land in qkv_lands], qkv_across_ref.at[i], True)
        for i in range(3)
    ]
    norm_sum = NormSum(links, norm_ref, norm_land_ref, dp_bits, tensors)

    def next_x(slot):
        x_copy(slot).wait_send()

    shard_copies = [one.own_copy(local_sem.at[5 + i]) for i, one in enumerate(ffn)]

    def start_phase(raw_ref, raw_qkv_ref):
        loads = [
            pltpu.make_async_copy(ref, raw_ref.at[n], local_sem.at[n])
            for n, ref in enumerate((x_ref, dual_in_ref, cot_post_ref, cot_dual_ref))
        ]
        load_qkv = pltpu.make_async_copy(w_qkv_ref, raw_qkv_ref, local_sem.at[4])
        small_loads = [pltpu.make_async_copy(seg_ref, seg_in_ref, local_sem.at[8])] + [
            pltpu.make_async_copy(ref, norms_ref.at[pl.ds(n, 1)], local_sem.at[9 + n])
            for n, ref in enumerate((gain_one_ref, bias_one_ref, gain_two_ref, bias_two_ref))
        ]
        start(loads[:1] + [load_qkv] + loads[1:] + small_loads + shard_copies)
        greet(dp_bits, tensors)
        load_qkv.wait()
        for i in range(3):
            all_qkv_ref[me, i] = raw_qkv_ref[i].T.reshape(all_qkv_ref.shape[2:])
        loads[0].wait()
        home_ref[0] = jnp.swapaxes(raw_ref[0], 0, 1)
        greeted(dp_bits, tensors)
        qkv.begin()
        x_copy(0).start()
        if last > 1:
            x_copy(last - 1).start()
        for slot in range(1, last - 1):
            x_copy(slot).start()
        x_col_ref[last] = home_ref[0, me // owners]
        norm_ref[...] = jnp.zeros_like(norm_ref)
        lse_columns_ref[...] = jnp.zeros_like(lse_columns_ref)
        own_seg_ref[...] = jnp.zeros_like(own_seg_ref)
        for copy in small_loads:
            copy.wait()
        seg_row = lax.broadcasted_iota(jnp.int32, seg_in_ref.shape, 0)
        own_seg = jnp.where(seg_row == me // owners, seg_in_ref[...], 0).astype(F32)
        seg_line_ref[0:1, :] = jnp.sum(own_seg, axis=0, keepdims=True)
        for slot in range(tensors):
            spot = pl.ds(pl.multiple_of(partner_of(slot) * rows, rows), rows)
            own_seg_ref[slot : slot + 1, :] = seg_line_ref[0:1, spot]
        seg_columns = own_seg_ref[...].T
        for slot in range(tensors):
            at = slice(slot * rows, (slot + 1) * rows)
            lane = lax.broadcasted_iota(jnp.int32, (rows, 2 * E), 1)
            same = seg_columns[:, slot : slot + 1] == lane.astype(F32)
            marks = jnp.where(lane < DOCUMENTS, same.astype(F32), 0.0)
            ones = jnp.where((lane >= DOCUMENTS) & (lane < DOCUMENTS + PARTS), 1.0, marks)
            key_marks_ref[at, :] = ones.astype(BF16)
            key_marks_t_ref[:, at] = ones.T.astype(BF16)
            line = lax.broadcasted_iota(jnp.int32, (2 * E, rows), 0)
            other = own_seg_ref[slot : slot + 1, :] != line.astype(F32)
            bias = jnp.where((line < DOCUMENTS) & other, NEGATIVE, 0.0)
            query_marks_ref[:, at] = bias.astype(BF16)
            query_marks_n_ref[at, :] = bias.T.astype(BF16)
        if owners > 1:
            g_qkv_ref[...] = jnp.zeros_like(g_qkv_ref)
        turned = 1
        for stage in range(qkv.count):
            if turned < 4:
                loads[turned].wait()
                home_ref[turned] = jnp.swapaxes(raw_ref[turned], 0, 1)
                turned += 1
            if stage == qkv.count - 1:
                next_x(0)
                near_ffn.begin()
                far_ffn[0].begin()
            qkv.advance(stage)
        for copy in shard_copies:
            copy.wait()

    pl.run_scoped(
        start_phase,
        pltpu.VMEM((4, rows, columns, width), BF16),
        pltpu.VMEM(w_qkv_ref.shape, BF16),
    )
    own_shards = pl.ds(me_low * (tensors // owners), tensors // owners)

    def w_t(i):
        return all_qkv_ref[own_shards, i].reshape(lanes, width)

    def forward_phase(
        hidden_ref,
        slope_ref,
        grad_inner_ref,
        up_two_ref,
        middle_ref,
        up_one_ref,
    ):
        order = [last, last - 1] + list(range(last - 1)) if last > 1 else [last, 0]
        for turn, slot in enumerate(order):
            if slot < last:
                x_copy(slot).wait_recv()
            if 0 < slot < last - 1:
                next_x(slot)
            block = x_col_ref[slot]
            at = slice(slot * rows, (slot + 1) * rows)
            q_ref[at, :] = dot_nt(block, w_t(0)).astype(BF16) * jnp.bfloat16(0.125)
            k_ref[at, :] = dot_nt(block, w_t(1)).astype(BF16)
            v_ref[at, :] = dot_nt(block, w_t(2)).astype(BF16)
            qt_ref[:, at] = dot_nt(w_t(0), block).astype(BF16) * jnp.bfloat16(0.125)
            kt_ref[:, at] = dot_nt(w_t(1), block).astype(BF16)
            xt_ref[:, at] = block.T
            if turn == min(2, last):
                near_ffn.advance(0)

        def gather_step(level, stage):
            def run():
                far_ffn[level].advance(stage)
                if stage == 0 and level + 1 < len(far_ffn):
                    far_ffn[level + 1].begin()

            return run

        steps = tensors * pairs
        def near_step(stage):
            return lambda: near_ffn.advance(stage)

        near_events = [
            (NEAR_DUE + GATHER_STEP * (stage - 1), near_step(stage))
            for stage in range(1, near_ffn.count)
        ]
        gather_events = sorted(
            (
                (GATHER_DUE + GATHER_LEVEL * level + GATHER_STEP * stage, level, stage)
                for level in range(tensor_bits)
                for stage in range(1 + dp_bits)
            ),
        )
        late = [gather_step(*which) for due, *which in gather_events if due >= 16]
        gather_events = [
            (due * steps // 16, gather_step(*which)) for due, *which in gather_events if due < 16
        ] + [(due * steps // 16, one) for due, one in near_events]

        @pl.loop(0, tensors)
        def _(slot):
            at_rows = pl.ds(pl.multiple_of(slot * rows, rows), rows)
            @pl.loop(0, pairs)
            def _(j):
                for due, one in gather_events:

                    @pl.when(slot * pairs + j == due)
                    def _():
                        one()

                at = pl.ds(pl.multiple_of(j * 2 * E, 2 * E), 2 * E)
                keys = with_marks(kt_ref[at, :], key_marks_t_ref[...])
                values = jnp.concatenate([v_ref[:, at], key_marks_ref[...]], axis=1)
                queries = q_ref[at_rows, at]
                marks = query_marks_n_ref[at_rows, :]
                lane = lax.broadcasted_iota(jnp.int32, queries.shape, 1)
                results = []
                for half in range(2):
                    own = (lane < E) if half == 0 else (lane >= E)
                    own_queries = jnp.where(own, queries, jnp.zeros_like(queries))
                    scores = dot_nn(jnp.concatenate([own_queries, marks], axis=1), keys)
                    top = jnp.max(scores, axis=1, keepdims=True)
                    raised = jnp.exp(scores - top).astype(BF16)
                    result = dot_nn(raised, values)
                    denom = result[:, 2 * E + DOCUMENTS : 2 * E + DOCUMENTS + 1]
                    results.append(result[:, : 2 * E] * (1.0 / denom))
                    lse = top + jnp.log(denom)
                    lse_columns_ref[...] = jnp.where(
                        lane == 2 * j + half, lse, lse_columns_ref[...]
                    )
                block = jnp.where(lane < E, results[0], results[1])
                o_ref[slot, :, at] = block

                @pl.when(slot < last)
                def _():
                    stage_ref[slot, :, at] = block.astype(BF16)

                @pl.when(slot == last)
                def _():
                    mixed_ref[last, :, at] = block.astype(BF16)

            lse_ref[slot] = lse_columns_ref[...].T[: lse_ref.shape[1]]

            @pl.when(slot < last)
            def _():
                mixed_copy(slot, partner_of(slot)).start()

        for one in late:
            one()

        gain_one, bias_one = norms_ref[0:1, :], norms_ref[1:2, :]
        gain_two, bias_two = norms_ref[2:3, :], norms_ref[3:4, :]

        def place_of(turn):
            first, final = 1 - (turn + columns - 1) // columns, (turn + 1) // columns
            return turn + 1 - first - (columns - 1) * final

        def slot_of(place, h):
            return last - owners * (columns - 1 - place) - flip(me_low, h)

        def mixed_at(place):
            return jnp.concatenate([mixed_ref[slot_of(place, h)] for h in range(owners)], axis=1)

        group = GROUP if columns % GROUP == 0 else 1

        @pl.loop(0, columns // group)
        def _(turn):
            places = [place_of(turn * group + n) for n in range(group)]
            taken = [partner_of(owners * place) // owners for place in places]
            for place in places:
                for r in range(owners):

                    @pl.when(owners * place + r < last)
                    def _():
                        mixed_copy(owners * place + r, partner_of(owners * place + r)).wait()

            def home(n):
                return jnp.concatenate([home_ref[n, column] for column in taken]).astype(F32)

            def replace(n, value):
                for m, column in enumerate(taken):
                    home_ref[n, column] = value[m * rows : (m + 1) * rows].astype(BF16)

            mixed = jnp.concatenate([mixed_at(place) for place in places])
            at = pl.ds(pl.multiple_of(turn * group * rows, group * rows), group * rows)
            branch_one = dot_nn(mixed, all_out_ref[...].reshape(width, width))
            normed_one, factor_one = norm_forward(home(0) + branch_one)
            middle = normed_one * gain_one + bias_one
            middle_low = middle.astype(BF16)
            middle_ref[:, at] = middle_low.T
            branch_two = jnp.zeros((group * rows, width), F32)
            for t in range(tensors):
                inner = dot_nn(middle_low, all_up_ref[t].reshape(width, share))
                square = inner * inner
                bend = jnp.tanh(GELU_A * (inner + GELU_B * (square * inner)))
                hidden = (0.5 * inner * (1.0 + bend)).astype(BF16)
                slope_ref[t] = 0.5 * (1.0 + bend) + (0.5 * GELU_A) * inner * (
                    1.0 - bend * bend
                ) * (1.0 + (3.0 * GELU_B) * square)
                hidden_ref[t, at, :] = hidden
                branch_two = branch_two + dot_nn(hidden, all_down_ref[t].reshape(share, width))
            normed_two, factor_two = norm_forward(middle + branch_two)
            cot_dual, upstream = home(3), home(2)
            replace(2, normed_two * gain_two + bias_two)
            replace(1, home(1) + branch_one + branch_two)
            d_two = norm_backward(upstream, normed_two, factor_two, gain_two)
            norm_ref[2:3, :] += jnp.sum(upstream * normed_two, axis=0, keepdims=True)
            norm_ref[3:4, :] += jnp.sum(upstream, axis=0, keepdims=True)
            up_two = (d_two + cot_dual).astype(BF16)
            up_two_ref[:, at] = up_two.T
            grad_middle = d_two
            for t in range(tensors):
                grad_hidden = dot_nt(up_two, all_down_ref[t].reshape(share, width))
                grad_inner = (grad_hidden * slope_ref[t]).astype(BF16)
                grad_inner_ref[t, at, :] = grad_inner
                grad_middle = grad_middle + dot_nt(grad_inner, all_up_ref[t].reshape(width, share))
            d_one = norm_backward(grad_middle, normed_one, factor_one, gain_one)
            norm_ref[0:1, :] += jnp.sum(grad_middle * normed_one, axis=0, keepdims=True)
            norm_ref[1:2, :] += jnp.sum(grad_middle, axis=0, keepdims=True)
            for m, column in enumerate(taken):
                base_ref[column] = d_one[m * rows : (m + 1) * rows]
            up_one = (d_one + cot_dual).astype(BF16)
            up_one_ref[:, at] = up_one.T
            grad_mixed = dot_nt(up_one, all_out_ref[...].reshape(width, width)).astype(BF16)
            for m, place in enumerate(places):
                for h in range(owners):
                    slot = slot_of(place, h)
                    piece = grad_mixed[m * rows : (m + 1) * rows, h * lanes : (h + 1) * lanes]

                    @pl.when(slot < last)
                    def _():
                        stage_ref[slot, :, :lanes] = piece
                        do_copy(slot, partner_of(slot)).start()

                    @pl.when(slot == last)
                    def _():
                        do_ref[last] = piece

        norm_sum.begin()
        cut = (2,) * dp_bits + (width >> dp_bits,)

        @pl.loop(0, tensors)
        def _(t):
            g_down = dot_nn(up_two_ref[...], hidden_ref[t]).astype(BF16)
            g_down_ref[t] = g_down.reshape(cut + (share,))

        down_scatter.begin()
        every = (slice(None),) * (dp_bits + 1)

        @pl.loop(0, tensors)
        def _(t):
            g_up = dot_nn(middle_ref[...], grad_inner_ref[t]).astype(BF16)
            g_up_ref[(t,) + every + (slice(0, share),)] = g_up.reshape(cut + (share,))

        all_mixed = jnp.concatenate([mixed_at(place_of(n)) for n in range(columns)], axis=0)
        g_out = dot_nn(up_one_ref[...], all_mixed).astype(BF16)
        for t in range(tensors):
            g_up_ref[(t,) + every + (slice(share, share + shard),)] = g_out[
                :, t * shard : (t + 1) * shard
            ].reshape(cut + (shard,))
        up_scatter.begin()

    pl.run_scoped(
        forward_phase,
        pltpu.VMEM((tensors, tokens, share), BF16),
        pltpu.VMEM((tensors, GROUP * rows, share), F32),
        pltpu.VMEM((tensors, tokens, share), BF16),
        pltpu.VMEM((width, tokens), BF16),
        pltpu.VMEM((width, tokens), BF16),
        pltpu.VMEM((width, tokens), BF16),
    )

    def backward_phase(dot_ref, delta_ref, dq_ref, dk_ref, dv_ref, grads_ref):
        dq_ref[...] = jnp.zeros_like(dq_ref)
        dk_ref[...] = jnp.zeros_like(dk_ref)
        dv_ref[...] = jnp.zeros_like(dv_ref)

        def receive(slot):
            if slot < last:
                do_copy(slot, partner_of(slot)).wait()
            at = slice(slot * rows, (slot + 1) * rows)
            dot_ref[:, at] = do_ref[slot].T
            product = (do_ref[slot].astype(F32) * o_ref[slot]).T
            delta_ref[slot, :heads] = jnp.sum(product.reshape(heads, E, rows), axis=1)

        def advance(scatter, step):
            def run():
                scatter.advance(step)
                if scatter is up_scatter:
                    norm_sum.advance(step)

            return run

        counts = [
            count for wave in range(tensors) for count in (tensors - wave, last - wave) if count
        ]
        begins, done = [], 0
        for count in counts:
            for j in range(pairs):
                begins.append((done + count * j / pairs) / (tensors * tensors))
            done += count
        count = down_scatter.steps
        wishes = []
        for scatter, dues in ((down_scatter, DOWN_DUES), (up_scatter, UP_DUES)):
            wishes.append((dues[0], advance(scatter, 0)))
            for step in range(1, count):
                due = dues[1] + (dues[2] - dues[1]) * (step - 1) / max(count - 2, 1)
                wishes.append((due, advance(scatter, step)))
        wishes = [(next(n for n, at in enumerate(begins) if at >= wish), one) for wish, one in wishes]

        def block_of(number, q_slot, q_count, k_slot, k_count):
            at_q = slice(q_slot * rows, (q_slot + q_count) * rows)
            at_k = slice(k_slot * rows, (k_slot + k_count) * rows)

            @pl.loop(0, pairs)
            def _(j):
                for place, one in wishes:
                    if place // pairs == number:

                        @pl.when(j == place % pairs)
                        def _():
                            one()

                at = pl.ds(pl.multiple_of(j * 2 * E, 2 * E), 2 * E)
                key_marks = key_marks_ref[at_k, :]
                keys = jnp.concatenate([k_ref[at_k, at], key_marks], axis=1)
                values = jnp.concatenate([v_ref[at_k, at], key_marks], axis=1)
                query_marks = query_marks_ref[:, at_q]
                no_marks = jnp.zeros_like(query_marks)
                queries = q_ref[at_q, at]
                ups = do_ref[q_slot : q_slot + q_count, :, at].reshape(q_count * rows, 2 * E)
                sums = []
                for half in range(2):

                    def row_of(ref):
                        row = pl.ds(2 * j + half, 1)
                        slots = range(q_slot, q_slot + q_count)
                        return jnp.concatenate([ref[slot, row, :] for slot in slots], axis=1)

                    minus_lse = with_row(query_marks, row_of(lse_ref))
                    minus_delta = with_row(no_marks, row_of(delta_ref))
                    probs = jnp.exp(dot_nn(keys, with_marks(half_rows(qt_ref[at, at_q], half), minus_lse)))
                    pushed = dot_nn(values, with_marks(half_rows(dot_ref[at, at_q], half), minus_delta))
                    delta = (probs * pushed).astype(BF16)
                    at_head = pl.ds(pl.multiple_of((2 * j + half) * E, E), E)
                    dq_ref[at_head, at_q] += dot_nn(kt_ref[at_head, at_k], delta)
                    sums.append((dot_nn(delta, queries), dot_nn(probs.astype(BF16), ups)))
                low_half = lax.broadcasted_iota(jnp.int32, sums[0][0].shape, 1) < E
                dk_ref[at_k, at] += jnp.where(low_half, sums[0][0], sums[1][0])
                dv_ref[at_k, at] += jnp.where(low_half, sums[0][1], sums[1][1])

        for wave in range(tensors):
            if wave == 0:
                receive(0)
            block_of(2 * wave, wave, 1, wave, tensors - wave)
            if wave == 0:
                for slot in range(1, tensors):
                    receive(slot)
            if wave < last:
                block_of(2 * wave + 1, wave + 1, last - wave, wave, 1)
            at = slice(wave * rows, (wave + 1) * rows)
            grads = (
                (dq_ref[:, at] * 0.125).T.astype(BF16),
                dk_ref[at, :].astype(BF16),
                dv_ref[at, :].astype(BF16),
            )
            part = jnp.zeros((rows, width), F32)
            for i in range(3):
                grads_ref[i, at, :] = grads[i]
                part = part + dot_nn(grads[i], w_t(i))

            if wave < last:
                stage_ref[wave] = part.astype(BF16)
                input_copy(wave, partner_of(wave)).start()
            else:
                base_ref[me // owners] += part

        for i in range(3):
            g = dot_nn(xt_ref[...], grads_ref[i]).astype(BF16)
            for t in range(tensors // owners):
                g_qkv_ref[i, me_low * (tensors // owners) + t] = g[
                    :, t * shard : (t + 1) * shard
                ].reshape((2,) * dp_bits + (width >> dp_bits, shard))
            qkv_scatters[i].begin()
            if i:
                qkv_scatters[i - 1].advance(0)

    pl.run_scoped(
        backward_phase,
        pltpu.VMEM((lanes, length), BF16),
        pltpu.VMEM((tensors, max(heads, 8), rows), F32),
        pltpu.VMEM((lanes, length), F32),
        pltpu.VMEM((length, lanes), F32),
        pltpu.VMEM((length, lanes), F32),
        pltpu.VMEM((3, length, lanes), BF16),
    )


    def end_phase(turned_ref):
        stores = [
            pltpu.make_async_copy(turned_ref.at[n], ref, local_sem.at[n])
            for n, ref in enumerate((post_ref, dual_ref, grad_post_ref))
        ]

        def store(n):
            made = base_ref[...].astype(BF16) if n == 2 else home_ref[2 - n]
            turned_ref[n] = jnp.swapaxes(made, 0, 1)
            stores[n].start()

        def advance(step):
            for one in qkv_scatters:
                one.advance(step)

        store(0)
        qkv_scatters[2].advance(0)
        store(1)
        if dp_bits > 1:
            advance(1)
        if last > 1:
            x_copy(last - 1).wait_send()
        for slot in range(last):
            input_copy(slot, partner_of(slot)).wait()
            base_ref[partner_of(slot) // owners] += input_land_ref[slot].astype(F32)
        store(2)
        for step in range(2, dp_bits):
            advance(step)
        small = [
            pltpu.make_async_copy(small_refs[n], ref, local_sem.at[8 + n])
            for n, ref in enumerate((r_qkv_ref, r_down_ref, r_up_ref, r_norm_ref))
        ]
        small_refs[1][...] = down_scatter.result()
        small_refs[2][...] = up_scatter.result()
        count = width // (tensors << dp_bits)
        first = (lax.axis_index("dp") * tensors + me) * count
        small_refs[3][...] = pltpu.roll(norm_sum.result(), width - first, 1)[:, :128]
        start(small[1:])
        for i in range(3):
            small_refs[0][i] = qkv_scatters[i].result()
        small[0].start()
        for copy in small:
            copy.wait()
        for copy in stores:
            copy.wait()

    pl.run_scoped(end_phase, pltpu.VMEM((3, rows, columns, width), BF16))


def hand_over_kernel(*refs):
    sources, results = refs[:7], refs[7:]
    for n in range(3):
        results[n][...] = sources[n][...].astype(F32)

    @pl.when(pl.program_id(0) == 0)
    def _():
        grad_qkv, grad_down, grad_up_out, grad_norm = sources[3:]
        share = results[4].shape[1]
        results[3][...] = grad_qkv[...]
        results[4][...] = grad_down[...]
        results[5][...] = grad_up_out[:, :share]
        results[6][...] = grad_up_out[:, share:]
        for n in range(4):
            results[7 + n][...] = grad_norm[n : n + 1, : results[7 + n].shape[1]]


def body(
    x_post,
    x_dual,
    cot_post,
    cot_dual,
    segment_ids,
    w_qkv,
    w_out,
    w_up,
    w_down,
    gain_one,
    bias_one,
    gain_two,
    bias_two,
):
    tensors, devices = lax.axis_size("tensor"), lax.axis_size("dp")
    dp_bits = log2(devices)
    rows, columns, width = x_post.shape
    length = tensors * rows
    owners = tensors // columns
    lanes = width // owners
    share, shard = w_up.shape[1], w_out.shape[0]
    piece = width // devices
    heads = lanes // E
    me = lax.axis_index("tensor")
    def cut(array, dim):
        bits = min(dp_bits, log2(array.shape[dim] // 16))
        shape = array.shape[:dim] + (2,) * bits + (array.shape[dim] >> bits,) + array.shape[dim + 1 :]
        return array.reshape(shape)

    shards = [cut(w_out, 0), cut(w_up, 0), cut(w_down, 0)]
    qkv_shape = jax.eval_shape(lambda w: cut(jnp.swapaxes(w, 1, 2), 1), w_qkv).shape
    in_place = pl.BlockSpec(memory_space=pl.ANY)
    shape = jax.ShapeDtypeStruct
    bits = (2,) * dp_bits

    def lands(lane_count, *lead):
        return [
            pltpu.VMEM(lead + (tensors,) + bits[: dp_bits - 1 - step] + (piece, lane_count), BF16)
            for step in range(dp_bits)
        ]

    small_out = (
        shape((3, piece, shard), F32),
        shape((piece, share), F32),
        shape((piece, share + shard), F32),
        shape((8, 128), F32),
    )
    cuts = [len(qkv_shape) - 3] + [len(one.shape) - 2 for one in shards]
    links = link_counts(tensors, dp_bits, cuts)
    layer = pl.pallas_call(
        functools.partial(layer_kernel, dp_bits, columns),
        out_shape=(
            shape((rows, columns, width), BF16),
            shape((rows, columns, width), BF16),
            shape((rows, columns, width), BF16),
        )
        + small_out,
        in_specs=[in_place] * 13,
        out_specs=(in_place,) * 7,
        scratch_shapes=[
            pltpu.VMEM((4, columns, rows, width), BF16),
            pltpu.VMEM((tensors, rows, width), BF16),
            pltpu.VMEM((tensors,) + qkv_shape, BF16),
        ]
        + [pltpu.VMEM((tensors,) + one.shape, BF16) for one in shards]
        + [
            pltpu.VMEM((tensors, rows, lanes), BF16),
            pltpu.VMEM((tensors, rows, lanes), BF16),
            pltpu.VMEM((tensors - 1, rows, width), BF16),
            pltpu.VMEM((tensors,) + bits + (piece, share), BF16),
            pltpu.VMEM((tensors,) + bits + (piece, share + shard), BF16),
            pltpu.VMEM((3, tensors) + bits + (piece, shard), BF16),
            lands(share),
            pltpu.VMEM((tensors - 1, piece, share), BF16),
            lands(share + shard),
            pltpu.VMEM((tensors - 1, piece, share + shard), BF16),
            lands(shard, 3),
            pltpu.VMEM((3, tensors - 1, piece, shard), BF16),
            pltpu.VMEM((8, width), F32),
            pltpu.VMEM((dp_bits + tensors - 1, 8, width), F32),
            pltpu.VMEM((length, lanes), BF16),
            pltpu.VMEM((length, lanes), BF16),
            pltpu.VMEM((length, lanes), BF16),
            pltpu.VMEM((lanes, length), BF16),
            pltpu.VMEM((lanes, length), BF16),
            pltpu.VMEM((width, length), BF16),
            pltpu.VMEM((tensors, rows, lanes), F32),
            pltpu.VMEM((tensors, max(heads, 8), rows), F32),
            pltpu.VMEM((columns, rows, width), F32),
            pltpu.VMEM((tensors - 1, rows, width), BF16),
            pltpu.VMEM((length, 2 * E), BF16),
            pltpu.VMEM((2 * E, length), BF16),
            pltpu.VMEM((2 * E, length), BF16),
            pltpu.VMEM((length, 2 * E), BF16),
            pltpu.VMEM((rows, 2 * E), F32),
            pltpu.VMEM((max(tensors, 8), rows), F32),
            pltpu.VMEM((8, length), F32),
            pltpu.VMEM((columns, length), jnp.int32),
            pltpu.VMEM((8, width), F32),
            [pltpu.VMEM(one.shape, F32) for one in small_out],
            pltpu.SemaphoreType.DMA((links[1],)),
            pltpu.SemaphoreType.DMA((links[0],)),
            pltpu.SemaphoreType.DMA((16,)),
        ],
        compiler_params=pltpu.CompilerParams(
            vmem_limit_bytes=VMEM_BYTES, collective_id=0, has_side_effects=True
        ),
        name="layer",
    )
    made = layer(
        segment_ids.T,
        x_post,
        x_dual,
        cot_post,
        cot_dual,
        w_qkv,
        *shards,
        *(one.reshape(1, width) for one in (gain_one, bias_one, gain_two, bias_two)),
    )
    count = width // (tensors * devices)
    blocks = 2
    block_spec = pl.BlockSpec((rows // blocks, columns, width), lambda i: (i, 0, 0))

    def whole_spec(one):
        return pl.BlockSpec(one.shape, lambda i: (0,) * len(one.shape))

    small = (
        shape((3, piece, shard), F32),
        shape((piece, share), F32),
        shape((piece, share), F32),
        shape((piece, shard), F32),
    ) + (shape((1, count), F32),) * 4
    results = pl.pallas_call(
        hand_over_kernel,
        out_shape=tuple(shape(one.shape, F32) for one in made[:3]) + small,
        grid=(blocks,),
        in_specs=[block_spec] * 3 + [whole_spec(one) for one in made[3:]],
        out_specs=(block_spec,) * 3 + tuple(whole_spec(one) for one in small),
        name="hand_over",
    )(*made)
    post_out, dual_out, grad_post, g_qkv, g_down, g_up, g_out = results[:7]
    norms = tuple(one.reshape(count) for one in results[7:])
    return (post_out, dual_out, grad_post, g_qkv, g_out.T, g_up, g_down.T) + norms


def solution(mesh):
    placed = (
        P("tensor", "dp", None),
        P("tensor", "dp", None),
        P("tensor", "dp", None),
        P("tensor", "dp", None),
        P(None, "dp"),
        P(None, None, "tensor"),
        P("tensor", None),
        P(None, "tensor"),
        P("tensor", None),
        P(),
        P(),
        P(),
        P(),
    )
    return jax.shard_map(
        body,
        mesh=mesh,
        in_specs=placed,
        out_specs=(
            P("tensor", "dp", None),
            P("tensor", "dp", None),
            P("tensor", "dp", None),
            P(None, "dp", "tensor"),
            P("tensor", "dp"),
            P("dp", "tensor"),
            P("tensor", "dp"),
            P(("dp", "tensor")),
            P(("dp", "tensor")),
            P(("dp", "tensor")),
            P(("dp", "tensor")),
        ),
        check_vma=False,
    )
```

```python
import functools
import itertools

import jax
import jax.numpy as jnp
from jax import lax
from jax.experimental import pallas as pl
from jax.experimental.pallas import tpu as pltpu
from jax.sharding import PartitionSpec as P

E = 64
EPSILON = 1e-05
NEGATIVE = -1e30
DOCUMENTS = 4
DOWN_DUES = (0.06, 0.35, 0.75)
UP_DUES = (0.10, 0.5, 0.9)
GATHER_DUE, GATHER_LEVEL, GATHER_STEP = 1, 4, 4
NEAR_DUE = 1
CHUNKS = 2
GROUP = 1
PARTS = 3
GELU_A = 0.7978845608028654
GELU_B = 0.044715
F32 = jnp.float32
BF16 = jnp.bfloat16
VMEM_BYTES = 63 * 1024 * 1024


def dot_nn(a, b):
    return lax.dot_general(a, b, (((1,), (0,)), ((), ())), preferred_element_type=F32)


def dot_nt(a, b):
    return lax.dot_general(a, b, (((1,), (1,)), ((), ())), preferred_element_type=F32)


def dot_tn(a, b):
    return lax.dot_general(a, b, (((0,), (0,)), ((), ())), preferred_element_type=F32)


def row_mean(a):
    return jnp.mean(a, axis=-1, keepdims=True)


def norm_forward(total):
    centre = total - row_mean(total)
    factor = lax.rsqrt(row_mean(centre * centre) + EPSILON)
    return centre * factor, factor


def norm_backward(upstream, normed, factor, gain):
    scaled = upstream * gain
    inner = scaled - row_mean(scaled) - normed * row_mean(scaled * normed)
    return factor * inner


def with_marks(block, marks):
    return jnp.concatenate([block, marks], axis=0)


def with_row(marks, row):
    line = lax.broadcasted_iota(jnp.int32, (16, row.shape[1]), 0)
    top = marks[:16].astype(F32)
    rest = -row
    for part in range(PARTS):
        term = rest.astype(BF16).astype(F32)
        rest = rest - term
        top = jnp.where(line == DOCUMENTS + part, term, top)
    return jnp.concatenate([top.astype(BF16), marks[16:]], axis=0)


def half_rows(block, half):
    zeros = jnp.zeros((E, block.shape[1]), block.dtype)
    if half == 0:
        return jnp.concatenate([block[:E], zeros], axis=0)
    return jnp.concatenate([zeros, block[E:]], axis=0)


MESH = pl.DeviceIdType.MESH


def bit_of(index, bit):
    return (index // (1 << bit)) % 2


def flip(index, mask):
    for bit in range(mask.bit_length()):
        if (mask >> bit) % 2:
            index = index + (1 - 2 * bit_of(index, bit)) * (1 << bit)
    return index


def log2(count):
    return count.bit_length() - 1


class Links:
    def __init__(self, send_sem, recv_sem):
        self.send_sem, self.recv_sem, self.used, self.pooled = send_sem, recv_sem, 0, 0

    def take(self, count):
        first = self.used
        self.used += count
        assert self.used <= self.recv_sem.shape[0]
        return first

    def pool(self, count):
        first = self.pooled
        self.pooled += count
        assert self.pooled <= self.send_sem.shape[0]
        return first

    def copy(self, src, dst, slot, send_slot, axis, partner):
        return pltpu.make_async_remote_copy(
            src_ref=src,
            dst_ref=dst,
            send_sem=self.send_sem.at[send_slot],
            recv_sem=self.recv_sem.at[slot],
            device_id={axis: partner},
            device_id_type=MESH,
        )

    def stages(self, stages):
        first = self.pool(max(len(stage) for stage in stages))
        return [
            [
                self.copy(src, dst, self.take(1), first + n, axis, partner)
                for n, (src, dst, axis, partner) in enumerate(stage)
            ]
            for stage in stages
        ]


def link_counts(tensors, dp_bits, cuts):
    others = tensors - 1
    levels = [0] * log2(tensors)
    for mask in range(2, tensors):
        levels[mask.bit_count() - 1] += 1
    receive = 4 * others + others * (1 + 3 * cuts[0]) + sum(others * (1 + cut) for cut in cuts[1:])
    receive += 5 * (1 + 2 * (dp_bits - 1) + others) + dp_bits + others
    send = 2 * others + 3 * others + 3 + 3 * sum(levels)
    send += 2 * max(2, tensors // 2) + 3 * max(2, others) + others
    return receive, send


def start(copies):
    for copy in copies:
        copy.start()


def finish(copies):
    for copy in copies:
        copy.wait_recv()
        copy.wait_send()


def greet(dp_bits, tensors):
    dp, me = lax.axis_index("dp"), lax.axis_index("tensor")
    barrier = pltpu.get_barrier_semaphore()
    for bit in range(dp_bits):
        pl.semaphore_signal(barrier, inc=1, device_id={"dp": flip(dp, 1 << bit)}, device_id_type=MESH)
    for step in range(1, tensors):
        pl.semaphore_signal(
            barrier, inc=1, device_id={"tensor": (me + step) % tensors}, device_id_type=MESH
        )


def greeted(dp_bits, tensors):
    pl.semaphore_wait(pltpu.get_barrier_semaphore(), dp_bits + tensors - 1)


class WeightGather:
    def __init__(self, src, dst, lead, cut_bits, dp_bits, first, direct=False):
        tensors = dst.shape[0]
        dp, me = lax.axis_index("dp"), lax.axis_index("tensor")
        bits = list(range(dp_bits - 1, dp_bits - 1 - cut_bits, -1))
        if src is None:
            src = dst.at[me]
        self.src, self.dst, self.own = src, dst, me
        inner = [()] if lead == 0 else [(i,) for i in range(dst.shape[1])]
        piece = (slice(None),) * lead + tuple(bit_of(dp, bit) for bit in bits)
        low = [bit for bit in bits if bit == 0]
        high = [bit for bit in bits if bit != 0]
        orders = (high[::-1] + low, high + low)
        count = first
        self.stages = {}
        for mask in range(1, tensors):
            near = mask if direct else mask & -mask
            block = flip(me, mask - near)
            stages = [[] for _ in range(1 + dp_bits)]
            stages[0].append(
                (
                    dst.at[(block,) + piece] if mask != near else src.at[piece],
                    dst.at[(block,) + piece],
                    "tensor",
                    flip(me, near),
                )
            )
            source = flip(me, mask)
            for i in inner:
                order = orders[count % 2]
                count += 1
                for phase, bit in enumerate(order):
                    done = order[:phase]
                    region = (source,) + i + tuple(
                        slice(None) if other in done else bit_of(dp, other) for other in bits
                    )
                    stages[1 + phase].append(
                        (dst.at[region], dst.at[region], "dp", flip(dp, 1 << bit))
                    )
            self.stages[mask] = stages

    def own_copy(self, sem):
        return pltpu.make_async_copy(self.src, self.dst.at[self.own], sem)


class Stages:
    def __init__(self, links, stages):
        self.copies = links.stages(stages)
        self.count = len(stages)

    def begin(self):
        start(self.copies[0])

    def advance(self, stage):
        finish(self.copies[stage])
        if stage + 1 < self.count:
            start(self.copies[stage + 1])


def shard_stages(weights, masks):
    count = len(weights[0].stages[masks[0]])
    return [
        [copy for one in weights for mask in masks for copy in one.stages[mask][stage]]
        for stage in range(count)
    ]


class GradScatter:
    def __init__(self, links, grad, lands, across, direct):
        self.links, self.grad, self.lands, self.across = links, grad, lands, across
        self.tensors = grad.shape[0]
        self.dp, self.me = lax.axis_index("dp"), lax.axis_index("tensor")
        dp_bits = len(lands)
        high = list(range(dp_bits - 1, 0, -1))
        middle = self.tensors // 2
        copies = [
            [
                (
                    grad.at[(slice(None),) * dp_bits + (1 - bit_of(self.dp, 0),)],
                    lands[0],
                    "dp",
                    flip(self.dp, 1),
                )
            ]
        ]
        sums = [[(0, self.tensors, grad, dp_bits - 1, bit_of(self.dp, 0), lands[0])]]
        for step in range(1, dp_bits):
            copies.append([])
            sums.append([])
        for begin, order in ((0, high[::-1]), (middle, high)):
            left = list(high)
            for step, bit in enumerate(order, 1):
                place = left.index(bit)
                left.remove(bit)
                part = pl.ds(begin, middle)
                index = (part,) + (slice(None),) * place + (1 - bit_of(self.dp, bit),)
                copies[step].append(
                    (
                        lands[step - 1].at[index],
                        lands[step].at[part],
                        "dp",
                        flip(self.dp, 1 << bit),
                    )
                )
                sums[step].append(
                    (begin, middle, lands[step - 1], place, bit_of(self.dp, bit), lands[step])
                )
        place = 0
        self.joins = []
        for bit in range(0 if direct else log2(self.tensors)):
            step, found, joins = 1 << bit, [], []
            for high in range(self.tensors >> (bit + 1)):
                mask = high * 2 * step
                found.append(
                    (
                        lands[-1].at[flip(self.me, mask + step)],
                        across.at[place],
                        "tensor",
                        flip(self.me, step),
                    )
                )
                joins.append((mask, place))
                place += 1
            copies.append(found)
            self.joins.append(joins)
        if direct:
            copies.append(
                [
                    (
                        lands[-1].at[flip(self.me, step)],
                        across.at[step - 1],
                        "tensor",
                        flip(self.me, step),
                    )
                    for step in range(1, self.tensors)
                ]
            )
            self.joins = [[(0, step) for step in range(self.tensors - 1)]]
        self.copies = links.stages(copies)
        self.sums = sums + [[] for _ in self.joins[1:]]
        self.steps = len(copies) - 1

    def begin(self):
        start(self.copies[0])

    def advance(self, step):
        finish(self.copies[step])
        for first, count, source, place, own, land in self.sums[step]:

            @pl.loop(first, first + count)
            def _(t):
                for spot in itertools.product((0, 1), repeat=len(land.shape) - 3):
                    whole = (t,) + spot[:place] + (own,) + spot[place:]
                    here = (t,) + spot
                    land[here] = land[here] + source[whole]

        if step >= len(self.lands):
            for mask, place in self.joins[step - len(self.lands)]:
                spot = flip(self.me, mask)
                total = self.lands[-1][spot].astype(F32) + self.across[place].astype(F32)
                self.lands[-1][spot] = total.astype(BF16)
        start(self.copies[step + 1])

    def result(self):
        finish(self.copies[-1])
        total = self.lands[-1][self.me].astype(F32)
        for _, place in self.joins[-1]:
            total = total + self.across[place].astype(F32)
        return total


class NormSum:
    def __init__(self, links, total, land, dp_bits, tensors):
        dp, me = lax.axis_index("dp"), lax.axis_index("tensor")
        self.total, self.land = total, land
        copies = [
            [(total, land.at[bit], "dp", flip(dp, 1 << bit))] for bit in range(dp_bits)
        ]
        copies.append(
            [
                (total, land.at[dp_bits + step - 1], "tensor", flip(me, step))
                for step in range(1, tensors)
            ]
        )
        self.copies = links.stages(copies)

    def begin(self):
        start(self.copies[0])

    def advance(self, step):
        if step + 1 < len(self.copies):
            finish(self.copies[step])
            self.total[...] += self.land[step]
            start(self.copies[step + 1])

    def result(self):
        finish(self.copies[-1])
        total = self.total[...]
        for step in range(len(self.copies) - 1, self.land.shape[0]):
            total = total + self.land[step]
        return total


def layer_kernel(
    dp_bits,
    columns,
    seg_ref,
    x_ref,
    dual_in_ref,
    cot_post_ref,
    cot_dual_ref,
    w_qkv_ref,
    w_out_ref,
    w_up_ref,
    w_down_ref,
    gain_one_ref,
    bias_one_ref,
    gain_two_ref,
    bias_two_ref,
    post_ref,
    dual_ref,
    grad_post_ref,
    r_qkv_ref,
    r_down_ref,
    r_up_ref,
    r_norm_ref,
    home_ref,
    x_col_ref,
    all_qkv_ref,
    all_out_ref,
    all_up_ref,
    all_down_ref,
    mixed_ref,
    do_ref,
    input_land_ref,
    g_down_ref,
    g_up_ref,
    g_qkv_ref,
    down_lands,
    down_across_ref,
    up_lands,
    up_across_ref,
    qkv_lands,
    qkv_across_ref,
    norm_ref,
    norm_land_ref,
    q_ref,
    k_ref,
    v_ref,
    qt_ref,
    kt_ref,
    xt_ref,
    o_ref,
    lse_ref,
    base_ref,
    stage_ref,
    key_marks_ref,
    key_marks_t_ref,
    query_marks_ref,
    query_marks_n_ref,
    lse_columns_ref,
    own_seg_ref,
    seg_line_ref,
    seg_in_ref,
    norms_ref,
    small_refs,
    send_sem,
    recv_sem,
    local_sem,
):
    tensors, rows, width = x_col_ref.shape
    owners = tensors // columns
    lanes = mixed_ref.shape[-1]
    heads = lanes // E
    pairs = heads // 2
    share = all_up_ref.shape[-1]
    shard = width // tensors
    last = tensors - 1
    length = tensors * rows
    tokens = columns * rows
    tensor_bits = log2(tensors)
    me = lax.axis_index("tensor")
    me_low = me % owners
    links = Links(send_sem, recv_sem)

    exchange_pool = links.pool(last)

    def slot_copies(sources, land):
        first = links.take(last)

        def one(slot, partner):
            source = sources.at[slot, :, pl.ds(0, land.shape[-1])]
            return links.copy(
                source, land.at[slot], first + slot, exchange_pool + slot, "tensor", partner
            )

        return one

    def partner_of(slot):
        mask = last - slot
        index = me
        for bit in range(log2(tensors)):
            index = index + bit_of(mask, bit) * (1 - 2 * bit_of(me, bit)) * (1 << bit)
        return index

    def gather(src, dst, lead, first, direct=False):
        return WeightGather(src, dst, lead, len(dst.shape) - lead - 3, dp_bits, first, direct)

    masks = list(range(1, tensors))
    levels = [[mask for mask in masks if mask.bit_count() == n + 1] for n in range(tensor_bits)]
    qkv = Stages(links, shard_stages([gather(None, all_qkv_ref, 1, 0, True)], masks))
    ffn = [
        gather(w_out_ref, all_out_ref, 0, 0),
        gather(w_up_ref, all_up_ref, 0, 0),
        gather(w_down_ref, all_down_ref, 0, 1),
    ]
    near_ffn = Stages(links, shard_stages(ffn, [1]))
    far_ffn = [
        Stages(links, shard_stages(ffn, [mask for mask in level if mask != 1])) for level in levels
    ]
    x_pool = links.pool(last)
    x_first = links.take(last)

    def x_copy(slot):
        partner = partner_of(slot)
        return links.copy(
            home_ref.at[0, partner // owners],
            x_col_ref.at[slot],
            x_first + slot,
            x_pool + slot,
            "tensor",
            partner,
        )

    mixed_copy = slot_copies(stage_ref, mixed_ref)
    do_copy = slot_copies(stage_ref, do_ref)
    input_copy = slot_copies(stage_ref, input_land_ref)
    down_scatter = GradScatter(links, g_down_ref, down_lands, down_across_ref, False)
    up_scatter = GradScatter(links, g_up_ref, up_lands, up_across_ref, False)
    qkv_scatters = [
        GradScatter(links, g_qkv_ref.at[i], [land.at[i] for land in qkv_lands], qkv_across_ref.at[i], True)
        for i in range(3)
    ]
    norm_sum = NormSum(links, norm_ref, norm_land_ref, dp_bits, tensors)

    def next_x(slot):
        x_copy(slot).wait_send()

    shard_copies = [one.own_copy(local_sem.at[5 + i]) for i, one in enumerate(ffn)]

    def start_phase(raw_ref, raw_qkv_ref):
        loads = [
            pltpu.make_async_copy(ref, raw_ref.at[n], local_sem.at[n])
            for n, ref in enumerate((x_ref, dual_in_ref, cot_post_ref, cot_dual_ref))
        ]
        load_qkv = pltpu.make_async_copy(w_qkv_ref, raw_qkv_ref, local_sem.at[4])
        small_loads = [pltpu.make_async_copy(seg_ref, seg_in_ref, local_sem.at[8])] + [
            pltpu.make_async_copy(ref, norms_ref.at[pl.ds(n, 1)], local_sem.at[9 + n])
            for n, ref in enumerate((gain_one_ref, bias_one_ref, gain_two_ref, bias_two_ref))
        ]
        greet(dp_bits, tensors)
        start(loads[:1] + [load_qkv] + loads[1:] + small_loads + shard_copies)
        load_qkv.wait()
        for i in range(3):
            all_qkv_ref[me, i] = raw_qkv_ref[i].T.reshape(all_qkv_ref.shape[2:])
        loads[0].wait()
        home_ref[0] = jnp.swapaxes(raw_ref[0], 0, 1)
        greeted(dp_bits, tensors)
        qkv.begin()
        for slot in ([last - 1] if last > 1 else []) + list(range(max(last - 1, 1))):
            x_copy(slot).start()
        x_col_ref[last] = home_ref[0, me // owners]
        norm_ref[...] = jnp.zeros_like(norm_ref)
        lse_columns_ref[...] = jnp.zeros_like(lse_columns_ref)
        own_seg_ref[...] = jnp.zeros_like(own_seg_ref)
        for copy in small_loads:
            copy.wait()
        seg_row = lax.broadcasted_iota(jnp.int32, seg_in_ref.shape, 0)
        own_seg = jnp.where(seg_row == me // owners, seg_in_ref[...], 0).astype(F32)
        seg_line_ref[0:1, :] = jnp.sum(own_seg, axis=0, keepdims=True)
        for slot in range(tensors):
            spot = pl.ds(pl.multiple_of(partner_of(slot) * rows, rows), rows)
            own_seg_ref[slot : slot + 1, :] = seg_line_ref[0:1, spot]
        seg_columns = own_seg_ref[...].T
        for slot in range(tensors):
            at = slice(slot * rows, (slot + 1) * rows)
            lane = lax.broadcasted_iota(jnp.int32, (rows, 2 * E), 1)
            same = seg_columns[:, slot : slot + 1] == lane.astype(F32)
            marks = jnp.where(lane < DOCUMENTS, same.astype(F32), 0.0)
            ones = jnp.where((lane >= DOCUMENTS) & (lane < DOCUMENTS + PARTS), 1.0, marks)
            key_marks_ref[at, :] = ones.astype(BF16)
            key_marks_t_ref[:, at] = ones.T.astype(BF16)
            line = lax.broadcasted_iota(jnp.int32, (2 * E, rows), 0)
            other = own_seg_ref[slot : slot + 1, :] != line.astype(F32)
            bias = jnp.where((line < DOCUMENTS) & other, NEGATIVE, 0.0)
            query_marks_ref[:, at] = bias.astype(BF16)
            query_marks_n_ref[at, :] = bias.T.astype(BF16)
        if owners > 1:
            g_qkv_ref[...] = jnp.zeros_like(g_qkv_ref)
        turned = 1
        for stage in range(qkv.count):
            if turned < 4:
                loads[turned].wait()
                home_ref[turned] = jnp.swapaxes(raw_ref[turned], 0, 1)
                turned += 1
            if stage == qkv.count - 1:
                next_x(0)
                near_ffn.begin()
                far_ffn[0].begin()
            qkv.advance(stage)
        for copy in shard_copies:
            copy.wait()

    pl.run_scoped(
        start_phase,
        pltpu.VMEM((4, rows, columns, width), BF16),
        pltpu.VMEM(w_qkv_ref.shape, BF16),
    )
    own_shards = pl.ds(me_low * (tensors // owners), tensors // owners)

    def w_t(i):
        return all_qkv_ref[own_shards, i].reshape(lanes, width)

    def forward_phase(
        hidden_ref,
        slope_ref,
        grad_inner_ref,
        up_two_ref,
        middle_ref,
        up_one_ref,
    ):
        order = [last, last - 1] + list(range(last - 1)) if last > 1 else [last, 0]
        for turn, slot in enumerate(order):
            if slot < last:
                x_copy(slot).wait_recv()
            if 0 < slot < last - 1:
                next_x(slot)
            block = x_col_ref[slot]
            at = slice(slot * rows, (slot + 1) * rows)
            q_ref[at, :] = dot_nt(block, w_t(0)).astype(BF16) * jnp.bfloat16(0.125)
            k_ref[at, :] = dot_nt(block, w_t(1)).astype(BF16)
            v_ref[at, :] = dot_nt(block, w_t(2)).astype(BF16)
            qt_ref[:, at] = dot_nt(w_t(0), block).astype(BF16) * jnp.bfloat16(0.125)
            kt_ref[:, at] = dot_nt(w_t(1), block).astype(BF16)
            xt_ref[:, at] = block.T
            if turn == min(2, last):
                near_ffn.advance(0)

        def gather_step(level, stage):
            def run():
                far_ffn[level].advance(stage)
                if stage == 0 and level + 1 < len(far_ffn):
                    far_ffn[level + 1].begin()

            return run

        steps = tensors * pairs
        def near_step(stage):
            return lambda: near_ffn.advance(stage)

        near_events = [
            (NEAR_DUE + GATHER_STEP * (stage - 1), near_step(stage))
            for stage in range(1, near_ffn.count)
        ]
        gather_events = sorted(
            (
                (GATHER_DUE + GATHER_LEVEL * level + GATHER_STEP * stage, level, stage)
                for level in range(tensor_bits)
                for stage in range(1 + dp_bits)
            ),
        )
        late = [gather_step(*which) for due, *which in gather_events if due >= 16]
        gather_events = [
            (due * steps // 16, gather_step(*which)) for due, *which in gather_events if due < 16
        ] + [(due * steps // 16, one) for due, one in near_events]

        @pl.loop(0, tensors)
        def _(slot):
            at_rows = pl.ds(pl.multiple_of(slot * rows, rows), rows)
            @pl.loop(0, pairs)
            def _(j):
                for due, one in gather_events:

                    @pl.when(slot * pairs + j == due)
                    def _():
                        one()

                at = pl.ds(pl.multiple_of(j * 2 * E, 2 * E), 2 * E)
                keys = with_marks(kt_ref[at, :], key_marks_t_ref[...])
                values = jnp.concatenate([v_ref[:, at], key_marks_ref[...]], axis=1)
                queries = q_ref[at_rows, at]
                marks = query_marks_n_ref[at_rows, :]
                lane = lax.broadcasted_iota(jnp.int32, queries.shape, 1)
                results = []
                for half in range(2):
                    own = (lane < E) if half == 0 else (lane >= E)
                    own_queries = jnp.where(own, queries, jnp.zeros_like(queries))
                    marked = jnp.concatenate([own_queries, marks], axis=1)
                    tops, sums = [], []
                    part = rows // CHUNKS
                    for n in range(CHUNKS):
                        scores = dot_nn(marked[n * part : (n + 1) * part], keys)
                        tops.append(jnp.max(scores, axis=1, keepdims=True))
                        sums.append(dot_nn(jnp.exp(scores - tops[-1]).astype(BF16), values))
                    top, result = jnp.concatenate(tops), jnp.concatenate(sums)
                    denom = result[:, 2 * E + DOCUMENTS : 2 * E + DOCUMENTS + 1]
                    results.append(result[:, : 2 * E] * (1.0 / denom))
                    lse = top + jnp.log(denom)
                    lse_columns_ref[...] = jnp.where(
                        lane == 2 * j + half, lse, lse_columns_ref[...]
                    )
                block = jnp.where(lane < E, results[0], results[1])
                o_ref[slot, :, at] = block

                @pl.when(slot < last)
                def _():
                    stage_ref[slot, :, at] = block.astype(BF16)

                @pl.when(slot == last)
                def _():
                    mixed_ref[last, :, at] = block.astype(BF16)

            lse_ref[slot] = lse_columns_ref[...].T[: lse_ref.shape[1]]

            @pl.when(slot < last)
            def _():
                mixed_copy(slot, partner_of(slot)).start()

        for one in late:
            one()

        gain_one, bias_one = norms_ref[0:1, :], norms_ref[1:2, :]
        gain_two, bias_two = norms_ref[2:3, :], norms_ref[3:4, :]

        def place_of(turn):
            first, final = 1 - (turn + columns - 1) // columns, (turn + 1) // columns
            return turn + 1 - first - (columns - 1) * final

        def slot_of(place, h):
            return last - owners * (columns - 1 - place) - flip(me_low, h)

        def mixed_at(place):
            return jnp.concatenate([mixed_ref[slot_of(place, h)] for h in range(owners)], axis=1)

        group = GROUP if columns % GROUP == 0 else 1

        @pl.loop(0, columns // group)
        def _(turn):
            places = [place_of(turn * group + n) for n in range(group)]
            taken = [partner_of(owners * place) // owners for place in places]
            for place in places:
                for r in range(owners):

                    @pl.when(owners * place + r < last)
                    def _():
                        mixed_copy(owners * place + r, partner_of(owners * place + r)).wait()

            def home(n):
                return jnp.concatenate([home_ref[n, column] for column in taken]).astype(F32)

            def replace(n, value):
                for m, column in enumerate(taken):
                    home_ref[n, column] = value[m * rows : (m + 1) * rows].astype(BF16)

            mixed = jnp.concatenate([mixed_at(place) for place in places])
            at = pl.ds(pl.multiple_of(turn * group * rows, group * rows), group * rows)
            branch_one = dot_nn(mixed, all_out_ref[...].reshape(width, width))
            normed_one, factor_one = norm_forward(home(0) + branch_one)
            middle = normed_one * gain_one + bias_one
            middle_low = middle.astype(BF16)
            middle_ref[:, at] = middle_low.T
            branch_two = jnp.zeros((group * rows, width), F32)
            for t in range(tensors):
                inner = dot_nn(middle_low, all_up_ref[t].reshape(width, share))
                square = inner * inner
                bend = jnp.tanh(GELU_A * (inner + GELU_B * (square * inner)))
                hidden = (0.5 * inner * (1.0 + bend)).astype(BF16)
                slope_ref[t] = 0.5 * (1.0 + bend) + (0.5 * GELU_A) * inner * (
                    1.0 - bend * bend
                ) * (1.0 + (3.0 * GELU_B) * square)
                hidden_ref[t, at, :] = hidden
                branch_two = branch_two + dot_nn(hidden, all_down_ref[t].reshape(share, width))
            normed_two, factor_two = norm_forward(middle + branch_two)
            cot_dual, upstream = home(3), home(2)
            replace(2, normed_two * gain_two + bias_two)
            replace(1, home(1) + branch_one + branch_two)
            d_two = norm_backward(upstream, normed_two, factor_two, gain_two)
            norm_ref[2:3, :] += jnp.sum(upstream * normed_two, axis=0, keepdims=True)
            norm_ref[3:4, :] += jnp.sum(upstream, axis=0, keepdims=True)
            up_two = (d_two + cot_dual).astype(BF16)
            up_two_ref[:, at] = up_two.T
            grad_middle = d_two
            for t in range(tensors):
                grad_hidden = dot_nt(up_two, all_down_ref[t].reshape(share, width))
                grad_inner = (grad_hidden * slope_ref[t]).astype(BF16)
                grad_inner_ref[t, at, :] = grad_inner
                grad_middle = grad_middle + dot_nt(grad_inner, all_up_ref[t].reshape(width, share))
            d_one = norm_backward(grad_middle, normed_one, factor_one, gain_one)
            norm_ref[0:1, :] += jnp.sum(grad_middle * normed_one, axis=0, keepdims=True)
            norm_ref[1:2, :] += jnp.sum(grad_middle, axis=0, keepdims=True)
            for m, column in enumerate(taken):
                base_ref[column] = d_one[m * rows : (m + 1) * rows]
            up_one = (d_one + cot_dual).astype(BF16)
            up_one_ref[:, at] = up_one.T
            grad_mixed = dot_nt(up_one, all_out_ref[...].reshape(width, width)).astype(BF16)
            for m, place in enumerate(places):
                for h in range(owners):
                    slot = slot_of(place, h)
                    piece = grad_mixed[m * rows : (m + 1) * rows, h * lanes : (h + 1) * lanes]

                    @pl.when(slot < last)
                    def _():
                        stage_ref[slot, :, :lanes] = piece
                        do_copy(slot, partner_of(slot)).start()

                    @pl.when(slot == last)
                    def _():
                        do_ref[last] = piece

        norm_sum.begin()
        cut = (2,) * dp_bits + (width >> dp_bits,)

        @pl.loop(0, tensors)
        def _(t):
            g_down = dot_nn(up_two_ref[...], hidden_ref[t]).astype(BF16)
            g_down_ref[t] = g_down.reshape(cut + (share,))

        down_scatter.begin()
        every = (slice(None),) * (dp_bits + 1)

        @pl.loop(0, tensors)
        def _(t):
            g_up = dot_nn(middle_ref[...], grad_inner_ref[t]).astype(BF16)
            g_up_ref[(t,) + every + (slice(0, share),)] = g_up.reshape(cut + (share,))

        all_mixed = jnp.concatenate([mixed_at(place_of(n)) for n in range(columns)], axis=0)
        g_out = dot_nn(up_one_ref[...], all_mixed).astype(BF16)
        for t in range(tensors):
            g_up_ref[(t,) + every + (slice(share, share + shard),)] = g_out[
                :, t * shard : (t + 1) * shard
            ].reshape(cut + (shard,))
        up_scatter.begin()

    pl.run_scoped(
        forward_phase,
        pltpu.VMEM((tensors, tokens, share), BF16),
        pltpu.VMEM((tensors, GROUP * rows, share), F32),
        pltpu.VMEM((tensors, tokens, share), BF16),
        pltpu.VMEM((width, tokens), BF16),
        pltpu.VMEM((width, tokens), BF16),
        pltpu.VMEM((width, tokens), BF16),
    )

    def backward_phase(dot_ref, delta_ref, dq_ref, dk_ref, dv_ref, grads_ref):
        dq_ref[...] = jnp.zeros_like(dq_ref)
        dk_ref[...] = jnp.zeros_like(dk_ref)
        dv_ref[...] = jnp.zeros_like(dv_ref)

        def receive(slot):
            if slot < last:
                do_copy(slot, partner_of(slot)).wait()
            at = slice(slot * rows, (slot + 1) * rows)
            dot_ref[:, at] = do_ref[slot].T
            product = (do_ref[slot].astype(F32) * o_ref[slot]).T
            delta_ref[slot, :heads] = jnp.sum(product.reshape(heads, E, rows), axis=1)

        def advance(scatter, step):
            def run():
                scatter.advance(step)
                if scatter is up_scatter:
                    norm_sum.advance(step)

            return run

        counts = [
            count for wave in range(tensors) for count in (tensors - wave, last - wave) if count
        ]
        begins, done = [], 0
        for count in counts:
            for j in range(pairs):
                begins.append((done + count * j / pairs) / (tensors * tensors))
            done += count
        count = down_scatter.steps
        wishes = []
        for scatter, dues in ((down_scatter, DOWN_DUES), (up_scatter, UP_DUES)):
            wishes.append((dues[0], advance(scatter, 0)))
            for step in range(1, count):
                due = dues[1] + (dues[2] - dues[1]) * (step - 1) / max(count - 2, 1)
                wishes.append((due, advance(scatter, step)))
        wishes = [(next(n for n, at in enumerate(begins) if at >= wish), one) for wish, one in wishes]

        def block_of(number, q_slot, q_count, k_slot, k_count):
            at_q = slice(q_slot * rows, (q_slot + q_count) * rows)
            at_k = slice(k_slot * rows, (k_slot + k_count) * rows)

            @pl.loop(0, pairs)
            def _(j):
                for place, one in wishes:
                    if place // pairs == number:

                        @pl.when(j == place % pairs)
                        def _():
                            one()

                at = pl.ds(pl.multiple_of(j * 2 * E, 2 * E), 2 * E)
                key_marks = key_marks_ref[at_k, :]
                keys = jnp.concatenate([k_ref[at_k, at], key_marks], axis=1)
                values = jnp.concatenate([v_ref[at_k, at], key_marks], axis=1)
                query_marks = query_marks_ref[:, at_q]
                no_marks = jnp.zeros_like(query_marks)
                queries = q_ref[at_q, at]
                ups = do_ref[q_slot : q_slot + q_count, :, at].reshape(q_count * rows, 2 * E)
                sums = []
                for half in range(2):

                    def row_of(ref):
                        row = pl.ds(2 * j + half, 1)
                        slots = range(q_slot, q_slot + q_count)
                        return jnp.concatenate([ref[slot, row, :] for slot in slots], axis=1)

                    minus_lse = with_row(query_marks, row_of(lse_ref))
                    minus_delta = with_row(no_marks, row_of(delta_ref))
                    probs = jnp.exp(dot_nn(keys, with_marks(half_rows(qt_ref[at, at_q], half), minus_lse)))
                    pushed = dot_nn(values, with_marks(half_rows(dot_ref[at, at_q], half), minus_delta))
                    delta = (probs * pushed).astype(BF16)
                    at_head = pl.ds(pl.multiple_of((2 * j + half) * E, E), E)
                    dq_ref[at_head, at_q] += dot_nn(kt_ref[at_head, at_k], delta)
                    sums.append((dot_nn(delta, queries), dot_nn(probs.astype(BF16), ups)))
                low_half = lax.broadcasted_iota(jnp.int32, sums[0][0].shape, 1) < E
                dk_ref[at_k, at] += jnp.where(low_half, sums[0][0], sums[1][0])
                dv_ref[at_k, at] += jnp.where(low_half, sums[0][1], sums[1][1])

        for wave in range(tensors):
            if wave == 0:
                receive(0)
            block_of(2 * wave, wave, 1, wave, tensors - wave)
            if wave == 0:
                for slot in range(1, tensors):
                    receive(slot)
            if wave < last:
                block_of(2 * wave + 1, wave + 1, last - wave, wave, 1)
            at = slice(wave * rows, (wave + 1) * rows)
            grads = (
                (dq_ref[:, at] * 0.125).T.astype(BF16),
                dk_ref[at, :].astype(BF16),
                dv_ref[at, :].astype(BF16),
            )
            part = jnp.zeros((rows, width), F32)
            for i in range(3):
                grads_ref[i, at, :] = grads[i]
                part = part + dot_nn(grads[i], w_t(i))

            if wave < last:
                stage_ref[wave] = part.astype(BF16)
                input_copy(wave, partner_of(wave)).start()
            else:
                base_ref[me // owners] += part

        for i in range(3):
            g = dot_nn(xt_ref[...], grads_ref[i]).astype(BF16)
            for t in range(tensors // owners):
                g_qkv_ref[i, me_low * (tensors // owners) + t] = g[
                    :, t * shard : (t + 1) * shard
                ].reshape((2,) * dp_bits + (width >> dp_bits, shard))
            qkv_scatters[i].begin()
            if i:
                qkv_scatters[i - 1].advance(0)

    pl.run_scoped(
        backward_phase,
        pltpu.VMEM((lanes, length), BF16),
        pltpu.VMEM((tensors, max(heads, 8), rows), F32),
        pltpu.VMEM((lanes, length), F32),
        pltpu.VMEM((length, lanes), F32),
        pltpu.VMEM((length, lanes), F32),
        pltpu.VMEM((3, length, lanes), BF16),
    )


    def end_phase(turned_ref):
        stores = [
            pltpu.make_async_copy(turned_ref.at[n], ref, local_sem.at[n])
            for n, ref in enumerate((post_ref, dual_ref, grad_post_ref))
        ]

        def store(n):
            made = base_ref[...].astype(BF16) if n == 2 else home_ref[2 - n]
            turned_ref[n] = jnp.swapaxes(made, 0, 1)
            stores[n].start()

        def advance(step):
            for one in qkv_scatters:
                one.advance(step)

        store(0)
        qkv_scatters[2].advance(0)
        store(1)
        if dp_bits > 1:
            advance(1)
        if last > 1:
            x_copy(last - 1).wait_send()
        for slot in range(last):
            input_copy(slot, partner_of(slot)).wait()
            base_ref[partner_of(slot) // owners] += input_land_ref[slot].astype(F32)
        store(2)
        for step in range(2, dp_bits):
            advance(step)
        small = [
            pltpu.make_async_copy(small_refs[n], ref, local_sem.at[8 + n])
            for n, ref in enumerate((r_qkv_ref, r_down_ref, r_up_ref, r_norm_ref))
        ]
        small_refs[1][...] = down_scatter.result()
        small_refs[2][...] = up_scatter.result()
        count = width // (tensors << dp_bits)
        first = (lax.axis_index("dp") * tensors + me) * count
        small_refs[3][...] = pltpu.roll(norm_sum.result(), width - first, 1)[:, :128]
        start(small[1:])
        for i in range(3):
            small_refs[0][i] = qkv_scatters[i].result()
        small[0].start()
        for copy in small:
            copy.wait()
        for copy in stores:
            copy.wait()

    pl.run_scoped(end_phase, pltpu.VMEM((3, rows, columns, width), BF16))


def hand_over_kernel(*refs):
    sources, results = refs[:7], refs[7:]
    for n in range(3):
        results[n][...] = sources[n][...].astype(F32)

    @pl.when(pl.program_id(0) == 0)
    def _():
        grad_qkv, grad_down, grad_up_out, grad_norm = sources[3:]
        share = results[4].shape[1]
        results[3][...] = grad_qkv[...]
        results[4][...] = grad_down[...]
        results[5][...] = grad_up_out[:, :share]
        results[6][...] = grad_up_out[:, share:]
        for n in range(4):
            results[7 + n][...] = grad_norm[n : n + 1, : results[7 + n].shape[1]]


def body(
    x_post,
    x_dual,
    cot_post,
    cot_dual,
    segment_ids,
    w_qkv,
    w_out,
    w_up,
    w_down,
    gain_one,
    bias_one,
    gain_two,
    bias_two,
):
    tensors, devices = lax.axis_size("tensor"), lax.axis_size("dp")
    dp_bits = log2(devices)
    rows, columns, width = x_post.shape
    length = tensors * rows
    owners = tensors // columns
    lanes = width // owners
    share, shard = w_up.shape[1], w_out.shape[0]
    piece = width // devices
    heads = lanes // E
    me = lax.axis_index("tensor")
    def cut(array, dim):
        bits = min(dp_bits, log2(array.shape[dim] // 16))
        shape = array.shape[:dim] + (2,) * bits + (array.shape[dim] >> bits,) + array.shape[dim + 1 :]
        return array.reshape(shape)

    shards = [cut(w_out, 0), cut(w_up, 0), cut(w_down, 0)]
    qkv_shape = jax.eval_shape(lambda w: cut(jnp.swapaxes(w, 1, 2), 1), w_qkv).shape
    in_place = pl.BlockSpec(memory_space=pl.ANY)
    shape = jax.ShapeDtypeStruct
    bits = (2,) * dp_bits

    def lands(lane_count, *lead):
        return [
            pltpu.VMEM(lead + (tensors,) + bits[: dp_bits - 1 - step] + (piece, lane_count), BF16)
            for step in range(dp_bits)
        ]

    small_out = (
        shape((3, piece, shard), F32),
        shape((piece, share), F32),
        shape((piece, share + shard), F32),
        shape((8, 128), F32),
    )
    cuts = [len(qkv_shape) - 3] + [len(one.shape) - 2 for one in shards]
    links = link_counts(tensors, dp_bits, cuts)
    layer = pl.pallas_call(
        functools.partial(layer_kernel, dp_bits, columns),
        out_shape=(
            shape((rows, columns, width), BF16),
            shape((rows, columns, width), BF16),
            shape((rows, columns, width), BF16),
        )
        + small_out,
        in_specs=[in_place] * 13,
        out_specs=(in_place,) * 7,
        scratch_shapes=[
            pltpu.VMEM((4, columns, rows, width), BF16),
            pltpu.VMEM((tensors, rows, width), BF16),
            pltpu.VMEM((tensors,) + qkv_shape, BF16),
        ]
        + [pltpu.VMEM((tensors,) + one.shape, BF16) for one in shards]
        + [
            pltpu.VMEM((tensors, rows, lanes), BF16),
            pltpu.VMEM((tensors, rows, lanes), BF16),
            pltpu.VMEM((tensors - 1, rows, width), BF16),
            pltpu.VMEM((tensors,) + bits + (piece, share), BF16),
            pltpu.VMEM((tensors,) + bits + (piece, share + shard), BF16),
            pltpu.VMEM((3, tensors) + bits + (piece, shard), BF16),
            lands(share),
            pltpu.VMEM((tensors - 1, piece, share), BF16),
            lands(share + shard),
            pltpu.VMEM((tensors - 1, piece, share + shard), BF16),
            lands(shard, 3),
            pltpu.VMEM((3, tensors - 1, piece, shard), BF16),
            pltpu.VMEM((8, width), F32),
            pltpu.VMEM((dp_bits + tensors - 1, 8, width), F32),
            pltpu.VMEM((length, lanes), BF16),
            pltpu.VMEM((length, lanes), BF16),
            pltpu.VMEM((length, lanes), BF16),
            pltpu.VMEM((lanes, length), BF16),
            pltpu.VMEM((lanes, length), BF16),
            pltpu.VMEM((width, length), BF16),
            pltpu.VMEM((tensors, rows, lanes), F32),
            pltpu.VMEM((tensors, max(heads, 8), rows), F32),
            pltpu.VMEM((columns, rows, width), F32),
            pltpu.VMEM((tensors - 1, rows, width), BF16),
            pltpu.VMEM((length, 2 * E), BF16),
            pltpu.VMEM((2 * E, length), BF16),
            pltpu.VMEM((2 * E, length), BF16),
            pltpu.VMEM((length, 2 * E), BF16),
            pltpu.VMEM((rows, 2 * E), F32),
            pltpu.VMEM((max(tensors, 8), rows), F32),
            pltpu.VMEM((8, length), F32),
            pltpu.VMEM((columns, length), jnp.int32),
            pltpu.VMEM((8, width), F32),
            [pltpu.VMEM(one.shape, F32) for one in small_out],
            pltpu.SemaphoreType.DMA((links[1],)),
            pltpu.SemaphoreType.DMA((links[0],)),
            pltpu.SemaphoreType.DMA((16,)),
        ],
        compiler_params=pltpu.CompilerParams(
            vmem_limit_bytes=VMEM_BYTES, collective_id=0, has_side_effects=True
        ),
        name="layer",
    )
    made = layer(
        segment_ids.T,
        x_post,
        x_dual,
        cot_post,
        cot_dual,
        w_qkv,
        *shards,
        *(one.reshape(1, width) for one in (gain_one, bias_one, gain_two, bias_two)),
    )
    count = width // (tensors * devices)
    blocks = 2
    block_spec = pl.BlockSpec((rows // blocks, columns, width), lambda i: (i, 0, 0))

    def whole_spec(one):
        return pl.BlockSpec(one.shape, lambda i: (0,) * len(one.shape))

    small = (
        shape((3, piece, shard), F32),
        shape((piece, share), F32),
        shape((piece, share), F32),
        shape((piece, shard), F32),
    ) + (shape((1, count), F32),) * 4
    results = pl.pallas_call(
        hand_over_kernel,
        out_shape=tuple(shape(one.shape, F32) for one in made[:3]) + small,
        grid=(blocks,),
        in_specs=[block_spec] * 3 + [whole_spec(one) for one in made[3:]],
        out_specs=(block_spec,) * 3 + tuple(whole_spec(one) for one in small),
        name="hand_over",
    )(*made)
    post_out, dual_out, grad_post, g_qkv, g_down, g_up, g_out = results[:7]
    norms = tuple(one.reshape(count) for one in results[7:])
    return (post_out, dual_out, grad_post, g_qkv, g_out.T, g_up, g_down.T) + norms


def solution(mesh):
    placed = (
        P("tensor", "dp", None),
        P("tensor", "dp", None),
        P("tensor", "dp", None),
        P("tensor", "dp", None),
        P(None, "dp"),
        P(None, None, "tensor"),
        P("tensor", None),
        P(None, "tensor"),
        P("tensor", None),
        P(),
        P(),
        P(),
        P(),
    )
    return jax.shard_map(
        body,
        mesh=mesh,
        in_specs=placed,
        out_specs=(
            P("tensor", "dp", None),
            P("tensor", "dp", None),
            P("tensor", "dp", None),
            P(None, "dp", "tensor"),
            P("tensor", "dp"),
            P("dp", "tensor"),
            P("tensor", "dp"),
            P(("dp", "tensor")),
            P(("dp", "tensor")),
            P(("dp", "tensor")),
            P(("dp", "tensor")),
        ),
        check_vma=False,
    )
```
